32 devices in a mesh: ctx: 8 (over z, x), wt: 4 (over y, core).
Axes of the slice: x: 2, y: 2, z: 4, core: 2. Of those that a mesh axis runs over, the one named last changes fastest.
Arguments:
- block_in: bfloat16 [4096, 2048], P(('ctx', 'wt')), may hold values from -6 to 6
- target: bfloat16 [4096, 2048], P(('ctx', 'wt')), may hold values from -6 to 6
- seq_lengths: int32 [3], replicated, may hold values from 1024 to 2048, as said below
- permutation: int32 [4096], replicated, may hold values from 0 to 4095, each once
- routes: int32 [4096, 2], P('ctx'), may hold values from 0 to 3, all different within a row
- attn_qkv: float32 [3, 2048, 2048], P(None, None, 'wt'), may hold values from -0.125 to 0.125
- attn_out: float32 [2048, 2048], P(None, 'wt'), may hold values from -3 to 3
- norm_gains: float32 [4, 2048], replicated, may hold values from 0.5 to 1.5
- router: float32 [2048, 4], replicated, may hold values from -0.09375 to 0.09375
- gate_up: float32 [2, 4, 2048, 1024], P(None, None, None, 'wt'), may hold values from -0.125 to 0.125
- down: float32 [4, 2048, 1024], P(None, None, 'wt'), may hold values from -0.5 to 0.5
Outputs:
- block_out: bfloat16 [4096, 2048], P(('ctx', 'wt'))
- input_grad: bfloat16 [4096, 2048], P(('ctx', 'wt'))
- qkv_grad: float32 [3, 2048, 2048], P(None, 'ctx', 'wt')
- out_grad: float32 [2048, 2048], P('ctx', 'wt')
- gains_grad: float32 [4, 2048], replicated
- router_grad: float32 [2048, 4], replicated
- gate_up_grad: float32 [2, 4, 2048, 1024], P(None, None, 'ctx', 'wt')
- down_grad: float32 [4, 2048, 1024], P(None, 'ctx', 'wt')
The draws below stay inside these ranges and needn't reach their ends.
Inputs may be any that keep to these rules, and one draw needn't show every extreme that they name: `seq_lengths`: the lengths sum to 4096, and one of them is 2048.
All inputs are finite; a program needn't handle non-finite values.
Results may differ from the reference program's by a relative error of at most 0.025.
Values may be sent and summed in bfloat16 or wider, within the bound.
No kernel may reach another device: no remote copies, remote signals or barrier semaphores. Data moves between devices by JAX's collectives and lax.ppermute only.
A program may use at most 320 MiB of HBM per device.

```python
import functools
import math
import jax
import jax.numpy as jnp
from jax import lax

D = 2048
HEADS = 16
HEAD_DIM = 128
FF = 1024
EXPERTS = 4
TOP = 2
MIN_LEN = 1024
TOKENS = 4096
SEQS = 3
MAX_LEN = 2048


def draw_seq_lengths(key, part):
    key = jax.random.fold_in(key, 7)
    slot_key, order_key = jax.random.split(key)
    others = SEQS - 1
    room = MAX_LEN - MIN_LEN
    leftover_total = TOKENS - MAX_LEN - others * MIN_LEN
    capacity = others * room
    slot_owner = (jnp.arange(capacity, dtype=jnp.int32) // room).astype(jnp.int32)
    shuffled = jax.random.permutation(slot_key, capacity)
    chosen = slot_owner[shuffled[:leftover_total]]
    counts = jnp.sum((chosen[:, None] == jnp.arange(others, dtype=jnp.int32)[None, :]).astype(jnp.int32), axis=0).astype(jnp.int32)
    full = jnp.concatenate([jnp.full((1,), MAX_LEN, jnp.int32), (MIN_LEN + counts).astype(jnp.int32)])
    order = jax.random.permutation(order_key, SEQS)
    return full[order].astype(jnp.int32)


def level_of(key, dims, shards, low, high):
    def one(dim, shards_of):
        heights = jax.random.uniform(jax.random.fold_in(jax.random.fold_in(key, 6), dim), (shards_of,), jnp.float32, low / len(shards), high / len(shards))
        return jnp.repeat(jnp.exp(heights), dims[dim] // shards_of).reshape((-1,) + (1,) * (len(dims) - dim - 1))

    factor_of = one(*shards[0])
    for cut in shards[1:]:
        factor_of = factor_of * one(*cut)
    return factor_of


def choose_distinct(own_key, rows, amount, top, lift):
    order = jax.random.permutation(jax.random.fold_in(own_key, 1), amount)
    boost = order
    for power in range(3):
        boost = boost * boost // amount
    boost = boost * lift // amount
    tickets = jax.random.randint(jax.random.fold_in(own_key, 2), (rows, amount), 0, 4096) + boost
    sure = jax.random.permutation(jax.random.fold_in(own_key, 3), rows)[jnp.arange(amount) % rows]
    tickets = jnp.where(jnp.arange(rows)[:, None] == sure[None, :], 1 << 14, tickets)
    merit = tickets * amount + jnp.arange(amount)
    return lax.top_k(merit.astype(jnp.int32), top)[1].astype(jnp.int32)


def normal_values(own_key, shape, spread, limit, shards=(), kind=jnp.bfloat16):
    array = jax.random.normal(own_key, shape, jnp.float32) * spread
    if len(shards) > 0:
        array = level_of(own_key, shape, shards, -0.22, 0.18) * array
    return jnp.clip(array, min=-limit, max=limit).astype(kind)


def setup_inputs(seed: int = 0) -> dict:
    keys = jax.random.split(jax.random.key(seed), 12)
    return {
        "block_in": normal_values(keys[0], (TOKENS, D), 1.0, 6.0, ((0, 32),)),
        "target": normal_values(keys[1], (TOKENS, D), 1.0, 6.0, ((0, 32),)),
        "seq_lengths": draw_seq_lengths(jax.random.fold_in(keys[11], 71), 0),
        "permutation": jax.random.permutation(keys[3], TOKENS).astype(jnp.int32),
        "routes": choose_distinct(keys[4], TOKENS, EXPERTS, TOP, 4096),
        "attn_qkv": normal_values(keys[5], (3, D, D), D ** -0.5, 0.125, ((2, 4),), jnp.float32),
        "attn_out": normal_values(keys[6], (D, D), 0.5, 3.0, ((1, 4),), jnp.float32),
        "norm_gains": jnp.clip(1.0 + 0.1 * jax.random.normal(keys[7], (4, D), jnp.float32), 0.5, 1.5),
        "router": normal_values(keys[8], (D, EXPERTS), (2 * D) ** -0.5, 0.09375, (), jnp.float32),
        "gate_up": normal_values(keys[9], (2, EXPERTS, D, FF), D ** -0.5, 0.125, ((3, 4),), jnp.float32),
        "down": normal_values(keys[10], (EXPERTS, D, FF), (FF // 8) ** -0.5, 0.5, ((2, 4),), jnp.float32),
    }


norm_eps = 1e-05
highest = lax.Precision.HIGHEST

@jax.custom_vjp
def low(v):
    return lax.optimization_barrier(v.astype(jnp.bfloat16)).astype(jnp.float32)

@jax.custom_vjp
def low_back(v):
    return v

def low_keep(v):
    return (low(v), None)

def low_pass(kept, grad):
    return (grad,)

def back_keep(v):
    return (v, None)

def back_low(kept, grad):
    return (low(grad),)
low.defvjp(low_keep, low_pass)
low_back.defvjp(back_keep, back_low)

def token_places(seq_lengths, permutation):
    seq_ends = jnp.cumsum(seq_lengths).astype(jnp.int32)
    seq_starts = (seq_ends - seq_lengths).astype(jnp.int32)
    token_index = permutation.astype(jnp.int32)
    seq_id = lax.optimization_barrier(jnp.sum((token_index[:, None] >= seq_ends[None, :]).astype(jnp.int32), axis=1)).astype(jnp.int32)
    member = seq_id[:, None] == jnp.arange(seq_lengths.shape[0], dtype=jnp.int32)[None, :]
    positions = token_index - lax.optimization_barrier(jnp.sum(jnp.where(member, seq_starts[None, :], 0), axis=1)).astype(jnp.int32)
    return (seq_id, positions.astype(jnp.int32))

def rope_tables(positions, head_dim):
    half_dim = head_dim // 2
    frequency = jnp.exp(jnp.arange(half_dim, dtype=jnp.float32) * (-2.0 * math.log(10000.0) / head_dim))
    angles = positions.astype(jnp.float32)[:, None] * frequency[None, :]
    return (jnp.cos(angles), jnp.sin(angles))

def rotate(vectors, cosine, sine_tab):
    half_dim = vectors.shape[-1] // 2
    lower_half = vectors[..., :half_dim]
    upper_half = vectors[..., half_dim:]
    cos_part = cosine[:, None, :]
    sin_part = sine_tab[:, None, :]
    return jnp.concatenate([lower_half * cos_part - upper_half * sin_part, upper_half * cos_part + lower_half * sin_part], axis=-1)

def rms_scale(vectors):
    return lax.rsqrt(lax.optimization_barrier(jnp.mean(vectors * vectors, axis=-1, keepdims=True)) + norm_eps)

def layer(block_in, attn_qkv, attn_out, norm_gains, router, gate_up, down, seq_id, positions, choose):
    tok_all = block_in.shape[0]
    cosine, sine_tab = rope_tables(positions, HEAD_DIM)
    score_scale = HEAD_DIM ** (-0.5)
    normed = low(block_in * rms_scale(block_in) * norm_gains[0])
    projected = jnp.einsum('td,kdc->ktc', normed, low(attn_qkv), precision=highest)
    query_raw = low_back(projected[0])
    key_raw = low_back(projected[1])
    value_rows = low(low_back(projected[2])).reshape(tok_all, HEADS, HEAD_DIM)
    query_rows = low(rotate((query_raw * rms_scale(query_raw) * norm_gains[2]).reshape(tok_all, HEADS, HEAD_DIM), cosine, sine_tab))
    key_rows = low(rotate((key_raw * rms_scale(key_raw) * norm_gains[3]).reshape(tok_all, HEADS, HEAD_DIM), cosine, sine_tab))
    block_len = math.gcd(tok_all, 512)
    block_count = tok_all // block_len

    def attend(block_item):
        query_blk, seq_blk, pos_blk = block_item
        scores = low_back(jnp.einsum('qhd,khd->hqk', query_blk, key_rows, precision=highest) * score_scale)
        allowed = (seq_blk[:, None] == seq_id[None, :]) & (positions[None, :] <= pos_blk[:, None])
        scores = jnp.where(allowed[None], scores, -1e+30)
        top_score = lax.optimization_barrier(jnp.max(scores, axis=-1, keepdims=True))
        weights = jnp.where(allowed[None], jnp.exp(scores - top_score), 0.0)
        prob_all = low(weights / lax.optimization_barrier(jnp.sum(weights, axis=-1, keepdims=True)))
        return jnp.einsum('hqk,khd->qhd', prob_all, value_rows, precision=highest)
    attended = lax.map(jax.checkpoint(attend), (query_rows.reshape(block_count, block_len, HEADS, HEAD_DIM), seq_id.reshape(block_count, block_len), positions.reshape(block_count, block_len)))
    attended = low(low_back(attended.reshape(tok_all, HEADS * HEAD_DIM)))
    residual = block_in + low_back(jnp.dot(attended, low(attn_out).T, precision=highest))
    mixed_rows = low(residual * rms_scale(residual) * norm_gains[1])
    logits = low_back(jnp.dot(mixed_rows, low(router), precision=highest))
    gate_w = jax.nn.softmax(logits, axis=-1) * choose
    pre_act = jnp.einsum('td,kedf->ketf', mixed_rows, low(gate_up), precision=highest)
    gate_in = low_back(pre_act[0])
    up_in = low_back(pre_act[1])
    hidden = low(low_back(gate_w.T[:, :, None] * jax.nn.silu(gate_in) * up_in))
    expert_sum = low_back(jnp.einsum('etf,edf->td', hidden, low(down), precision=highest))
    return residual + expert_sum

def reference(block_in, target, seq_lengths, permutation, routes, attn_qkv, attn_out, norm_gains, router, gate_up, down):
    seq_id, positions = token_places(seq_lengths, permutation)
    choose = lax.optimization_barrier(jnp.sum((routes[:, :, None] == jnp.arange(EXPERTS, dtype=jnp.int32)[None, None, :]).astype(jnp.float32), axis=1))
    forward = functools.partial(layer, seq_id=seq_id, positions=positions, choose=choose)
    target_f = target.astype(jnp.float32)

    def objective(block_in, attn_qkv, attn_out, norm_gains, router, gate_up, down):
        out_f = forward(block_in, attn_qkv, attn_out, norm_gains, router, gate_up, down)
        gap = out_f - target_f
        return (0.5 * jnp.sum(gap * gap), out_f)
    loss_value, pull_back, out_f = jax.vjp(objective, block_in.astype(jnp.float32), attn_qkv, attn_out, norm_gains, router, gate_up, down, has_aux=True)
    grad_list = pull_back(jnp.ones_like(loss_value))
    return (out_f.astype(jnp.bfloat16), grad_list[0].astype(jnp.bfloat16), grad_list[1], grad_list[2], grad_list[3], grad_list[4], grad_list[5], grad_list[6])
```

```python
import functools
import math

import jax
import jax.numpy as jnp
from jax import lax
from jax.experimental import pallas as pl
from jax.experimental.pallas import tpu as pltpu
from jax.sharding import Mesh
from jax.sharding import PartitionSpec as P

HEAD_DIM = 128
LOG2E = math.log2(math.e)
VMEM_BYTES = 56 * 1024 * 1024

norm_eps = 1e-05
f32 = jnp.float32
bf16 = jnp.bfloat16

SWAP = [(0, 1), (1, 0)]
DOT_NT = (((1,), (1,)), ((), ()))
DOT_NN = (((1,), (0,)), ((), ()))


def attend_kernel(groups, chunk, score_scale, q_ref, tok_q_ref, start_q_ref, *refs):
    key_refs = refs[: 3 * groups]
    o_ref, lse_ref = refs[3 * groups : 3 * groups + 2]
    vt_refs = refs[3 * groups + 2 :]
    rows = q_ref.shape[0]

    @pl.when(pl.program_id(0) == 0)
    def _():
        for g in range(groups):
            v_ref, vt_ref = key_refs[3 * g + 1], vt_refs[g]

            def turn(j, carry):
                r = pl.ds(pl.multiple_of(j * chunk, chunk), chunk)
                vt_ref[:, r] = v_ref[r, :].T
                return carry

            lax.fori_loop(0, v_ref.shape[0] // chunk, turn, 0)

    queries = q_ref[...]
    tok_q = tok_q_ref[...]
    start_q = start_q_ref[...]
    state = (
        jnp.full((1, rows), -1e30, f32),
        jnp.zeros((1, rows), f32),
        jnp.zeros((queries.shape[1], rows), f32),
    )
    for g in range(groups):
        k_ref, _, tok_k_ref = key_refs[3 * g : 3 * g + 3]
        vt_ref = vt_refs[g]

        def step(j, carry):
            run_max, run_sum, acc = carry
            r = pl.ds(pl.multiple_of(j * chunk, chunk), chunk)
            s = lax.dot_general(k_ref[r, :], queries, DOT_NT, preferred_element_type=f32)
            tok_k = tok_k_ref[r, :]
            s = jnp.where((tok_k <= tok_q) & (tok_k >= start_q), s * score_scale, -1e30)
            new_max = jnp.maximum(run_max, jnp.max(s, axis=0, keepdims=True))
            p = jnp.exp2(s - new_max)
            shrink = jnp.exp2(run_max - new_max)
            run_sum = run_sum * shrink + jnp.sum(p, axis=0, keepdims=True)
            acc = acc * shrink + lax.dot_general(
                vt_ref[:, r], p.astype(bf16), DOT_NN, preferred_element_type=f32
            )
            return new_max, run_sum, acc

        steps = k_ref.shape[0] // chunk
        state = lax.fori_loop(0, steps, step, state, unroll=steps <= 4)
    run_max, run_sum, acc = state
    o_ref[...] = (acc / run_sum).T
    lse_ref[...] = run_max + jnp.log2(run_sum)


def attend(packed, tok_q, start_q, key_groups):
    rows = packed.shape[0]
    block = min(1024, rows)
    chunk = 1024
    row = pl.BlockSpec((1, block), lambda i: (0, i))
    in_specs = [pl.BlockSpec((block, HEAD_DIM), lambda i: (i, 0)), row, row]
    operands = [packed, tok_q, start_q]
    scratch = []
    keys = 0
    for array, k_col, v_col, tok_k in key_groups:
        count = array.shape[0]
        keys += count
        in_specs += [
            pl.BlockSpec((count, HEAD_DIM), lambda i, col=k_col: (0, col)),
            pl.BlockSpec((count, HEAD_DIM), lambda i, col=v_col: (0, col)),
            pl.BlockSpec((count, 1), lambda i: (0, 0)),
        ]
        operands += [array, array, tok_k]
        scratch.append(pltpu.VMEM((HEAD_DIM, count), bf16))
    return pl.pallas_call(
        functools.partial(
            attend_kernel, len(key_groups), chunk, LOG2E / math.sqrt(HEAD_DIM)
        ),
        grid=(rows // block,),
        in_specs=in_specs,
        out_specs=[pl.BlockSpec((block, HEAD_DIM), lambda i: (i, 0)), row],
        out_shape=[
            jax.ShapeDtypeStruct((rows, HEAD_DIM), f32),
            jax.ShapeDtypeStruct((1, rows), f32),
        ],
        scratch_shapes=scratch,
        compiler_params=pltpu.CompilerParams(vmem_limit_bytes=VMEM_BYTES),
        cost_estimate=pl.CostEstimate(
            flops=8 * rows * keys * HEAD_DIM,
            bytes_accessed=4 * (rows + keys) * HEAD_DIM,
            transcendentals=rows * keys,
        ),
        name="attend",
    )(*operands)


def attend_grad_kernel(
    chunk,
    score_scale,
    grad_scale,
    q_ref,
    do_ref,
    lse_ref,
    delta_ref,
    tok_q_ref,
    start_q_ref,
    dq_in_ref,
    k_ref,
    v_ref,
    tok_k_ref,
    dq_ref,
    dkv_ref,
    kt_ref,
    dk_acc,
    dv_acc,
):
    steps = k_ref.shape[0] // chunk

    @pl.when(pl.program_id(0) == 0)
    def _():
        dk_acc[...] = jnp.zeros_like(dk_acc)
        dv_acc[...] = jnp.zeros_like(dv_acc)

        def turn(j, carry):
            r = pl.ds(pl.multiple_of(j * chunk, chunk), chunk)
            kt_ref[:, r] = k_ref[r, :].T
            return carry

        lax.fori_loop(0, steps, turn, 0)

    queries = q_ref[...]
    d_out = do_ref[...]
    tok_q = tok_q_ref[...]
    start_q = start_q_ref[...]
    lse = lse_ref[...]
    delta = delta_ref[...]

    def step(j, dq_t):
        r = pl.ds(pl.multiple_of(j * chunk, chunk), chunk)
        s = lax.dot_general(k_ref[r, :], queries, DOT_NT, preferred_element_type=f32)
        tok_k = tok_k_ref[r, :]
        allowed = (tok_k <= tok_q) & (tok_k >= start_q)
        p = jnp.exp2(jnp.where(allowed, s * score_scale - lse, -1e30))
        dp = lax.dot_general(v_ref[r, :], d_out, DOT_NT, preferred_element_type=f32)
        ds = (p * (dp - delta)).astype(bf16)
        dv_acc[r, :] += lax.dot_general(
            p.astype(bf16), d_out, DOT_NN, preferred_element_type=f32
        )
        dk_acc[r, :] += lax.dot_general(ds, queries, DOT_NN, preferred_element_type=f32)
        return dq_t + lax.dot_general(kt_ref[:, r], ds, DOT_NN, preferred_element_type=f32)

    dq_t = lax.fori_loop(
        0,
        steps,
        step,
        jnp.zeros((queries.shape[1], queries.shape[0]), f32),
        unroll=steps <= 4,
    )
    dq_ref[...] = dq_in_ref[...] + (dq_t * grad_scale).T

    @pl.when(pl.program_id(0) == pl.num_programs(0) - 1)
    def _():
        dkv_ref[:, :HEAD_DIM] = (dk_acc[...] * grad_scale).astype(dkv_ref.dtype)
        dkv_ref[:, HEAD_DIM:] = dv_acc[...].astype(dkv_ref.dtype)


def attend_grad(packed, d_out, lse, delta, tok_q, start_q, dq_in, key_group, out_type):
    rows = packed.shape[0]
    array, k_col, v_col, tok_k = key_group
    keys = array.shape[0]
    block = min(1024, rows)
    chunk = 1024
    row = pl.BlockSpec((1, block), lambda i: (0, i))
    head = pl.BlockSpec((block, HEAD_DIM), lambda i: (i, 0))
    return pl.pallas_call(
        functools.partial(
            attend_grad_kernel,
            chunk,
            LOG2E / math.sqrt(HEAD_DIM),
            1.0 / math.sqrt(HEAD_DIM),
        ),
        grid=(rows // block,),
        in_specs=[
            head,
            head,
            row,
            row,
            row,
            row,
            head,
            pl.BlockSpec((keys, HEAD_DIM), lambda i: (0, k_col)),
            pl.BlockSpec((keys, HEAD_DIM), lambda i: (0, v_col)),
            pl.BlockSpec((keys, 1), lambda i: (0, 0)),
        ],
        out_specs=[head, pl.BlockSpec((keys, 2 * HEAD_DIM), lambda i: (0, 0))],
        out_shape=[
            jax.ShapeDtypeStruct((rows, HEAD_DIM), f32),
            jax.ShapeDtypeStruct((keys, 2 * HEAD_DIM), out_type),
        ],
        scratch_shapes=[
            pltpu.VMEM((HEAD_DIM, keys), bf16),
            pltpu.VMEM((keys, HEAD_DIM), f32),
            pltpu.VMEM((keys, HEAD_DIM), f32),
        ],
        compiler_params=pltpu.CompilerParams(vmem_limit_bytes=VMEM_BYTES),
        cost_estimate=pl.CostEstimate(
            flops=16 * rows * keys * HEAD_DIM,
            bytes_accessed=12 * (rows + keys) * HEAD_DIM,
            transcendentals=rows * keys,
        ),
        name="attend_grad",
    )(packed, d_out, lse, delta, tok_q, start_q, dq_in, array, array, tok_k)


def pack_kernel(raw0_ref, raw1_ref, inv_ref, cos_ref, sin_ref, gain_ref, out_ref):
    half = raw0_ref.shape[1]
    for i, raw_ref in enumerate((raw0_ref, raw1_ref)):
        r = slice(i * half, (i + 1) * half)
        for j in range(2):
            u = raw_ref[j] * inv_ref[r, j : j + 1] * gain_ref[j : j + 1, :]
            turned = u * cos_ref[r, :] + pltpu.roll(u, HEAD_DIM // 2, 1) * sin_ref[r, :]
            out_ref[0, r, j * HEAD_DIM : (j + 1) * HEAD_DIM] = turned.astype(bf16)
        out_ref[0, r, 2 * HEAD_DIM :] = raw_ref[2].astype(bf16)


def pack_heads(raw0, raw1, inv, cos_tab, sin_tab, gains):
    half = raw0.shape[1]
    rows = 2 * half
    heads = raw0.shape[2] // HEAD_DIM
    raw = pl.BlockSpec((3, half, HEAD_DIM), lambda h: (0, 0, h))
    table = pl.BlockSpec((rows, HEAD_DIM), lambda h: (0, 0))
    return pl.pallas_call(
        pack_kernel,
        grid=(heads,),
        in_specs=[
            raw,
            raw,
            pl.BlockSpec((rows, 2), lambda h: (0, 0)),
            table,
            table,
            pl.BlockSpec((2, HEAD_DIM), lambda h: (0, h)),
        ],
        out_specs=pl.BlockSpec((1, rows, 3 * HEAD_DIM), lambda h: (h, 0, 0)),
        out_shape=jax.ShapeDtypeStruct((heads, rows, 3 * HEAD_DIM), bf16),
        cost_estimate=pl.CostEstimate(
            flops=20 * rows * heads * HEAD_DIM,
            bytes_accessed=18 * rows * heads * HEAD_DIM,
            transcendentals=0,
        ),
        name="pack_heads",
    )(raw0, raw1, inv, cos_tab, sin_tab, gains)


def raw_grad_kernel(dq_ref, dkv_ref, packed_ref, coef_ref, cos_ref, sin_ref, gain_ref, out_ref, sum_ref):
    @pl.when(pl.program_id(0) == 0)
    def _():
        sum_ref[...] = jnp.zeros_like(sum_ref)

    cos_tab = cos_ref[...]
    sin_tab = sin_ref[...]

    def turn_back(u):
        return u * cos_tab - pltpu.roll(u, HEAD_DIM // 2, 1) * sin_tab

    for j, grad_ref in enumerate((dq_ref, dkv_ref)):
        gain = gain_ref[j : j + 1, :]
        cols = slice(j * HEAD_DIM, (j + 1) * HEAD_DIM)
        d_norm = turn_back(grad_ref[:, :HEAD_DIM])
        hat = turn_back(packed_ref[:, cols].astype(f32)) / gain
        sum_ref[j : j + 1, :] += jnp.sum(d_norm * hat, axis=0, keepdims=True)
        inv = coef_ref[:, 2 * j : 2 * j + 1]
        inner = coef_ref[:, 2 * j + 1 : 2 * j + 2]
        out_ref[:, cols] = (inv * (d_norm * gain - hat * inner)).astype(bf16)
    out_ref[:, 2 * HEAD_DIM :] = dkv_ref[:, HEAD_DIM:].astype(bf16)


def raw_grad(d_query, d_kv, packed, coef, cos_tab, sin_tab, gains):
    rows = packed.shape[0]
    block = min(512, rows)

    def wide(cols):
        return pl.BlockSpec((block, cols), lambda i: (i, 0))

    whole = pl.BlockSpec((2, HEAD_DIM), lambda i: (0, 0))
    return pl.pallas_call(
        raw_grad_kernel,
        grid=(rows // block,),
        in_specs=[
            wide(HEAD_DIM),
            wide(2 * HEAD_DIM),
            wide(3 * HEAD_DIM),
            wide(4),
            wide(HEAD_DIM),
            wide(HEAD_DIM),
            whole,
        ],
        out_specs=[wide(3 * HEAD_DIM), whole],
        out_shape=[
            jax.ShapeDtypeStruct((rows, 3 * HEAD_DIM), bf16),
            jax.ShapeDtypeStruct((2, HEAD_DIM), f32),
        ],
        cost_estimate=pl.CostEstimate(
            flops=40 * rows * HEAD_DIM, bytes_accessed=40 * rows * HEAD_DIM, transcendentals=0
        ),
        name="raw_grad",
    )(d_query, d_kv, packed, coef, cos_tab, sin_tab, gains)


def token_places(seq_lengths, permutation):
    seq_ends = jnp.cumsum(seq_lengths)
    seq_starts = seq_ends - seq_lengths
    seq_id = jnp.sum((permutation[:, None] >= seq_ends[None, :]).astype(jnp.int32), axis=1)
    member = seq_id[:, None] == jnp.arange(seq_lengths.shape[0], dtype=jnp.int32)[None, :]
    return jnp.sum(jnp.where(member, seq_starts[None, :], 0), axis=1)


def near_first(a, axis, y_pos, c_pos):
    a = jnp.where(y_pos == 0, a, jnp.flip(a, axis))
    return jnp.where(c_pos == 0, a, jnp.flip(a, axis + 1))


def norm_back(grad_out, hat_rows, inv_rows, gain_row):
    grad_hat = grad_out * gain_row
    return inv_rows * (grad_hat - hat_rows * jnp.mean(grad_hat * hat_rows, axis=-1, keepdims=True))


def gather_halves(rows):
    core = lax.ppermute(rows, "c", SWAP)
    far = lax.ppermute(rows, "y", SWAP)
    far_core = lax.ppermute(far, "c", SWAP)
    return [jnp.concatenate([rows, core]), jnp.concatenate([far, far_core])]


def scatter_halves(parts):
    near, far = parts
    n = near.shape[0] // 2
    far_sum = far[:n].astype(f32) + lax.ppermute(far[n:], "c", SWAP).astype(f32)
    far_sum = lax.ppermute(far_sum.astype(bf16), "y", SWAP).astype(f32)
    near_sum = near[:n].astype(f32) + lax.ppermute(near[n:], "c", SWAP).astype(f32)
    return near_sum + far_sum


def sum_near(a):
    a = a + jnp.flip(lax.ppermute(a, "c", SWAP), -2)
    return a + jnp.flip(lax.ppermute(a, "y", SWAP), -3)


def sum_line(a, z_count):
    step = 1
    while step < z_count:
        a = a + lax.ppermute(a, "z", [(i, i ^ step) for i in range(z_count)])
        step *= 2
    return a


def scatter_line(part, z_pos, z_count):
    up = down = None
    last = z_count - 1
    for s in range(last):
        to_up = lax.dynamic_index_in_dim(part, jnp.clip(last - s + z_pos, 0, last), 0, False)
        to_down = lax.dynamic_index_in_dim(part, jnp.clip(z_pos + s - last, 0, last), 0, False)
        if s > 0:
            to_up = (to_up.astype(f32) + up.astype(f32)).astype(bf16)
            to_down = (to_down.astype(f32) + down.astype(f32)).astype(bf16)
        up = lax.ppermute(to_up, "z", [(i, i + 1) for i in range(s + 1)])
        down = lax.ppermute(to_down, "z", [(last - i, last - i - 1) for i in range(s + 1)])
    mine = lax.dynamic_index_in_dim(part, z_pos, 0, False).astype(f32)
    return mine + up.astype(f32) + down.astype(f32)


def local(
    z_count,
    x_count,
    block_in,
    target,
    seq_lengths,
    permutation,
    routes,
    attn_qkv,
    attn_out,
    norm_gains,
    router,
    gate_up,
    down,
):
    z_pos = lax.axis_index("z")
    x_pos = lax.axis_index("x")
    y_pos = lax.axis_index("y")
    c_pos = lax.axis_index("c")
    pair = x_count == 2
    local_rows, model_width = block_in.shape
    tok_rows = 4 * local_rows
    line_rows = z_count * tok_rows
    head_cols = attn_qkv.shape[2]
    hidden_cols = gate_up.shape[3]
    experts = gate_up.shape[1]
    wide_block = model_width // z_count
    out_block = wide_block // x_count
    wt_pos = y_pos * 2 + c_pos

    qkv_b = attn_qkv.astype(bf16)
    out_b = attn_out.astype(bf16)
    gu_b = gate_up.astype(bf16)
    down_b = down.astype(bf16)
    router_b = router.astype(bf16)

    resid_in = block_in.astype(f32)
    inv_first = lax.rsqrt(jnp.mean(resid_in * resid_in, axis=-1, keepdims=True) + norm_eps)
    hat_first = resid_in * inv_first
    normed = (hat_first * norm_gains[0]).astype(bf16)
    normed_h = gather_halves(normed)

    start_all = token_places(seq_lengths, permutation)
    shape = (z_count, x_count, 2, 2, local_rows)
    tok_all = near_first(permutation.reshape(shape), 2, y_pos, c_pos)
    start_all = near_first(start_all.reshape(shape), 2, y_pos, c_pos)

    def of_x(a, at):
        return lax.dynamic_index_in_dim(a, at, 1, False).reshape(line_rows)

    tok_own = of_x(tok_all, x_pos)
    start_own = of_x(start_all, x_pos)
    tok_q = tok_own.reshape(1, line_rows)
    start_q = start_own.reshape(1, line_rows)
    half_dim = HEAD_DIM // 2
    frequency = jnp.exp(
        jnp.arange(half_dim, dtype=f32) * (-2.0 * math.log(10000.0) / HEAD_DIM)
    )
    angles = (tok_own - start_own).astype(f32)[:, None] * frequency[None, :]
    cosine, sine = jnp.cos(angles), jnp.sin(angles)
    cos_tab = jnp.concatenate([cosine, cosine], axis=1)
    sin_tab = jnp.concatenate([-sine, sine], axis=1)

    raw_h = [
        jnp.einsum("td,kdc->ktc", n, qkv_b, preferred_element_type=f32) for n in normed_h
    ]
    squares = jnp.concatenate([jnp.sum(r[:2] * r[:2], axis=-1) for r in raw_h], axis=1)
    squares = sum_near(squares.reshape(2, 2, 2, local_rows)).reshape(2, tok_rows)
    inv_qk = lax.rsqrt(squares / model_width + norm_eps)
    inv_line = lax.all_gather(inv_qk, "z", axis=0)
    gain_qk = lax.dynamic_slice_in_dim(norm_gains[2:], wt_pos * head_cols, head_cols, 1)
    payload = pack_heads(
        raw_h[0],
        raw_h[1],
        inv_qk.T,
        lax.dynamic_slice_in_dim(cos_tab, z_pos * tok_rows, tok_rows),
        lax.dynamic_slice_in_dim(sin_tab, z_pos * tok_rows, tok_rows),
        gain_qk,
    )
    packed = lax.all_to_all(payload, "z", 0, 0, tiled=True).reshape(line_rows, 3 * HEAD_DIM)
    kv_own = packed[:, HEAD_DIM:]
    tok_col = tok_own.reshape(line_rows, 1)
    if pair:
        kv_far = lax.ppermute(kv_own, "x", SWAP)
        groups = [
            (kv_far, 0, 1, of_x(tok_all, 1 - x_pos).reshape(line_rows, 1)),
            (packed, 1, 2, tok_col),
        ]
        key_groups = groups[::-1]
    else:
        kv_all = lax.all_gather(kv_own, "x", axis=0)
        tok_x = jnp.moveaxis(tok_all, 1, 0).reshape(x_count, line_rows, 1)
        groups = [(kv_all[i], 0, 1, tok_x[i]) for i in range(x_count)]
        key_groups = [
            (kv_all.reshape(-1, 2 * HEAD_DIM), 0, 1, tok_x.reshape(-1, 1))
        ]
    attn_f, row_lse = attend(packed, tok_q, start_q, key_groups)

    def to_tokens(rows, cols):
        parts = lax.all_to_all(
            rows.reshape(z_count, tok_rows, cols), "z", 0, 0, tiled=True
        )
        return parts

    attn_parts = to_tokens(attn_f.astype(bf16), HEAD_DIM)
    attn_b = jnp.moveaxis(attn_parts, 0, 1).reshape(tok_rows, head_cols)
    half = tok_rows // 2

    def halves(a):
        return [a[:half], a[half:]]

    attn_y = scatter_halves(
        [
            lax.dot_general(a, out_b, DOT_NT, preferred_element_type=f32).astype(bf16)
            for a in halves(attn_b)
        ]
    )
    residual = resid_in + attn_y
    inv_second = lax.rsqrt(jnp.mean(residual * residual, axis=-1, keepdims=True) + norm_eps)
    hat_second = residual * inv_second
    mixed_rows = (hat_second * norm_gains[1]).astype(bf16)
    mixed_h = gather_halves(mixed_rows)

    route_rows = near_first(routes.reshape(2, 2, local_rows, -1), 0, y_pos, c_pos)
    route_rows = route_rows.reshape(tok_rows, -1)
    choose = jnp.sum(
        (route_rows[:, :, None] == jnp.arange(experts, dtype=jnp.int32)[None, None, :]).astype(f32),
        axis=1,
    )
    choose_h = halves(choose)
    prob_h = [
        jax.nn.softmax(jnp.dot(m, router_b, preferred_element_type=f32), axis=-1)
        for m in mixed_h
    ]
    gate_w_h = [p * ch for p, ch in zip(prob_h, choose_h)]
    pre_h = [
        jnp.einsum("td,kedf->ketf", m, gu_b, preferred_element_type=f32) for m in mixed_h
    ]
    hidden_h = []
    for pre, gate_w in zip(pre_h, gate_w_h):
        gate_act = pre[0] * jax.nn.sigmoid(pre[0])
        hidden_h.append((gate_w.T[:, :, None] * gate_act * pre[1]).astype(bf16))
    expert_y = scatter_halves(
        [
            jnp.einsum("etf,edf->td", h, down_b, preferred_element_type=f32).astype(bf16)
            for h in hidden_h
        ]
    )
    out_local = residual + expert_y
    block_out = out_local.astype(bf16)
    cot_local = out_local - target.astype(f32)
    cot_h = gather_halves(cot_local.astype(bf16))

    d_pre_h = []
    d_mixed_parts = []
    router_parts = []
    for cot, pre, gate_w, prob, ch, mixed in zip(
        cot_h, pre_h, gate_w_h, prob_h, choose_h, mixed_h
    ):
        d_hid = (
            jnp.einsum("td,edf->etf", cot, down_b, preferred_element_type=f32)
            .astype(bf16)
            .astype(f32)
        )
        gate_in, up_in = pre[0], pre[1]
        gate_sig = jax.nn.sigmoid(gate_in)
        gate_act = gate_in * gate_sig
        d_gate_w = jnp.sum(d_hid * gate_act * up_in, axis=-1).T
        scaled = d_hid * gate_w.T[:, :, None]
        d_gate_in = scaled * up_in * gate_sig * (1.0 + gate_in * (1.0 - gate_sig))
        d_up_in = scaled * gate_act
        d_pre = jnp.stack([d_gate_in, d_up_in]).astype(bf16)
        d_pre_h.append(d_pre)
        d_prob = d_gate_w * ch
        d_logit = (prob * (d_prob - jnp.sum(prob * d_prob, axis=-1, keepdims=True))).astype(bf16)
        d_mixed_parts.append(
            (
                jnp.einsum("ketf,kedf->td", d_pre, gu_b, preferred_element_type=f32)
                + lax.dot_general(d_logit, router_b, DOT_NT, preferred_element_type=f32)
            ).astype(bf16)
        )
        router_parts.append(
            lax.dot_general(d_logit, mixed, (((0,), (0,)), ((), ())), preferred_element_type=f32)
        )
    router_rows = router_parts[0] + router_parts[1]
    d_mixed = scatter_halves(d_mixed_parts)
    gain_second = jnp.sum(d_mixed * hat_second, axis=0, keepdims=True)
    d_resid = cot_local + norm_back(d_mixed, hat_second, inv_second, norm_gains[1])
    d_resid_h = gather_halves(d_resid.astype(bf16))
    d_attn = jnp.concatenate(
        [jnp.dot(d, out_b, preferred_element_type=f32).astype(bf16) for d in d_resid_h]
    )

    d_attn_parts = jnp.moveaxis(d_attn.reshape(tok_rows, z_count, HEAD_DIM), 1, 0)
    d_out = lax.all_to_all(d_attn_parts, "z", 0, 0, tiled=True).reshape(line_rows, HEAD_DIM)
    delta = jnp.sum(d_out.astype(f32) * attn_f, axis=-1).reshape(1, line_rows)
    d_query = jnp.zeros((line_rows, HEAD_DIM), f32)
    d_kv = []
    for i, group in enumerate(groups):
        out_type = f32 if pair and i == 1 else bf16
        d_query, d_group = attend_grad(
            packed, d_out, row_lse, delta, tok_q, start_q, d_query, group, out_type
        )
        d_kv.append(d_group)
    if pair:
        d_kv = d_kv[1] + lax.ppermute(d_kv[0], "x", SWAP).astype(f32)
    else:
        d_kv = lax.psum_scatter(jnp.stack(d_kv), "x", scatter_dimension=0).astype(f32)
    inner = jnp.stack(
        [
            jnp.sum(d_query * packed[:, :HEAD_DIM].astype(f32), axis=-1),
            jnp.sum(d_kv[:, :HEAD_DIM] * packed[:, HEAD_DIM : 2 * HEAD_DIM].astype(f32), axis=-1),
        ]
    )
    inner = sum_line(sum_near(inner.reshape(2, z_count, 2, 2, local_rows)), z_count)
    inner = inner.reshape(2, line_rows) / model_width
    inv_line = jnp.moveaxis(inv_line, 0, 1).reshape(2, line_rows)
    coef = jnp.stack([inv_line[0], inner[0], inv_line[1], inner[1]], axis=1)
    head_gain = lax.dynamic_slice_in_dim(gain_qk, z_pos * HEAD_DIM, HEAD_DIM, 1)
    d_raw, gain_sums = raw_grad(
        d_query, d_kv, packed, coef, cos_tab, sin_tab, head_gain
    )
    gain_full = lax.dynamic_update_slice_in_dim(
        jnp.zeros((2, model_width), f32), gain_sums, (wt_pos * z_count + z_pos) * HEAD_DIM, 1
    )

    d_proj = jnp.moveaxis(
        to_tokens(d_raw, 3 * HEAD_DIM).reshape(z_count, tok_rows, 3, HEAD_DIM), 2, 0
    )
    d_proj = jnp.moveaxis(d_proj, 1, 2).reshape(3, tok_rows, head_cols)
    d_normed_h = [
        jnp.einsum("ktc,kdc->td", d, qkv_b, preferred_element_type=f32)
        for d in (d_proj[:, :half], d_proj[:, half:])
    ]
    d_normed = scatter_halves([d.astype(bf16) for d in d_normed_h])
    gain_first = jnp.sum(d_normed * hat_first, axis=0, keepdims=True)
    input_grad = (d_resid + norm_back(d_normed, hat_first, inv_first, norm_gains[0])).astype(bf16)

    def sum_all(a):
        a = a + lax.ppermute(a, "c", SWAP)
        a = a + lax.ppermute(a, "y", SWAP)
        a = a + lax.ppermute(a, "x", SWAP) if pair else lax.psum(a, "x")
        return sum_line(a, z_count)

    small = sum_all(jnp.concatenate([gain_second, gain_full, router_rows]))
    gains_grad = jnp.concatenate([sum_all(gain_first), small[:3]])
    router_grad = small[3:].T

    def scatter_x(a):
        if pair:
            mine = lax.dynamic_index_in_dim(a, x_pos, 0, False)
            other = lax.dynamic_index_in_dim(a, 1 - x_pos, 0, False)
            return mine.astype(f32) + lax.ppermute(other.astype(bf16), "x", SWAP).astype(f32)
        return lax.psum_scatter(a.astype(bf16), "x", scatter_dimension=0).astype(f32)

    def split_x(rows):
        a = rows.reshape(tok_rows, z_count, x_count, out_block)
        mine = lax.dynamic_index_in_dim(a, x_pos, 2, False)
        other = lax.dynamic_index_in_dim(a, 1 - x_pos, 2, False)
        return [mine, lax.ppermute(other, "x", SWAP)]

    def weight_grad(wide_h, narrow, spec):
        wide = jnp.concatenate(wide_h)
        if pair:
            narrow_far = lax.ppermute(narrow, "x", SWAP)
            mine, far = split_x(wide)
            part = jnp.einsum(spec, mine, narrow, preferred_element_type=f32)
            part = part + jnp.einsum(spec, far, narrow_far, preferred_element_type=f32)
        else:
            a = wide.reshape(tok_rows, z_count, x_count, out_block)
            part = scatter_x(
                jnp.stack(
                    [
                        jnp.einsum(spec, a[:, :, i], narrow, preferred_element_type=f32)
                        for i in range(x_count)
                    ]
                )
            )
        return scatter_line(part.astype(bf16), z_pos, z_count)

    down_part = weight_grad(cot_h, jnp.concatenate(hidden_h, axis=1), "tbd,etf->bedf")
    gate_up_part = weight_grad(mixed_h, jnp.concatenate(d_pre_h, axis=2), "tbd,ketf->bkedf")
    out_part = weight_grad(d_resid_h, attn_b, "tbd,tc->bdc")

    normed_all = jnp.concatenate(normed_h)
    normed_half = lax.dynamic_slice_in_dim(
        normed_all, c_pos * (model_width // 2), model_width // 2, 1
    )
    normed_half = lax.all_gather(normed_half, "z", axis=0, tiled=True)
    normed_other = lax.ppermute(normed_half, "c", SWAP)
    tn = (((0,), (0,)), ((), ()))
    grad_mine = lax.dot_general(normed_half, d_raw, tn, preferred_element_type=f32).astype(bf16)
    d_raw_other = jnp.flip(
        d_raw.reshape(z_count, 2, 2, local_rows, 3 * HEAD_DIM), 2
    ).reshape(line_rows, 3 * HEAD_DIM)
    grad_other = lax.dot_general(
        normed_other, d_raw_other, tn, preferred_element_type=f32
    ).astype(bf16)
    qkv_full = jnp.where(
        c_pos == 0,
        jnp.stack([grad_mine, grad_other]),
        jnp.stack([grad_other, grad_mine]),
    ).reshape(z_count, x_count, out_block, 3 * HEAD_DIM)
    qkv_line = scatter_x(jnp.moveaxis(qkv_full, 1, 0)).astype(bf16)
    qkv_heads = lax.all_to_all(qkv_line, "z", 0, 0, tiled=True)
    qkv_part = (
        qkv_heads.reshape(z_count, out_block, 3, HEAD_DIM)
        .transpose(2, 1, 0, 3)
        .reshape(3, out_block, head_cols)
        .astype(f32)
    )
    return (
        block_out,
        input_grad,
        qkv_part,
        out_part,
        gains_grad,
        router_grad,
        gate_up_part,
        down_part,
    )


def solution(mesh):
    ctx_count = mesh.shape["ctx"]

    def run(*args):
        heads = args[5].shape[2] // HEAD_DIM
        z_count = heads // mesh.shape["wt"]
        x_count = ctx_count // z_count
        grid = Mesh(mesh.devices.reshape(z_count, x_count, 2, 2), ("z", "x", "y", "c"))
        ctx, wt = ("z", "x"), ("y", "c")
        return jax.shard_map(
            functools.partial(local, z_count, x_count),
            mesh=grid,
            in_specs=(
                P(ctx + wt, None),
                P(ctx + wt, None),
                P(),
                P(),
                P(ctx, None),
                P(None, None, wt),
                P(None, wt),
                P(),
                P(),
                P(None, None, None, wt),
                P(None, None, wt),
            ),
            out_specs=(
                P(ctx + wt, None),
                P(ctx + wt, None),
                P(None, ctx, wt),
                P(ctx, wt),
                P(),
                P(),
                P(None, None, ctx, wt),
                P(None, ctx, wt),
            ),
            check_vma=False,
        )(*args)

    return run
```

```python
import functools
import math

import jax
import jax.numpy as jnp
from jax import lax
from jax.experimental import pallas as pl
from jax.experimental.pallas import tpu as pltpu
from jax.sharding import Mesh
from jax.sharding import PartitionSpec as P

HEAD_DIM = 128
LOG2E = math.log2(math.e)
VMEM_BYTES = 56 * 1024 * 1024

norm_eps = 1e-05
f32 = jnp.float32
bf16 = jnp.bfloat16

SWAP = [(0, 1), (1, 0)]


def cost(us):
    return pl.CostEstimate(flops=int(us * 1e9), bytes_accessed=1 << 20, transcendentals=0)
DOT_NT = (((1,), (1,)), ((), ()))
DOT_NN = (((1,), (0,)), ((), ()))


def attend_kernel(groups, chunk, score_scale, q_ref, tok_q_ref, start_q_ref, *refs):
    key_refs = refs[: 3 * groups]
    o_ref, lse_ref = refs[-groups - 2 : -groups]
    vt_refs = refs[-groups:]
    rows = q_ref.shape[0]

    @pl.when(pl.program_id(0) == 0)
    def _():
        for g in range(groups):
            v_ref, vt_ref = key_refs[3 * g + 1], vt_refs[g]

            def turn(j, carry):
                r = pl.ds(pl.multiple_of(j * chunk, chunk), chunk)
                vt_ref[:, r] = v_ref[r, :].T
                return carry

            lax.fori_loop(0, v_ref.shape[0] // chunk, turn, 0)

    queries = q_ref[...]
    tok_q = tok_q_ref[...]
    start_q = start_q_ref[...]
    state = (
        jnp.full((1, rows), -1e30, f32),
        jnp.zeros((1, rows), f32),
        jnp.zeros((queries.shape[1], rows), f32),
    )
    for g in range(groups):
        k_ref, _, tok_k_ref = key_refs[3 * g : 3 * g + 3]
        vt_ref = vt_refs[g]

        def step(j, carry):
            run_max, run_sum, acc = carry
            r = pl.ds(pl.multiple_of(j * chunk, chunk), chunk)
            s = lax.dot_general(k_ref[r, :], queries, DOT_NT, preferred_element_type=f32)
            tok_k = tok_k_ref[r, :]
            s = jnp.where((tok_k <= tok_q) & (tok_k >= start_q), s * score_scale, -1e30)
            new_max = jnp.maximum(run_max, jnp.max(s, axis=0, keepdims=True))
            p = jnp.exp2(s - new_max)
            shrink = jnp.exp2(run_max - new_max)
            run_sum = run_sum * shrink + jnp.sum(p, axis=0, keepdims=True)
            acc = acc * shrink + lax.dot_general(
                vt_ref[:, r], p.astype(bf16), DOT_NN, preferred_element_type=f32
            )
            return new_max, run_sum, acc

        steps = k_ref.shape[0] // chunk
        state = lax.fori_loop(0, steps, step, state, unroll=steps <= 4)
    run_max, run_sum, acc = state
    o_ref[...] = (acc / run_sum).T
    lse_ref[...] = run_max + jnp.log2(run_sum)


def attend(queries, tok_q, start_q, key_groups, earlier=()):
    rows = queries.shape[0]
    block = min(1024, rows)
    chunk = 1024
    row = pl.BlockSpec((1, block), lambda i: (0, i))
    in_specs = [pl.BlockSpec((block, HEAD_DIM), lambda i: (i, 0)), row, row]
    operands = [queries, tok_q, start_q]
    scratch = []
    keys = 0
    for group in key_groups:
        count = group[0].shape[0]
        keys += count
        in_specs += [pl.BlockSpec(a.shape, lambda i: (0, 0)) for a in group]
        operands += group
        scratch.append(pltpu.VMEM((HEAD_DIM, count), bf16))
    in_specs += [pl.BlockSpec(memory_space=pl.ANY)] * len(earlier)
    operands += earlier
    return pl.pallas_call(
        functools.partial(
            attend_kernel, len(key_groups), chunk, LOG2E / math.sqrt(HEAD_DIM)
        ),
        grid=(rows // block,),
        in_specs=in_specs,
        out_specs=[pl.BlockSpec((block, HEAD_DIM), lambda i: (i, 0)), row],
        out_shape=[
            jax.ShapeDtypeStruct((rows, HEAD_DIM), f32),
            jax.ShapeDtypeStruct((1, rows), f32),
        ],
        scratch_shapes=scratch,
        compiler_params=pltpu.CompilerParams(vmem_limit_bytes=VMEM_BYTES),
        cost_estimate=cost(8),
        name="attend",
    )(*operands)


def attend_grad_kernel(
    chunk,
    score_scale,
    grad_scale,
    q_ref,
    do_ref,
    lse_ref,
    delta_ref,
    tok_q_ref,
    start_q_ref,
    dq_in_ref,
    k_ref,
    v_ref,
    tok_k_ref,
    *refs,
):
    dq_ref, dk_ref, dv_ref, kt_ref, dk_acc, dv_acc = refs[-6:]
    steps = k_ref.shape[0] // chunk

    @pl.when(pl.program_id(0) == 0)
    def _():
        dk_acc[...] = jnp.zeros_like(dk_acc)
        dv_acc[...] = jnp.zeros_like(dv_acc)

        def turn(j, carry):
            r = pl.ds(pl.multiple_of(j * chunk, chunk), chunk)
            kt_ref[:, r] = k_ref[r, :].T
            return carry

        lax.fori_loop(0, steps, turn, 0)

    queries = q_ref[...]
    d_out = do_ref[...]
    tok_q = tok_q_ref[...]
    start_q = start_q_ref[...]
    lse = lse_ref[...]
    delta = delta_ref[...]

    def step(j, dq_t):
        r = pl.ds(pl.multiple_of(j * chunk, chunk), chunk)
        s = lax.dot_general(k_ref[r, :], queries, DOT_NT, preferred_element_type=f32)
        tok_k = tok_k_ref[r, :]
        allowed = (tok_k <= tok_q) & (tok_k >= start_q)
        p = jnp.exp2(jnp.where(allowed, s * score_scale - lse, -1e30))
        dp = lax.dot_general(v_ref[r, :], d_out, DOT_NT, preferred_element_type=f32)
        ds = (p * (dp - delta)).astype(bf16)
        dv_acc[r, :] += lax.dot_general(
            p.astype(bf16), d_out, DOT_NN, preferred_element_type=f32
        )
        dk_acc[r, :] += lax.dot_general(ds, queries, DOT_NN, preferred_element_type=f32)
        return dq_t + lax.dot_general(kt_ref[:, r], ds, DOT_NN, preferred_element_type=f32)

    dq_t = lax.fori_loop(
        0,
        steps,
        step,
        jnp.zeros((queries.shape[1], queries.shape[0]), f32),
        unroll=steps <= 4,
    )
    dq_ref[...] = dq_in_ref[...] + (dq_t * grad_scale).T

    @pl.when(pl.program_id(0) == pl.num_programs(0) - 1)
    def _():
        dk_ref[...] = (dk_acc[...] * grad_scale).astype(dk_ref.dtype)
        dv_ref[...] = dv_acc[...].astype(dv_ref.dtype)


def attend_grad(
    queries, d_out, lse, delta, tok_q, start_q, dq_in, key_group, out_type, earlier=()
):
    rows = queries.shape[0]
    keys = key_group[0].shape[0]
    block = min(1024, rows)
    chunk = 1024
    row = pl.BlockSpec((1, block), lambda i: (0, i))
    head = pl.BlockSpec((block, HEAD_DIM), lambda i: (i, 0))
    whole = pl.BlockSpec((keys, HEAD_DIM), lambda i: (0, 0))
    return pl.pallas_call(
        functools.partial(
            attend_grad_kernel,
            chunk,
            LOG2E / math.sqrt(HEAD_DIM),
            1.0 / math.sqrt(HEAD_DIM),
        ),
        grid=(rows // block,),
        in_specs=[
            head,
            head,
            row,
            row,
            row,
            row,
            head,
            whole,
            whole,
            pl.BlockSpec((keys, 1), lambda i: (0, 0)),
        ]
        + [pl.BlockSpec(memory_space=pl.ANY)] * len(earlier),
        out_specs=[head, whole, whole],
        out_shape=[
            jax.ShapeDtypeStruct((rows, HEAD_DIM), f32),
            jax.ShapeDtypeStruct((keys, HEAD_DIM), out_type),
            jax.ShapeDtypeStruct((keys, HEAD_DIM), out_type),
        ],
        scratch_shapes=[
            pltpu.VMEM((HEAD_DIM, keys), bf16),
            pltpu.VMEM((keys, HEAD_DIM), f32),
            pltpu.VMEM((keys, HEAD_DIM), f32),
        ],
        compiler_params=pltpu.CompilerParams(vmem_limit_bytes=VMEM_BYTES),
        cost_estimate=cost(8),
        name="attend_grad",
    )(queries, d_out, lse, delta, tok_q, start_q, dq_in, *key_group, *earlier)


def pack_kernel(raw0_ref, raw1_ref, inv_ref, cos_ref, sin_ref, gain_ref, q_ref, k_ref):
    half = raw0_ref.shape[1]
    for i, raw_ref in enumerate((raw0_ref, raw1_ref)):
        r = slice(i * half, (i + 1) * half)
        for j in range(2):
            u = raw_ref[j] * inv_ref[r, j : j + 1] * gain_ref[j : j + 1, :]
            turned = u * cos_ref[r, :] + pltpu.roll(u, HEAD_DIM // 2, 1) * sin_ref[r, :]
            (q_ref, k_ref)[j][0, r, :] = turned.astype(bf16)


def pack_heads(raw0, raw1, inv, cos_tab, sin_tab, gains):
    half = raw0.shape[1]
    rows = 2 * half
    heads = raw0.shape[2] // HEAD_DIM
    raw = pl.BlockSpec((2, half, HEAD_DIM), lambda h: (0, 0, h))
    head = pl.BlockSpec((1, rows, HEAD_DIM), lambda h: (h, 0, 0))
    table = pl.BlockSpec((rows, HEAD_DIM), lambda h: (0, 0))
    return pl.pallas_call(
        pack_kernel,
        grid=(heads,),
        in_specs=[
            raw,
            raw,
            pl.BlockSpec((rows, 2), lambda h: (0, 0)),
            table,
            table,
            pl.BlockSpec((2, HEAD_DIM), lambda h: (0, h)),
        ],
        out_specs=[head, head],
        out_shape=[jax.ShapeDtypeStruct((heads, rows, HEAD_DIM), bf16)] * 2,
        cost_estimate=cost(3),
        name="pack_heads",
    )(raw0, raw1, inv, cos_tab, sin_tab, gains)


def raw_grad_kernel(
    dq_ref, dk_ref, dv_ref, q_ref, k_ref, coef_ref, cos_ref, sin_ref, gain_ref, *refs
):
    out_ref, sum_ref = refs[-2:]

    @pl.when(pl.program_id(0) == 0)
    def _():
        sum_ref[...] = jnp.zeros_like(sum_ref)

    cos_tab = cos_ref[...]
    sin_tab = sin_ref[...]

    def turn_back(u):
        return u * cos_tab - pltpu.roll(u, HEAD_DIM // 2, 1) * sin_tab

    for j, (grad_ref, rows_ref) in enumerate(((dq_ref, q_ref), (dk_ref, k_ref))):
        gain = gain_ref[j : j + 1, :]
        cols = slice(j * HEAD_DIM, (j + 1) * HEAD_DIM)
        d_norm = turn_back(grad_ref[...])
        hat = turn_back(rows_ref[...].astype(f32)) / gain
        sum_ref[j : j + 1, :] += jnp.sum(d_norm * hat, axis=0, keepdims=True)
        inv = coef_ref[:, 2 * j : 2 * j + 1]
        inner = coef_ref[:, 2 * j + 1 : 2 * j + 2]
        out_ref[:, cols] = (inv * (d_norm * gain - hat * inner)).astype(bf16)
    out_ref[:, 2 * HEAD_DIM :] = dv_ref[...].astype(bf16)


def raw_grad(d_query, d_key, d_value, queries, keys, coef, cos_tab, sin_tab, gains):
    rows = queries.shape[0]
    block = min(512, rows)

    def wide(cols):
        return pl.BlockSpec((block, cols), lambda i: (i, 0))

    whole = pl.BlockSpec((2, HEAD_DIM), lambda i: (0, 0))
    return pl.pallas_call(
        raw_grad_kernel,
        grid=(rows // block,),
        in_specs=[
            *[wide(HEAD_DIM)] * 5,
            wide(4),
            wide(HEAD_DIM),
            wide(HEAD_DIM),
            whole,
        ],
        out_specs=[wide(3 * HEAD_DIM), whole],
        out_shape=[
            jax.ShapeDtypeStruct((rows, 3 * HEAD_DIM), bf16),
            jax.ShapeDtypeStruct((2, HEAD_DIM), f32),
        ],
        cost_estimate=cost(3),
        name="raw_grad",
    )(d_query, d_key, d_value, queries, keys, coef, cos_tab, sin_tab, gains)


def weight_grad_kernel(pieces, experts, out_block, at_ref, *refs):
    wide0, wide1, wide_far = refs[:3]
    narrow = refs[3 : 3 + pieces]
    out_ref, wide_t, tall = refs[-3:]
    half = wide0.shape[0]
    blocks = wide_far.shape[1] // out_block

    @pl.when(pl.program_id(0) == 0)
    def _():
        for z in range(blocks):
            rows = slice(z * out_block, (z + 1) * out_block)
            cols = (2 * z + at_ref[0]) * out_block
            cols = pl.ds(pl.multiple_of(cols, out_block), out_block)
            for i, piece in enumerate((wide0, wide1)):
                wide_t[rows, i * half : (i + 1) * half] = piece[:, cols].T
            wide_t[rows, 2 * half :] = wide_far[:, rows].T

    at = 0
    for i, piece in enumerate(narrow):
        if experts and i == pieces - 1:
            routes = refs[3 + pieces][...]
            e = lax.rem(pl.program_id(0), experts)
            block = jnp.zeros(piece.shape[2:], f32)
            for slot in range(piece.shape[1]):
                block = jnp.where(routes[:, slot : slot + 1] == e, piece[0, slot].astype(f32), block)
            block = block.astype(bf16)
        else:
            block = piece[...].reshape(piece.shape[-2:])
        tall[at : at + block.shape[0], :] = block
        at += block.shape[0]
    out = jnp.dot(wide_t[...], tall[...], preferred_element_type=f32)
    out_ref[...] = out.astype(bf16).reshape(out_ref.shape)


def weight_grad(wide_h, wide_far, narrow, out_block, at, routes=None, experts=0, earlier=()):
    half, width = wide_h[0].shape
    out_width = wide_far.shape[1]
    specs = []
    operands = []
    for piece in narrow:
        if isinstance(piece, tuple):
            array, row = piece
            cols = 256
            count = array.shape[1] // cols
            specs.append(pl.BlockSpec((half, cols), lambda j, x, row=row: (row, j)))
            operands.append(array)
        elif piece.ndim == 4:
            kinds, slots, rows, cols = piece.shape
            count = kinds * experts
            specs.append(
                pl.BlockSpec((1, slots, rows, cols), lambda j, x: (j // experts, 0, 0, 0))
            )
            operands.append(piece)
        else:
            count, rows, cols = piece.shape
            specs.append(pl.BlockSpec((1, rows, cols), lambda j, x: (j, 0, 0)))
            operands.append(piece)
    if experts:
        specs.append(pl.BlockSpec(routes.shape, lambda j, x: (0, 0)))
        operands.append(routes)

    def kernel(x_ref, *refs):
        used = 3 + len(operands)
        weight_grad_kernel(len(narrow), experts, out_block, x_ref, *refs[:used], *refs[-3:])

    return pl.pallas_call(
        kernel,
        grid_spec=pltpu.PrefetchScalarGridSpec(
            num_scalar_prefetch=1,
            grid=(count,),
            in_specs=[pl.BlockSpec(w.shape, lambda j, x: (0, 0)) for w in (*wide_h, wide_far)]
            + specs
            + [pl.BlockSpec(memory_space=pl.ANY)] * len(earlier),
            out_specs=pl.BlockSpec((1, out_width, cols), lambda j, x: (j, 0, 0)),
            scratch_shapes=[
                pltpu.VMEM((out_width, 4 * half), bf16),
                pltpu.VMEM((4 * half, cols), bf16),
            ],
        ),
        out_shape=jax.ShapeDtypeStruct((count, out_width, cols), bf16),
        compiler_params=pltpu.CompilerParams(vmem_limit_bytes=VMEM_BYTES),
        cost_estimate=cost(0.1),
        name="weight_grad",
    )(at.reshape(1), *wide_h, wide_far, *operands, *earlier)


def waits(earlier):
    return [pl.BlockSpec(memory_space=pl.ANY)] * len(earlier)


def params():
    return pltpu.CompilerParams(vmem_limit_bytes=VMEM_BYTES)


def attn_out_grad_kernel(a_ref, w_ref, *refs):
    out_ref = refs[-1]
    y = jnp.dot(a_ref[...], w_ref[...], preferred_element_type=f32).astype(bf16)
    for h in range(out_ref.shape[0]):
        out_ref[h] = y[:, h * HEAD_DIM : (h + 1) * HEAD_DIM]


def attn_out_grad_half(grads, half, weights, into=None, earlier=()):
    count, width = grads.shape
    cols = weights.shape[1]
    heads = cols // HEAD_DIM
    block = cols // 2
    row = pl.BlockSpec((count, width), lambda j: (0, 0))
    into = () if into is None else (into,)
    return pl.pallas_call(
        attn_out_grad_kernel,
        grid=(2,),
        in_specs=[row, pl.BlockSpec((width, block), lambda j: (0, j))]
        + waits(into)
        + waits(earlier),
        out_specs=pl.BlockSpec((heads // 2, count, HEAD_DIM), lambda j: (j, half, 0)),
        out_shape=jax.ShapeDtypeStruct((heads, 2 * count, HEAD_DIM), bf16),
        input_output_aliases={2: 0} if into else {},
        compiler_params=params(),
        cost_estimate=cost(1),
        name="attn_out_grad",
    )(grads, weights, *into, *earlier)


def project_grad_kernel(x_ref, w_ref, n_ref, *refs):
    out_ref, sum_ref, rows = refs[-3:]
    heads = x_ref.shape[0]
    cols = heads * HEAD_DIM

    @pl.when(pl.program_id(0) == 0)
    def _():
        for k in range(3):
            for h in range(heads):
                at = k * cols + h * HEAD_DIM
                rows[:, at : at + HEAD_DIM] = x_ref[h, :, k * HEAD_DIM : (k + 1) * HEAD_DIM]

    y = None
    for k in range(3):
        term = lax.dot_general(
            rows[:, k * cols : (k + 1) * cols], w_ref[k], DOT_NT, preferred_element_type=f32
        )
        y = term if y is None else y + term
    out_ref[...] = y.astype(bf16)
    sum_ref[...] = jnp.sum(y * n_ref[...].astype(f32), axis=0, keepdims=True)


def project_grad_half(parts, half, weights, normed, earlier=()):
    heads, count, cols = parts.shape
    count //= 2
    width = weights.shape[1]
    block = width // 4
    out = pl.BlockSpec((count, block), lambda i: (0, i))
    return pl.pallas_call(
        project_grad_kernel,
        grid=(4,),
        in_specs=[
            pl.BlockSpec((heads, count, cols), lambda i: (0, half, 0)),
            pl.BlockSpec((3, block, weights.shape[2]), lambda i: (0, i, 0)),
            out,
        ]
        + waits(earlier),
        out_specs=[out, pl.BlockSpec((1, block), lambda i: (0, i))],
        out_shape=[
            jax.ShapeDtypeStruct((count, width), bf16),
            jax.ShapeDtypeStruct((1, width), f32),
        ],
        scratch_shapes=[pltpu.VMEM((count, heads * cols), bf16)],
        compiler_params=params(),
        cost_estimate=cost(1),
        name="project_grad",
    )(parts, weights, normed, *earlier)


def row_sum(refs):
    return refs[0][...].astype(f32) + refs[1][...].astype(f32) + refs[2][...].astype(f32)


def inv_rms(rows):
    return lax.rsqrt(jnp.mean(rows * rows, axis=-1, keepdims=True) + norm_eps)


def mix_kernel(near, near_got, far_got, in_ref, gain_ref, *refs):
    residual_ref, mixed_ref = refs[-2:]
    residual = in_ref[...].astype(f32) + row_sum((near, near_got, far_got))
    residual_ref[...] = residual
    mixed_ref[...] = (residual * inv_rms(residual) * gain_ref[...]).astype(bf16)


def gap_kernel(near, near_got, far_got, residual_ref, target_ref, *refs):
    out_ref, gap_ref, gap_b_ref = refs[-3:]
    out = residual_ref[...] + row_sum((near, near_got, far_got))
    out_ref[...] = out.astype(bf16)
    gap = out - target_ref[...].astype(f32)
    gap_ref[...] = gap
    gap_b_ref[...] = gap.astype(bf16)


def resid_grad_kernel(near, near_got, far_got, residual_ref, gap_ref, gain_ref, *refs):
    grad_ref, grad_b_ref, sum_ref = refs[-3:]
    d_mixed = row_sum((near, near_got, far_got))
    residual = residual_ref[...]
    inv = inv_rms(residual)
    hat = residual * inv
    grad = gap_ref[...] + norm_back(d_mixed, hat, inv, gain_ref[...])
    grad_ref[...] = grad
    grad_b_ref[...] = grad.astype(bf16)

    @pl.when(pl.program_id(0) == 0)
    def _():
        sum_ref[...] = jnp.zeros_like(sum_ref)

    sum_ref[...] += jnp.sum(d_mixed * hat, axis=0, keepdims=True)


def input_grad_kernel(near, near_got, far_got, in_ref, grad_ref, gain_ref, *refs):
    rows = in_ref[...].astype(f32)
    inv = inv_rms(rows)
    d_normed = row_sum((near, near_got, far_got))
    grad = grad_ref[...] + norm_back(d_normed, rows * inv, inv, gain_ref[...])
    refs[-1][...] = grad.astype(bf16)


def row_call(kernel, terms, rows, gain, outs, earlier=()):
    count, width = rows[0].shape
    block = min(32, count)
    spec = pl.BlockSpec((block, width), lambda i: (i, 0))
    line = pl.BlockSpec((1, width), lambda i: (0, 0))
    gains = [] if gain is None else [gain.reshape(1, width)]
    return pl.pallas_call(
        kernel,
        grid=(count // block,),
        in_specs=[spec] * (len(terms) + len(rows))
        + [line] * len(gains)
        + [pl.BlockSpec(memory_space=pl.ANY)] * len(earlier),
        out_specs=[line if o is None else spec for o in outs],
        out_shape=[
            jax.ShapeDtypeStruct((1, width) if o is None else (count, width), f32 if o is None else o)
            for o in outs
        ],
        compiler_params=pltpu.CompilerParams(vmem_limit_bytes=VMEM_BYTES),
        cost_estimate=cost(0.1),
        name=kernel.__name__,
    )(*terms, *rows, *gains, *earlier)


def pick_kernel(cols, z_count, c_ref, r0_ref, r1_ref, *refs):
    out_ref = refs[-1]
    half = r0_ref.shape[0]
    out_ref[:half] = r0_ref[...]
    out_ref[half:] = r1_ref[...]


def pick_half(rows_h, at, earlier=()):
    half, width = rows_h[0].shape
    cols = width // 2
    block = cols // 2
    return pl.pallas_call(
        functools.partial(pick_kernel, cols, 2),
        grid_spec=pltpu.PrefetchScalarGridSpec(
            num_scalar_prefetch=1,
            grid=(2,),
            in_specs=[pl.BlockSpec((half, block), lambda j, c: (0, 2 * c[0] + j))] * 2
            + [pl.BlockSpec(memory_space=pl.ANY)] * len(earlier),
            out_specs=pl.BlockSpec((2 * half, block), lambda j, c: (0, j)),
        ),
        out_shape=jax.ShapeDtypeStruct((2 * half, cols), rows_h[0].dtype),
        cost_estimate=cost(0.1),
        name="pick_half",
    )(at.reshape(1), *rows_h, *earlier)


def token_places(seq_lengths, permutation):
    seq_ends = jnp.cumsum(seq_lengths)
    seq_starts = seq_ends - seq_lengths
    seq_id = jnp.sum((permutation[:, None] >= seq_ends[None, :]).astype(jnp.int32), axis=1)
    member = seq_id[:, None] == jnp.arange(seq_lengths.shape[0], dtype=jnp.int32)[None, :]
    return jnp.sum(jnp.where(member, seq_starts[None, :], 0), axis=1)


def near_first(a, axis, y_pos, c_pos):
    a = jnp.where(y_pos == 0, a, jnp.flip(a, axis))
    return jnp.where(c_pos == 0, a, jnp.flip(a, axis + 1))


def norm_back(grad_out, hat_rows, inv_rows, gain_row):
    grad_hat = grad_out * gain_row
    return inv_rows * (grad_hat - hat_rows * jnp.mean(grad_hat * hat_rows, axis=-1, keepdims=True))


def gather_halves(rows):
    core = lax.ppermute(rows, "c", SWAP)
    far = lax.ppermute(rows, "y", SWAP)
    far_core = lax.ppermute(far, "c", SWAP)
    return [jnp.concatenate([rows, core]), jnp.concatenate([far, far_core])]


def scatter_halves(parts):
    near, far = parts
    n = near.shape[0] // 2
    sent = far[:n].astype(f32) + lax.ppermute(far[n:], "c", SWAP).astype(f32)
    sent = sent.astype(bf16)
    far_got = lax.ppermute(sent, "y", SWAP)
    near_got = lax.ppermute(near[n:], "c", SWAP)
    return (near, near_got, far_got), sent


def gather_line(a, z_pos, z_count):
    last = z_count - 1
    up = down = a
    ups, downs = [], []
    for s in range(last):
        up = lax.ppermute(up, "z", [(i, i + 1) for i in range(s, last)])
        down = lax.ppermute(down, "z", [(i, i - 1) for i in range(1, z_count - s)])
        ups.append(up)
        downs.append(down)
    near = [a] + [
        jnp.where(z_pos >= s + 1, ups[s], downs[last - 1 - s]) for s in range(last)
    ]
    near = jnp.stack(near)
    return ups, downs, jnp.concatenate(
        [
            lax.dynamic_index_in_dim(near, (z_pos - z + z_count) % z_count, 0, False)
            for z in range(z_count)
        ]
    )


def sum_near(a):
    a = a + jnp.flip(lax.ppermute(a, "c", SWAP), -2)
    return a + jnp.flip(lax.ppermute(a, "y", SWAP), -3)


def sum_line(a, z_count):
    step = 1
    while step < z_count:
        a = a + lax.ppermute(a, "z", [(i, i ^ step) for i in range(z_count)])
        step *= 2
    return a


def local(
    z_count,
    x_count,
    block_in,
    target,
    seq_lengths,
    permutation,
    routes,
    attn_qkv,
    attn_out,
    norm_gains,
    router,
    gate_up,
    down,
):
    z_pos = lax.axis_index("z")
    x_pos = lax.axis_index("x")
    y_pos = lax.axis_index("y")
    c_pos = lax.axis_index("c")
    pair = x_count == 2
    local_rows, model_width = block_in.shape
    tok_rows = 4 * local_rows
    line_rows = z_count * tok_rows
    head_cols = attn_qkv.shape[2]
    hidden_cols = gate_up.shape[3]
    experts = gate_up.shape[1]
    wide_block = model_width // z_count
    out_block = wide_block // x_count
    wt_pos = y_pos * 2 + c_pos

    qkv_b = attn_qkv.astype(bf16)
    out_b = attn_out.astype(bf16)
    gu_b = gate_up.astype(bf16)
    down_b = down.astype(bf16)
    router_b = router.astype(bf16)

    def scatter_x(a):
        if pair:
            mine = lax.dynamic_index_in_dim(a, x_pos, 0, False)
            other = lax.dynamic_index_in_dim(a, 1 - x_pos, 0, False)
            return mine.astype(f32) + lax.ppermute(other.astype(bf16), "x", SWAP).astype(f32)
        return lax.psum_scatter(a.astype(bf16), "x", scatter_dimension=0).astype(f32)

    def of_parity(rows_h, at):
        return jnp.concatenate(
            [
                jnp.concatenate(
                    [
                        lax.dynamic_slice_in_dim(
                            r, z * wide_block + at * out_block, out_block, 1
                        )
                        for z in range(z_count)
                    ],
                    axis=1,
                )
                for r in rows_h
            ]
        )

    def far_wide(rows_h):
        return lax.ppermute(of_parity(rows_h, 1 - x_pos), "x", SWAP)

    def swap_x(parts):
        return [lax.ppermute(p, "x", SWAP) for p in parts]

    resid_in = block_in.astype(f32)
    inv_first = lax.rsqrt(jnp.mean(resid_in * resid_in, axis=-1, keepdims=True) + norm_eps)
    hat_first = resid_in * inv_first
    normed = (hat_first * norm_gains[0]).astype(bf16)
    normed_h = gather_halves(normed)

    start_all = token_places(seq_lengths, permutation)
    shape = (z_count, x_count, 2, 2, local_rows)
    tok_all = near_first(permutation.reshape(shape), 2, y_pos, c_pos)
    start_all = near_first(start_all.reshape(shape), 2, y_pos, c_pos)

    def of_x(a, at):
        return lax.dynamic_index_in_dim(a, at, 1, False).reshape(line_rows)

    tok_own = of_x(tok_all, x_pos)
    start_own = of_x(start_all, x_pos)
    tok_q = tok_own.reshape(1, line_rows)
    start_q = start_own.reshape(1, line_rows)
    half_dim = HEAD_DIM // 2
    frequency = jnp.exp(
        jnp.arange(half_dim, dtype=f32) * (-2.0 * math.log(10000.0) / HEAD_DIM)
    )
    angles = (tok_own - start_own).astype(f32)[:, None] * frequency[None, :]
    cosine, sine = jnp.cos(angles), jnp.sin(angles)
    cos_tab = jnp.concatenate([cosine, cosine], axis=1)
    sin_tab = jnp.concatenate([-sine, sine], axis=1)

    raw_h = [
        jnp.einsum("td,kdc->ktc", n, qkv_b, preferred_element_type=f32) for n in normed_h
    ]
    squares = jnp.concatenate([jnp.sum(r[:2] * r[:2], axis=-1) for r in raw_h], axis=1)
    squares = sum_near(squares.reshape(2, 2, 2, local_rows)).reshape(2, tok_rows)
    inv_qk = lax.rsqrt(squares / model_width + norm_eps)
    inv_slots = jnp.where(
        (jnp.arange(z_count, dtype=jnp.int32) == z_pos)[:, None, None], inv_qk[None], 0.0
    )
    inv_line = sum_line(inv_slots, z_count)
    gain_qk = lax.dynamic_slice_in_dim(norm_gains[2:], wt_pos * head_cols, head_cols, 1)

    normed_pick = pick_half(normed_h, c_pos)

    def to_heads_apart(parts):
        near = [lax.dynamic_index_in_dim(parts, z_pos, 0, False)]
        for d in range(1, z_count):
            there = lax.dynamic_index_in_dim(parts, (z_pos + d) % z_count, 0, False)
            near.append(
                lax.ppermute(there, "z", [(i, (i + d) % z_count) for i in range(z_count)])
            )
        near = jnp.stack(near)
        return jnp.concatenate(
            [
                lax.dynamic_index_in_dim(near, (z_pos - z + z_count) % z_count, 0, False)
                for z in range(z_count)
            ]
        )

    def to_heads(parts):
        return lax.all_to_all(parts, "z", 0, 0, tiled=True).reshape(line_rows, HEAD_DIM)

    def from_x(a):
        if pair:
            return lax.ppermute(a, "x", SWAP)
        return lax.all_gather(a, "x", axis=0)

    v_heads = jnp.concatenate(
        [
            jnp.moveaxis(r[2].astype(bf16).reshape(-1, z_count, HEAD_DIM), 1, 0)
            for r in raw_h
        ],
        axis=1,
    )
    values = to_heads(v_heads)
    values_far = from_x(values)
    q_heads, k_heads = pack_heads(
        raw_h[0],
        raw_h[1],
        inv_qk.T,
        lax.dynamic_slice_in_dim(cos_tab, z_pos * tok_rows, tok_rows),
        lax.dynamic_slice_in_dim(sin_tab, z_pos * tok_rows, tok_rows),
        gain_qk,
    )
    keys = to_heads_apart(k_heads)
    keys_far = from_x(keys)
    queries = to_heads_apart(q_heads)
    tok_col = tok_own.reshape(line_rows, 1)
    if pair:
        tok_far = of_x(tok_all, 1 - x_pos).reshape(line_rows, 1)
        groups = [(keys_far, values_far, tok_far), (keys, values, tok_col)]
        key_groups = groups[::-1]
    else:
        tok_x = jnp.moveaxis(tok_all, 1, 0).reshape(x_count, line_rows, 1)
        groups = [(keys_far[i], values_far[i], tok_x[i]) for i in range(x_count)]
        key_groups = [
            (
                keys_far.reshape(-1, HEAD_DIM),
                values_far.reshape(-1, HEAD_DIM),
                tok_x.reshape(-1, 1),
            )
        ]
    attn_f, row_lse = attend(
        queries, tok_q, start_q, key_groups, (normed_pick,)
    )

    def to_tokens(rows, cols):
        parts = lax.all_to_all(
            rows.reshape(z_count, tok_rows, cols), "z", 0, 0, tiled=True
        )
        return parts

    attn_parts = to_tokens(attn_f.astype(bf16), HEAD_DIM)
    attn_b = jnp.moveaxis(attn_parts, 0, 1).reshape(tok_rows, head_cols)
    normed_up, normed_down, normed_half = gather_line(normed_pick, z_pos, z_count)
    attn_far = lax.ppermute(attn_b, "x", SWAP) if pair else attn_b
    half = tok_rows // 2

    def halves(a):
        return [a[:half], a[half:]]

    attn_y, _ = scatter_halves(
        [
            lax.dot_general(a, out_b, DOT_NT, preferred_element_type=f32).astype(bf16)
            for a in halves(attn_b)
        ]
    )
    residual, mixed_rows = row_call(
        mix_kernel, attn_y, (block_in,), norm_gains[1], (f32, bf16),
        (normed_up[0], normed_down[0], attn_far),
    )
    mixed_h = gather_halves(mixed_rows)
    mixed_far = far_wide(mixed_h) if pair else mixed_rows

    route_rows = near_first(routes.reshape(2, 2, local_rows, -1), 0, y_pos, c_pos)
    route_rows = route_rows.reshape(tok_rows, -1)
    if pair:
        routes_far = lax.ppermute(route_rows.T.astype(f32), "x", SWAP).T.astype(jnp.int32)
    choose = jnp.sum(
        (route_rows[:, :, None] == jnp.arange(experts, dtype=jnp.int32)[None, None, :]).astype(f32),
        axis=1,
    )
    choose_h = halves(choose)
    prob_h = [
        jax.nn.softmax(jnp.dot(m, router_b, preferred_element_type=f32), axis=-1)
        for m in mixed_h
    ]
    gate_w_h = [p * ch for p, ch in zip(prob_h, choose_h)]
    pre_h = [
        jnp.einsum("td,kedf->ketf", m, gu_b, preferred_element_type=f32) for m in mixed_h
    ]
    hidden_h = []
    for pre, gate_w in zip(pre_h, gate_w_h):
        gate_act = pre[0] * jax.nn.sigmoid(pre[0])
        hidden_h.append((gate_w.T[:, :, None] * gate_act * pre[1]).astype(bf16))
    expert_y, _ = scatter_halves(
        [
            jnp.einsum("etf,edf->td", h, down_b, preferred_element_type=f32).astype(bf16)
            for h in hidden_h
        ]
    )
    block_out, cot_local, cot_b = row_call(
        gap_kernel, expert_y, (residual, target), None, (bf16, f32, bf16),
        (normed_up[1], normed_down[1], mixed_far),
    )
    cot_h = gather_halves(cot_b)

    d_pre_h = []
    d_mixed_parts = []
    router_parts = []
    for cot, pre, gate_w, prob, ch, mixed in zip(
        cot_h, pre_h, gate_w_h, prob_h, choose_h, mixed_h
    ):
        d_hid = (
            jnp.einsum("td,edf->etf", cot, down_b, preferred_element_type=f32)
            .astype(bf16)
            .astype(f32)
        )
        gate_in, up_in = pre[0], pre[1]
        gate_sig = jax.nn.sigmoid(gate_in)
        gate_act = gate_in * gate_sig
        d_gate_w = jnp.sum(d_hid * gate_act * up_in, axis=-1).T
        scaled = d_hid * gate_w.T[:, :, None]
        d_gate_in = scaled * up_in * gate_sig * (1.0 + gate_in * (1.0 - gate_sig))
        d_up_in = scaled * gate_act
        d_pre = jnp.stack([d_gate_in, d_up_in]).astype(bf16)
        d_pre_h.append(d_pre)
        d_prob = d_gate_w * ch
        d_logit = (prob * (d_prob - jnp.sum(prob * d_prob, axis=-1, keepdims=True))).astype(bf16)
        d_mixed_parts.append(
            (
                jnp.einsum("ketf,kedf->td", d_pre, gu_b, preferred_element_type=f32)
                + lax.dot_general(d_logit, router_b, DOT_NT, preferred_element_type=f32)
            ).astype(bf16)
        )
        router_parts.append(
            lax.dot_general(d_logit, mixed, (((0,), (0,)), ((), ())), preferred_element_type=f32)
        )
    router_rows = router_parts[0] + router_parts[1]
    d_mixed, d_mixed_sent = scatter_halves(d_mixed_parts)

    hidden = jnp.concatenate(hidden_h, axis=1)
    d_pre = jnp.concatenate(d_pre_h, axis=2)

    def compact(a):
        taken = route_rows.T[:, None, :, None]
        parts = []
        for slot in range(route_rows.shape[1]):
            part = a[:, 0]
            for e in range(1, experts):
                part = jnp.where(taken[slot] == e, a[:, e], part)
            parts.append(part)
        return jnp.stack(parts, axis=1)

    def plain_part(wide_h, narrow, spec):
        return scatter_x(
            jnp.stack(
                [
                    jnp.einsum(spec, of_parity(wide_h, i), narrow, preferred_element_type=f32)
                    for i in range(x_count)
                ]
            )
        ).astype(bf16)

    d_resid, d_resid_b, gain_second = row_call(
        resid_grad_kernel,
        d_mixed,
        (residual, cot_local),
        norm_gains[1],
        (f32, bf16, None),
    )
    d_resid_h = gather_halves(d_resid_b)
    if pair:
        hidden_far = lax.ppermute(compact(hidden[None]), "x", SWAP)
        cot_far = far_wide(cot_h)
        d_pre_far = lax.ppermute(compact(d_pre), "x", SWAP)
        down_part = weight_grad(
            cot_h,
            cot_far,
            [hidden, hidden_far],
            out_block,
            x_pos,
            routes_far,
            experts,
            (d_resid_b, normed_up[2], normed_down[2]),
        )
    else:
        down_part = plain_part(cot_h, jnp.concatenate(hidden_h, axis=1), "td,etf->edf")
        gate_up_part = plain_part(
            mixed_h, d_pre, "td,ketf->kedf"
        ).reshape(2 * experts, -1, hidden_cols)
    d_attn = attn_out_grad_half(d_resid_h[0], 0, out_b)
    d_attn = attn_out_grad_half(d_resid_h[1], 1, out_b, d_attn, (down_part,))

    d_out = to_heads(d_attn)
    delta = jnp.sum(d_out.astype(f32) * attn_f, axis=-1).reshape(1, line_rows)
    d_query = jnp.zeros((line_rows, HEAD_DIM), f32)
    if pair:
        d_resid_far = far_wide(d_resid_h)
        gate_up_part = weight_grad(
            mixed_h,
            mixed_far,
            [d_pre.reshape(2 * experts, tok_rows, hidden_cols), d_pre_far],
            out_block,
            x_pos,
            routes_far,
            experts,
            (d_attn,),
        )
    d_kv = []
    inner_k = []
    earlier = (gate_up_part,)
    for i, group in enumerate(groups):
        last = i == len(groups) - 1
        d_query, *d_group = attend_grad(
            queries,
            d_out,
            row_lse,
            delta,
            tok_q,
            start_q,
            d_query,
            group,
            f32 if pair and last else bf16,
            earlier,
        )
        if pair and not last:
            out_part = weight_grad(
                d_resid_h,
                d_resid_far,
                [(attn_b, 0), (attn_b, 1), (attn_far, 0), (attn_far, 1)],
                out_block,
                x_pos,
                earlier=(d_group[0],),
            )
            earlier = (out_part,)
        d_kv.append(d_group)
        inner_k.append(jnp.sum(d_group[0].astype(f32) * group[0].astype(f32), axis=-1))
    if pair:
        d_key, d_value = [
            own + lax.ppermute(far, "x", SWAP).astype(f32) for far, own in zip(*d_kv)
        ]
        inner_k = inner_k[1] + lax.ppermute(inner_k[0], "x", SWAP)
    else:
        d_key, d_value = [
            lax.psum_scatter(jnp.stack(parts), "x", scatter_dimension=0).astype(f32)
            for parts in zip(*d_kv)
        ]
        inner_k = lax.psum_scatter(jnp.stack(inner_k), "x", scatter_dimension=0)
    inner = jnp.stack([jnp.sum(d_query * queries.astype(f32), axis=-1), inner_k])
    inner = sum_line(sum_near(inner.reshape(2, z_count, 2, 2, local_rows)), z_count)
    inner = inner.reshape(2, line_rows) / model_width
    inv_line = jnp.moveaxis(inv_line, 0, 1).reshape(2, line_rows)
    coef = jnp.stack([inv_line[0], inner[0], inv_line[1], inner[1]], axis=1)
    head_gain = lax.dynamic_slice_in_dim(gain_qk, z_pos * HEAD_DIM, HEAD_DIM, 1)
    d_raw, gain_sums = raw_grad(
        d_query, d_key, d_value, queries, keys, coef, cos_tab, sin_tab, head_gain
    )
    gain_full = lax.dynamic_update_slice_in_dim(
        jnp.zeros((2, model_width), f32), gain_sums, (wt_pos * z_count + z_pos) * HEAD_DIM, 1
    )

    d_proj = to_tokens(d_raw, 3 * HEAD_DIM)
    far_n, gain_first1 = project_grad_half(d_proj, 1, qkv_b, normed_h[1])
    near_n, gain_first0 = project_grad_half(d_proj, 0, qkv_b, normed_h[0], (far_n,))
    down_part = lax.psum_scatter(down_part, "z", scatter_dimension=1, tiled=True).astype(f32)
    gate_up_part = (
        lax.psum_scatter(gate_up_part, "z", scatter_dimension=1, tiled=True)
        .astype(f32)
        .reshape(2, experts, out_block, hidden_cols)
    )
    d_normed, _ = scatter_halves([near_n, far_n])
    gain_first = (gain_first0 + gain_first1) / norm_gains[:1]
    (input_grad,) = row_call(
        input_grad_kernel,
        d_normed,
        (block_in, d_resid),
        norm_gains[0],
        (bf16,),
    )

    def sum_all(a):
        a = a + lax.ppermute(a, "c", SWAP)
        a = a + lax.ppermute(a, "y", SWAP)
        a = a + lax.ppermute(a, "x", SWAP) if pair else lax.psum(a, "x")
        return sum_line(a, z_count)

    small = sum_all(jnp.concatenate([gain_first, gain_second, gain_full, router_rows]))
    gains_grad = small[:4]
    router_grad = small[4:].T

    if pair:
        out_part = lax.psum_scatter(out_part, "z", scatter_dimension=1, tiled=True)
        out_part = jnp.moveaxis(out_part, 0, 1).reshape(out_block, head_cols).astype(f32)
    else:
        out_part = plain_part(d_resid_h, attn_b, "td,tc->dc")
        out_part = lax.psum_scatter(out_part, "z", scatter_dimension=0, tiled=True).astype(f32)

    normed_other = lax.ppermute(normed_half, "c", SWAP)
    tn = (((0,), (0,)), ((), ()))
    grad_mine = lax.dot_general(normed_half, d_raw, tn, preferred_element_type=f32).astype(bf16)
    d_raw_other = jnp.flip(
        d_raw.reshape(z_count, 2, 2, local_rows, 3 * HEAD_DIM), 2
    ).reshape(line_rows, 3 * HEAD_DIM)
    grad_other = lax.dot_general(
        normed_other, d_raw_other, tn, preferred_element_type=f32
    ).astype(bf16)
    qkv_full = jnp.where(
        c_pos == 0,
        jnp.stack([grad_mine, grad_other]),
        jnp.stack([grad_other, grad_mine]),
    ).reshape(z_count, x_count, out_block, 3 * HEAD_DIM)
    qkv_line = scatter_x(jnp.moveaxis(qkv_full, 1, 0)).astype(bf16)
    qkv_heads = lax.all_to_all(qkv_line, "z", 0, 0, tiled=True)
    qkv_part = (
        qkv_heads.reshape(z_count, out_block, 3, HEAD_DIM)
        .transpose(2, 1, 0, 3)
        .reshape(3, out_block, head_cols)
        .astype(f32)
    )
    return (
        block_out,
        input_grad,
        qkv_part,
        out_part,
        gains_grad,
        router_grad,
        gate_up_part,
        down_part,
    )


def solution(mesh):
    ctx_count = mesh.shape["ctx"]

    def run(*args):
        heads = args[5].shape[2] // HEAD_DIM
        z_count = heads // mesh.shape["wt"]
        x_count = ctx_count // z_count
        grid = Mesh(mesh.devices.reshape(z_count, x_count, 2, 2), ("z", "x", "y", "c"))
        ctx, wt = ("z", "x"), ("y", "c")
        return jax.shard_map(
            functools.partial(local, z_count, x_count),
            mesh=grid,
            in_specs=(
                P(ctx + wt, None),
                P(ctx + wt, None),
                P(),
                P(),
                P(ctx, None),
                P(None, None, wt),
                P(None, wt),
                P(),
                P(),
                P(None, None, None, wt),
                P(None, None, wt),
            ),
            out_specs=(
                P(ctx + wt, None),
                P(ctx + wt, None),
                P(None, ctx, wt),
                P(ctx, wt),
                P(),
                P(),
                P(None, None, ctx, wt),
                P(None, ctx, wt),
            ),
            check_vma=False,
        )(*args)

    return run
```

```python
import functools
import math

import jax
import jax.numpy as jnp
from jax import lax
from jax.experimental import pallas as pl
from jax.experimental.pallas import tpu as pltpu
from jax.sharding import Mesh
from jax.sharding import PartitionSpec as P

HEAD_DIM = 128
LOG2E = math.log2(math.e)

norm_eps = 1e-05
f32 = jnp.float32
bf16 = jnp.bfloat16

SWAP = [(0, 1), (1, 0)]


def cost(us):
    return pl.CostEstimate(flops=int(us * 1e9), bytes_accessed=1 << 20, transcendentals=0)
DOT_NT = (((1,), (1,)), ((), ()))
DOT_NN = (((1,), (0,)), ((), ()))


def attend_kernel(groups, chunk, score_scale, q_ref, tok_q_ref, start_q_ref, *refs):
    key_refs = refs[: 3 * groups]
    o_ref, lse_ref = refs[-groups - 2 : -groups]
    vt_refs = refs[-groups:]
    rows = q_ref.shape[0]

    @pl.when(pl.program_id(0) == 0)
    def _():
        for g in range(groups):
            v_ref, vt_ref = key_refs[3 * g + 1], vt_refs[g]

            def turn(j, carry):
                r = pl.ds(pl.multiple_of(j * chunk, chunk), chunk)
                vt_ref[:, r] = v_ref[r, :].T
                return carry

            lax.fori_loop(0, v_ref.shape[0] // chunk, turn, 0)

    queries = q_ref[...]
    tok_q = tok_q_ref[...]
    start_q = start_q_ref[...]
    state = (
        jnp.full((1, rows), -1e30, f32),
        jnp.zeros((1, rows), f32),
        jnp.zeros((queries.shape[1], rows), f32),
    )
    for g in range(groups):
        k_ref, _, tok_k_ref = key_refs[3 * g : 3 * g + 3]
        vt_ref = vt_refs[g]

        def step(j, carry):
            run_max, run_sum, acc = carry
            r = pl.ds(pl.multiple_of(j * chunk, chunk), chunk)
            s = lax.dot_general(k_ref[r, :], queries, DOT_NT, preferred_element_type=f32)
            tok_k = tok_k_ref[r, :]
            s = jnp.where((tok_k <= tok_q) & (tok_k >= start_q), s * score_scale, -1e30)
            new_max = jnp.maximum(run_max, jnp.max(s, axis=0, keepdims=True))
            p = jnp.exp2(s - new_max)
            shrink = jnp.exp2(run_max - new_max)
            run_sum = run_sum * shrink + jnp.sum(p, axis=0, keepdims=True)
            acc = acc * shrink + lax.dot_general(
                vt_ref[:, r], p.astype(bf16), DOT_NN, preferred_element_type=f32
            )
            return new_max, run_sum, acc

        steps = k_ref.shape[0] // chunk
        state = lax.fori_loop(0, steps, step, state, unroll=steps <= 4)
    run_max, run_sum, acc = state
    o_ref[...] = (acc / run_sum).T
    lse_ref[...] = run_max + jnp.log2(run_sum)


def attend(queries, tok_q, start_q, key_groups, earlier=()):
    rows = queries.shape[0]
    block = min(1024, rows)
    chunk = 1024
    row = pl.BlockSpec((1, block), lambda i: (0, i))
    in_specs = [pl.BlockSpec((block, HEAD_DIM), lambda i: (i, 0)), row, row]
    operands = [queries, tok_q, start_q]
    scratch = []
    keys = 0
    for group in key_groups:
        count = group[0].shape[0]
        keys += count
        in_specs += [pl.BlockSpec(a.shape, lambda i: (0, 0)) for a in group]
        operands += group
        scratch.append(pltpu.VMEM((HEAD_DIM, count), bf16))
    in_specs += [pl.BlockSpec(memory_space=pl.ANY)] * len(earlier)
    operands += earlier
    return pl.pallas_call(
        functools.partial(
            attend_kernel, len(key_groups), chunk, LOG2E / math.sqrt(HEAD_DIM)
        ),
        grid=(rows // block,),
        in_specs=in_specs,
        out_specs=[pl.BlockSpec((block, HEAD_DIM), lambda i: (i, 0)), row],
        out_shape=[
            jax.ShapeDtypeStruct((rows, HEAD_DIM), f32),
            jax.ShapeDtypeStruct((1, rows), f32),
        ],
        scratch_shapes=scratch,
        compiler_params=params(48),
        cost_estimate=cost(19),
        name="attend",
    )(*operands)


def attend_grad_kernel(
    chunk,
    score_scale,
    grad_scale,
    q_ref,
    do_ref,
    lse_ref,
    delta_ref,
    tok_q_ref,
    start_q_ref,
    dq_in_ref,
    k_ref,
    v_ref,
    tok_k_ref,
    *refs,
):
    dq_ref, dk_ref, dv_ref, kt_ref, dk_acc, dv_acc = refs[-6:]
    steps = k_ref.shape[0] // chunk

    @pl.when(pl.program_id(0) == 0)
    def _():
        dk_acc[...] = jnp.zeros_like(dk_acc)
        dv_acc[...] = jnp.zeros_like(dv_acc)

        def turn(j, carry):
            r = pl.ds(pl.multiple_of(j * chunk, chunk), chunk)
            kt_ref[:, r] = k_ref[r, :].T
            return carry

        lax.fori_loop(0, steps, turn, 0)

    queries = q_ref[...]
    d_out = do_ref[...]
    tok_q = tok_q_ref[...]
    start_q = start_q_ref[...]
    lse = lse_ref[...]
    delta = delta_ref[...]

    def step(j, dq_t):
        r = pl.ds(pl.multiple_of(j * chunk, chunk), chunk)
        s = lax.dot_general(k_ref[r, :], queries, DOT_NT, preferred_element_type=f32)
        tok_k = tok_k_ref[r, :]
        allowed = (tok_k <= tok_q) & (tok_k >= start_q)
        p = jnp.exp2(jnp.where(allowed, s * score_scale - lse, -1e30))
        dp = lax.dot_general(v_ref[r, :], d_out, DOT_NT, preferred_element_type=f32)
        ds = (p * (dp - delta)).astype(bf16)
        dv_acc[r, :] += lax.dot_general(
            p.astype(bf16), d_out, DOT_NN, preferred_element_type=f32
        )
        dk_acc[r, :] += lax.dot_general(ds, queries, DOT_NN, preferred_element_type=f32)
        return dq_t + lax.dot_general(kt_ref[:, r], ds, DOT_NN, preferred_element_type=f32)

    dq_t = lax.fori_loop(
        0,
        steps,
        step,
        jnp.zeros((queries.shape[1], queries.shape[0]), f32),
        unroll=steps <= 4,
    )
    dq_ref[...] = dq_in_ref[...] + (dq_t * grad_scale).T

    @pl.when(pl.program_id(0) == pl.num_programs(0) - 1)
    def _():
        dk_ref[...] = (dk_acc[...] * grad_scale).astype(dk_ref.dtype)
        dv_ref[...] = dv_acc[...].astype(dv_ref.dtype)


def attend_grad(
    queries, d_out, lse, delta, tok_q, start_q, dq_in, key_group, out_type, earlier=()
):
    rows = queries.shape[0]
    keys = key_group[0].shape[0]
    block = min(1024, rows)
    chunk = 1024
    row = pl.BlockSpec((1, block), lambda i: (0, i))
    head = pl.BlockSpec((block, HEAD_DIM), lambda i: (i, 0))
    whole = pl.BlockSpec((keys, HEAD_DIM), lambda i: (0, 0))
    return pl.pallas_call(
        functools.partial(
            attend_grad_kernel,
            chunk,
            LOG2E / math.sqrt(HEAD_DIM),
            1.0 / math.sqrt(HEAD_DIM),
        ),
        grid=(rows // block,),
        in_specs=[
            head,
            head,
            row,
            row,
            row,
            row,
            head,
            whole,
            whole,
            pl.BlockSpec((keys, 1), lambda i: (0, 0)),
        ]
        + [pl.BlockSpec(memory_space=pl.ANY)] * len(earlier),
        out_specs=[head, whole, whole],
        out_shape=[
            jax.ShapeDtypeStruct((rows, HEAD_DIM), f32),
            jax.ShapeDtypeStruct((keys, HEAD_DIM), out_type),
            jax.ShapeDtypeStruct((keys, HEAD_DIM), out_type),
        ],
        scratch_shapes=[
            pltpu.VMEM((HEAD_DIM, keys), bf16),
            pltpu.VMEM((keys, HEAD_DIM), f32),
            pltpu.VMEM((keys, HEAD_DIM), f32),
        ],
        compiler_params=params(48),
        cost_estimate=cost(0.5),
        name="attend_grad",
    )(queries, d_out, lse, delta, tok_q, start_q, dq_in, *key_group, *earlier)


def pack_kernel(raw0_ref, raw1_ref, inv_ref, cos_ref, sin_ref, gain_ref, q_ref, k_ref):
    half = raw0_ref.shape[1]
    for i, raw_ref in enumerate((raw0_ref, raw1_ref)):
        r = slice(i * half, (i + 1) * half)
        for j in range(2):
            u = raw_ref[j] * inv_ref[r, j : j + 1] * gain_ref[j : j + 1, :]
            turned = u * cos_ref[r, :] + pltpu.roll(u, HEAD_DIM // 2, 1) * sin_ref[r, :]
            (q_ref, k_ref)[j][0, r, :] = turned.astype(bf16)


def pack_heads(raw0, raw1, inv, cos_tab, sin_tab, gains):
    half = raw0.shape[1]
    rows = 2 * half
    heads = raw0.shape[2] // HEAD_DIM
    raw = pl.BlockSpec((2, half, HEAD_DIM), lambda h: (0, 0, h))
    head = pl.BlockSpec((1, rows, HEAD_DIM), lambda h: (h, 0, 0))
    table = pl.BlockSpec((rows, HEAD_DIM), lambda h: (0, 0))
    return pl.pallas_call(
        pack_kernel,
        grid=(heads,),
        in_specs=[
            raw,
            raw,
            pl.BlockSpec((rows, 2), lambda h: (0, 0)),
            table,
            table,
            pl.BlockSpec((2, HEAD_DIM), lambda h: (0, h)),
        ],
        out_specs=[head, head],
        out_shape=[jax.ShapeDtypeStruct((heads, rows, HEAD_DIM), bf16)] * 2,
        cost_estimate=cost(4.7),
        name="pack_heads",
    )(raw0, raw1, inv, cos_tab, sin_tab, gains)


def raw_grad_kernel(
    dq_ref, dk_ref, dv_ref, q_ref, k_ref, coef_ref, cos_ref, sin_ref, gain_ref, *refs
):
    out_ref, sum_ref = refs[-2:]

    @pl.when(pl.program_id(0) == 0)
    def _():
        sum_ref[...] = jnp.zeros_like(sum_ref)

    cos_tab = cos_ref[...]
    sin_tab = sin_ref[...]

    def turn_back(u):
        return u * cos_tab - pltpu.roll(u, HEAD_DIM // 2, 1) * sin_tab

    for j, (grad_ref, rows_ref) in enumerate(((dq_ref, q_ref), (dk_ref, k_ref))):
        gain = gain_ref[j : j + 1, :]
        cols = slice(j * HEAD_DIM, (j + 1) * HEAD_DIM)
        d_norm = turn_back(grad_ref[...])
        hat = turn_back(rows_ref[...].astype(f32)) / gain
        sum_ref[j : j + 1, :] += jnp.sum(d_norm * hat, axis=0, keepdims=True)
        inv = coef_ref[:, 2 * j : 2 * j + 1]
        inner = coef_ref[:, 2 * j + 1 : 2 * j + 2]
        out_ref[:, cols] = (inv * (d_norm * gain - hat * inner)).astype(bf16)
    out_ref[:, 2 * HEAD_DIM :] = dv_ref[...].astype(bf16)


def raw_grad(d_query, d_key, d_value, queries, keys, coef, cos_tab, sin_tab, gains, earlier):
    rows = queries.shape[0]
    block = min(512, rows)

    def wide(cols):
        return pl.BlockSpec((block, cols), lambda i: (i, 0))

    whole = pl.BlockSpec((2, HEAD_DIM), lambda i: (0, 0))
    return pl.pallas_call(
        raw_grad_kernel,
        grid=(rows // block,),
        in_specs=[
            *[wide(HEAD_DIM)] * 5,
            wide(4),
            wide(HEAD_DIM),
            wide(HEAD_DIM),
            whole,
            pl.BlockSpec(memory_space=pl.ANY),
        ],
        out_specs=[wide(3 * HEAD_DIM), whole],
        out_shape=[
            jax.ShapeDtypeStruct((rows, 3 * HEAD_DIM), bf16),
            jax.ShapeDtypeStruct((2, HEAD_DIM), f32),
        ],
        cost_estimate=cost(6),
        name="raw_grad",
    )(d_query, d_key, d_value, queries, keys, coef, cos_tab, sin_tab, gains, earlier)


def weight_grad_kernel(experts, out_block, at_ref, *refs):
    wide, far, narrow, compact = refs[:2], refs[2:4], refs[4:6], refs[6:8]
    out_ref, wide_t, tall = refs[-3:]
    half = wide[0].shape[0]
    blocks = far[0].shape[1] // out_block

    @pl.when(pl.program_id(0) == 0)
    def _():
        for z in range(blocks):
            rows = slice(z * out_block, (z + 1) * out_block)
            cols = (2 * z + at_ref[0]) * out_block
            cols = pl.ds(pl.multiple_of(cols, out_block), out_block)
            for i in range(2):
                wide_t[rows, i * half : (i + 1) * half] = wide[i][:, cols].T
                wide_t[rows, (2 + i) * half : (3 + i) * half] = far[i][:, rows].T

    e = lax.rem(pl.program_id(0), experts) if experts else None
    for i in range(2):
        tall[i * half : (i + 1) * half, :] = narrow[i][0]
        there = slice((2 + i) * half, (3 + i) * half)
        if not experts:
            tall[there, :] = compact[i][0]
            continue
        routes = refs[8][i * half : (i + 1) * half, :]
        block = jnp.zeros((half, tall.shape[1]), f32)
        for slot in range(routes.shape[1]):
            block = jnp.where(
                routes[:, slot : slot + 1] == e, compact[i][0, slot].astype(f32), block
            )
        tall[there, :] = block.astype(bf16)
    out_ref[0] = jnp.dot(wide_t[...], tall[...], preferred_element_type=f32).astype(bf16)


def weight_grad(wide_h, far_h, narrow, far_narrow, out_block, at, routes=None, experts=0, earlier=()):
    half, width = wide_h[0].shape
    out_width = far_h[0].shape[1]
    count, _, cols = narrow[0][0].shape

    def part(at):
        return pl.BlockSpec((1, half, cols), lambda j, x: (j, at, 0))

    specs = [part(at) for _, at in narrow]
    if experts:
        slots = routes.shape[1]
        specs += [pl.BlockSpec((1, slots, half, cols), lambda j, x: (j // experts, 0, 0, 0))] * 2
        specs.append(pl.BlockSpec(routes.shape, lambda j, x: (0, 0)))
        earlier = (routes, *earlier)
    else:
        specs += [part(at) for _, at in far_narrow]
    return pl.pallas_call(
        functools.partial(weight_grad_kernel, experts, out_block),
        grid_spec=pltpu.PrefetchScalarGridSpec(
            num_scalar_prefetch=1,
            grid=(count,),
            in_specs=[pl.BlockSpec(w.shape, lambda j, x: (0, 0)) for w in (*wide_h, *far_h)]
            + specs
            + waits(earlier[1:] if experts else earlier),
            out_specs=pl.BlockSpec((1, out_width, cols), lambda j, x: (j, 0, 0)),
            scratch_shapes=[
                pltpu.VMEM((out_width, 4 * half), bf16),
                pltpu.VMEM((4 * half, cols), bf16),
            ],
        ),
        out_shape=jax.ShapeDtypeStruct((count, out_width, cols), bf16),
        compiler_params=params(32),
        cost_estimate=cost(0.1),
        name="weight_grad",
    )(
        at.reshape(1),
        *wide_h,
        *far_h,
        *[a for a, _ in narrow],
        *[a for a, _ in far_narrow],
        *earlier,
    )


def waits(earlier):
    return [pl.BlockSpec(memory_space=pl.ANY)] * len(earlier)


def params(mib=16):
    return pltpu.CompilerParams(vmem_limit_bytes=mib * 1024 * 1024)


def project_kernel(x_ref, w_ref, *refs):
    raw_ref, sq_ref, v_ref = refs[-3:]
    kind, j = pl.program_id(0), pl.program_id(1)
    raw = jnp.dot(x_ref[...], w_ref[0], preferred_element_type=f32)

    @pl.when(kind < 2)
    def _():
        raw_ref[0] = raw
        ones = jnp.ones((8, raw.shape[1]), f32)
        square = lax.dot_general(
            ones, raw * raw, DOT_NT, precision=lax.Precision.HIGHEST, preferred_element_type=f32
        )
        sq_ref[0] = jnp.where(j == 0, square, sq_ref[0] + square)

    @pl.when(kind == 2)
    def _():
        for h in range(v_ref.shape[0]):
            v_ref[h] = raw[:, h * HEAD_DIM : (h + 1) * HEAD_DIM].astype(bf16)


def project(x, weights, earlier=()):
    count, width = x.shape
    cols = weights.shape[2]
    block = cols // 2
    heads = block // HEAD_DIM
    row = pl.BlockSpec((count, width), lambda k, j: (0, 0))

    def held(k, j):
        return jnp.minimum(k, 1), jnp.where(k == 2, 1, j)

    return pl.pallas_call(
        project_kernel,
        grid=(3, 2),
        in_specs=[row, pl.BlockSpec((1, width, block), lambda k, j: (k, 0, j))]
        + waits(earlier),
        out_specs=[
            pl.BlockSpec((1, count, block), lambda k, j: (held(k, j)[0], 0, held(k, j)[1])),
            pl.BlockSpec((1, 8, count), lambda k, j: (jnp.minimum(k, 1), 0, 0)),
            pl.BlockSpec((heads, count, HEAD_DIM), lambda k, j: (jnp.where(k == 2, j, 0), 0, 0)),
        ],
        out_shape=[
            jax.ShapeDtypeStruct((2, count, cols), f32),
            jax.ShapeDtypeStruct((2, 8, count), f32),
            jax.ShapeDtypeStruct((2 * heads, count, HEAD_DIM), bf16),
        ],
        compiler_params=params(32),
        cost_estimate=cost(0.1),
        name="project",
    )(x, weights, *earlier)


def attn_out_kernel(x_ref, w_ref, *refs):
    own_ref, other_ref, rows = refs[-3:]
    count = own_ref.shape[0]

    @pl.when(pl.program_id(0) == 0)
    def _():
        for h in range(x_ref.shape[0]):
            rows[:, h * HEAD_DIM : (h + 1) * HEAD_DIM] = x_ref[h]

    y = lax.dot_general(rows[...], w_ref[...], DOT_NT, preferred_element_type=f32).astype(bf16)
    own_ref[...] = y[:count]
    other_ref[...] = y[count:]


def attn_out_half(parts, half, weights, earlier=()):
    heads, count, _ = parts.shape
    count //= 2
    width, cols = weights.shape
    block = width // 4
    out = pl.BlockSpec((count // 2, block), lambda i: (0, i))
    return pl.pallas_call(
        attn_out_kernel,
        grid=(4,),
        in_specs=[
            pl.BlockSpec((heads, count, HEAD_DIM), lambda i: (0, half, 0)),
            pl.BlockSpec((block, cols), lambda i: (i, 0)),
        ]
        + waits(earlier),
        out_specs=[out, out],
        out_shape=[jax.ShapeDtypeStruct((count // 2, width), bf16)] * 2,
        scratch_shapes=[pltpu.VMEM((count, cols), bf16)],
        compiler_params=params(32),
        cost_estimate=cost(0.1),
        name="attn_out",
    )(parts, weights, *earlier)


def attn_out_grad_kernel(a_ref, w_ref, *refs):
    out_ref = refs[-1]
    y = jnp.dot(a_ref[...], w_ref[...], preferred_element_type=f32).astype(bf16)
    for h in range(out_ref.shape[0]):
        out_ref[h] = y[:, h * HEAD_DIM : (h + 1) * HEAD_DIM]


def attn_out_grad_half(grads, half, weights, into=None, earlier=()):
    count, width = grads.shape
    cols = weights.shape[1]
    heads = cols // HEAD_DIM
    block = cols // 2
    row = pl.BlockSpec((count, width), lambda j: (0, 0))
    into = () if into is None else (into,)
    return pl.pallas_call(
        attn_out_grad_kernel,
        grid=(2,),
        in_specs=[row, pl.BlockSpec((width, block), lambda j: (0, j))]
        + waits(into)
        + waits(earlier),
        out_specs=pl.BlockSpec((heads // 2, count, HEAD_DIM), lambda j: (j, half, 0)),
        out_shape=jax.ShapeDtypeStruct((heads, 2 * count, HEAD_DIM), bf16),
        input_output_aliases={2: 0} if into else {},
        compiler_params=params(16),
        cost_estimate=cost(0.1),
        name="attn_out_grad",
    )(grads, weights, *into, *earlier)


def project_grad_kernel(x_ref, w_ref, n_ref, *refs):
    own_ref, other_ref, sum_ref, rows = refs[-4:]
    count = own_ref.shape[0]
    heads = x_ref.shape[0]
    cols = heads * HEAD_DIM

    @pl.when(pl.program_id(0) == 0)
    def _():
        for k in range(3):
            for h in range(heads):
                at = k * cols + h * HEAD_DIM
                rows[:, at : at + HEAD_DIM] = x_ref[h, :, k * HEAD_DIM : (k + 1) * HEAD_DIM]

    y = None
    for k in range(3):
        term = lax.dot_general(
            rows[:, k * cols : (k + 1) * cols], w_ref[k], DOT_NT, preferred_element_type=f32
        )
        y = term if y is None else y + term
    own_ref[...] = y[:count].astype(bf16)
    other_ref[...] = y[count:].astype(bf16)
    sum_ref[...] = jnp.sum(y * n_ref[...].astype(f32), axis=0, keepdims=True)


def project_grad_half(parts, half, weights, normed, earlier=()):
    heads, count, cols = parts.shape
    count //= 2
    width = weights.shape[1]
    block = width // 4
    out = pl.BlockSpec((count, block), lambda i: (0, i))
    part = pl.BlockSpec((count // 2, block), lambda i: (0, i))
    return pl.pallas_call(
        project_grad_kernel,
        grid=(4,),
        in_specs=[
            pl.BlockSpec((heads, count, cols), lambda i: (0, half, 0)),
            pl.BlockSpec((3, block, weights.shape[2]), lambda i: (0, i, 0)),
            out,
        ]
        + waits(earlier),
        out_specs=[part, part, pl.BlockSpec((1, block), lambda i: (0, i))],
        out_shape=[
            jax.ShapeDtypeStruct((count // 2, width), bf16),
            jax.ShapeDtypeStruct((count // 2, width), bf16),
            jax.ShapeDtypeStruct((1, width), f32),
        ],
        scratch_shapes=[pltpu.VMEM((count, heads * cols), bf16)],
        compiler_params=params(24),
        cost_estimate=cost(6),
        name="project_grad",
    )(parts, weights, normed, *earlier)


def qkv_grad_kernel(wide_ref, grad_ref, grad_other_ref, out_ref, out_other_ref, tall, wide_t):
    rows, cols = grad_ref.shape

    @pl.when(pl.program_id(0) == 0)
    def _():
        tall[:, :cols] = grad_ref[...]
        block = rows // 16
        for i in range(16):
            tall[i * block : (i + 1) * block, cols:] = grad_other_ref[
                (i ^ 1) * block : ((i ^ 1) + 1) * block, :
            ]

    wide_t[...] = wide_ref[...].T
    out = jnp.dot(wide_t[...], tall[...], preferred_element_type=f32).astype(bf16)
    out_ref[...] = out[:, :cols]
    out_other_ref[...] = out[:, cols:]


def qkv_grad(wide, grad, grad_other, z_count):
    assert z_count == 4
    rows, width = wide.shape
    cols = grad.shape[1]
    block = min(256, width)
    whole = pl.BlockSpec(grad.shape, lambda i: (0, 0))
    out = pl.BlockSpec((block, cols), lambda i: (i, 0))
    return pl.pallas_call(
        qkv_grad_kernel,
        grid=(width // block,),
        in_specs=[pl.BlockSpec((rows, block), lambda i: (0, i)), whole, whole],
        out_specs=[out, out],
        scratch_shapes=[pltpu.VMEM((rows, 2 * cols), bf16), pltpu.VMEM((block, rows), bf16)],
        out_shape=[jax.ShapeDtypeStruct((width, cols), bf16)] * 2,
        compiler_params=params(40),
        cost_estimate=cost(10),
        name="qkv_grad",
    )(wide, grad, grad_other)


def arrange(near, z_pos, earlier=()):
    rows, cols = near[0].shape
    z_count = len(near)

    def kernel(z_ref, *refs):
        for i in range(z_count):

            @pl.when(pl.program_id(0) == i)
            def _():
                refs[-1][...] = refs[i][...]

    return pl.pallas_call(
        kernel,
        grid_spec=pltpu.PrefetchScalarGridSpec(
            num_scalar_prefetch=1,
            grid=(z_count,),
            in_specs=[pl.BlockSpec((rows, cols), lambda i, z: (0, 0))] * z_count + waits(earlier),
            out_specs=pl.BlockSpec(
                (rows, cols), lambda i, z: (lax.rem(z[0] - i + z_count, z_count), 0)
            ),
        ),
        out_shape=jax.ShapeDtypeStruct((z_count * rows, cols), near[0].dtype),
        compiler_params=params(),
        cost_estimate=cost(0.1),
        name="arrange",
    )(z_pos.reshape(1), *near, *earlier)


def own_grad_kernel(w0_ref, w1_ref, n0_ref, n1_ref, *refs):
    out_ref, wide_t = refs[-2:]
    half = w0_ref.shape[0]

    @pl.when(pl.program_id(0) == 0)
    def _():
        wide_t[:, :half] = w0_ref[...].T
        wide_t[:, half:] = w1_ref[...].T

    tall = jnp.concatenate(
        [n0_ref[...].reshape(n0_ref.shape[-2:]), n1_ref[...].reshape(n1_ref.shape[-2:])]
    )
    out_ref[0] = jnp.dot(wide_t[...], tall, preferred_element_type=f32).astype(bf16)


def own_grad(wide_h, narrow_h, earlier=()):
    half, width = wide_h[0].shape
    count, rows, cols = narrow_h[0].shape
    narrow = [
        pl.BlockSpec((1, half, cols), lambda j, at=i * (rows // half - 1): (j, at, 0))
        for i in range(2)
    ]
    return pl.pallas_call(
        own_grad_kernel,
        grid=(count,),
        in_specs=[pl.BlockSpec((half, width), lambda j: (0, 0))] * 2 + narrow + waits(earlier),
        out_specs=pl.BlockSpec((1, width, cols), lambda j: (j, 0, 0)),
        out_shape=jax.ShapeDtypeStruct((count, width, cols), bf16),
        scratch_shapes=[pltpu.VMEM((width, 2 * half), bf16)],
        compiler_params=params(24),
        cost_estimate=cost(0.1),
        name="own_grad",
    )(*wide_h, *narrow_h, *earlier)


def join_kernel(a_ref, b_ref, *refs):
    n = a_ref.shape[0]
    refs[-1][:n] = a_ref[...]
    refs[-1][n:] = b_ref[...]


def join_rows(a, b, earlier=()):
    rows, width = a.shape
    block = width // 2
    part = pl.BlockSpec((rows, block), lambda j: (0, j))
    return pl.pallas_call(
        join_kernel,
        grid=(2,),
        in_specs=[part, part] + waits(earlier),
        out_specs=pl.BlockSpec((2 * rows, block), lambda j: (0, j)),
        out_shape=jax.ShapeDtypeStruct((2 * rows, width), a.dtype),
        compiler_params=params(),
        cost_estimate=cost(0.1),
        name="join_rows",
    )(a, b, *earlier)


def pass_kernel(in_ref, *refs):
    refs[-1][...] = in_ref[...]


def pass_rows(a, earlier):
    rows, width = a.shape
    spec = pl.BlockSpec((rows, width // 2), lambda j: (0, j))
    return pl.pallas_call(
        pass_kernel,
        grid=(2,),
        in_specs=[spec] + waits(earlier),
        out_specs=spec,
        out_shape=jax.ShapeDtypeStruct(a.shape, a.dtype),
        compiler_params=params(),
        cost_estimate=cost(0.1),
        name="pass_rows",
    )(a, *earlier)


def round_kernel(in_ref, *refs):
    refs[-1][...] = in_ref[...].astype(bf16)


def round_weights(a, earlier=()):
    flat = a.reshape(-1, a.shape[-1])
    rows, cols = flat.shape
    block = min(rows, 1 << 20 >> (cols.bit_length() - 1))
    spec = pl.BlockSpec((block, cols), lambda i: (i, 0))
    out = pl.pallas_call(
        round_kernel,
        grid=(rows // block,),
        in_specs=[spec] + waits(earlier),
        out_specs=spec,
        out_shape=jax.ShapeDtypeStruct(flat.shape, bf16),
        compiler_params=params(),
        cost_estimate=cost(9),
        name="round_weights",
    )(flat, *earlier)
    return out.reshape(a.shape)


def add_kernel(a_ref, b_ref, *refs):
    refs[-1][...] = (a_ref[...].astype(f32) + b_ref[...].astype(f32)).astype(bf16)


def add_rows(a, b, earlier=()):
    spec = pl.BlockSpec((1, *a.shape[1:]), lambda i: (i, 0, 0))
    return pl.pallas_call(
        add_kernel,
        grid=(a.shape[0],),
        in_specs=[spec, spec] + waits(earlier),
        out_specs=spec,
        out_shape=jax.ShapeDtypeStruct(a.shape, bf16),
        compiler_params=params(),
        cost_estimate=cost(1),
        name="add_rows",
    )(a, b, *earlier)


def stack_kernel(a_ref, b_ref, gain_ref, second_ref, qk_ref, router_ref, out_ref):
    out_ref[0:1, :] = (a_ref[...] + b_ref[...]) / gain_ref[0:1, :]
    out_ref[1:2, :] = second_ref[...]
    out_ref[2:4, :] = qk_ref[...]
    out_ref[4:8, :] = router_ref[...]


def stack_rows(*rows):
    return pl.pallas_call(
        stack_kernel,
        out_shape=jax.ShapeDtypeStruct((8, rows[0].shape[1]), f32),
        compiler_params=params(),
        cost_estimate=cost(0.1),
        name="stack_rows",
    )(*rows)


def row_sum(refs):
    return refs[0][...].astype(f32) + refs[1][...].astype(f32) + refs[2][...].astype(f32)


def inv_rms(rows):
    return lax.rsqrt(jnp.mean(rows * rows, axis=-1, keepdims=True) + norm_eps)


def mix_kernel(near, near_got, far_got, in_ref, gain_ref, *refs):
    residual_ref, mixed_ref = refs[-2:]
    residual = in_ref[...].astype(f32) + row_sum((near, near_got, far_got))
    residual_ref[...] = residual
    mixed_ref[...] = (residual * inv_rms(residual) * gain_ref[...]).astype(bf16)


def gap_kernel(near, near_got, far_got, residual_ref, target_ref, *refs):
    out_ref, gap_ref, gap_b_ref = refs[-3:]
    out = residual_ref[...] + row_sum((near, near_got, far_got))
    out_ref[...] = out.astype(bf16)
    gap = out - target_ref[...].astype(f32)
    gap_ref[...] = gap
    gap_b_ref[...] = gap.astype(bf16)


def resid_grad_kernel(near, near_got, far_got, residual_ref, gap_ref, gain_ref, *refs):
    grad_ref, grad_b_ref, sum_ref = refs[-3:]
    d_mixed = row_sum((near, near_got, far_got))
    residual = residual_ref[...]
    inv = inv_rms(residual)
    hat = residual * inv
    grad = gap_ref[...] + norm_back(d_mixed, hat, inv, gain_ref[...])
    grad_ref[...] = grad
    grad_b_ref[...] = grad.astype(bf16)

    @pl.when(pl.program_id(0) == 0)
    def _():
        sum_ref[...] = jnp.zeros_like(sum_ref)

    sum_ref[...] += jnp.sum(d_mixed * hat, axis=0, keepdims=True)


def input_grad_kernel(near, near_got, far_got, in_ref, grad_ref, gain_ref, *refs):
    rows = in_ref[...].astype(f32)
    inv = inv_rms(rows)
    d_normed = row_sum((near, near_got, far_got))
    grad = grad_ref[...] + norm_back(d_normed, rows * inv, inv, gain_ref[...])
    refs[-1][...] = grad.astype(bf16)


def row_call(kernel, terms, rows, gain, outs, earlier=()):
    count, width = rows[0].shape
    block = min(32, count)
    spec = pl.BlockSpec((block, width), lambda i: (i, 0))
    line = pl.BlockSpec((1, width), lambda i: (0, 0))
    gains = [] if gain is None else [gain.reshape(1, width)]
    return pl.pallas_call(
        kernel,
        grid=(count // block,),
        in_specs=[spec] * (len(terms) + len(rows))
        + [line] * len(gains)
        + [pl.BlockSpec(memory_space=pl.ANY)] * len(earlier),
        out_specs=[line if o is None else spec for o in outs],
        out_shape=[
            jax.ShapeDtypeStruct((1, width) if o is None else (count, width), f32 if o is None else o)
            for o in outs
        ],
        compiler_params=params(16),
        cost_estimate=cost(0.1),
        name=kernel.__name__,
    )(*terms, *rows, *gains, *earlier)


def pick_kernel(cols, z_count, c_ref, r0_ref, r1_ref, *refs):
    out_ref = refs[-1]
    half = r0_ref.shape[0]
    out_ref[:half] = r0_ref[...]
    out_ref[half:] = r1_ref[...]


def pick_half(rows_h, at, earlier=()):
    half, width = rows_h[0].shape
    cols = width // 2
    block = cols // 2
    return pl.pallas_call(
        functools.partial(pick_kernel, cols, 2),
        grid_spec=pltpu.PrefetchScalarGridSpec(
            num_scalar_prefetch=1,
            grid=(2,),
            in_specs=[pl.BlockSpec((half, block), lambda j, c: (0, 2 * c[0] + j))] * 2
            + [pl.BlockSpec(memory_space=pl.ANY)] * len(earlier),
            out_specs=pl.BlockSpec((2 * half, block), lambda j, c: (0, j)),
        ),
        out_shape=jax.ShapeDtypeStruct((2 * half, cols), rows_h[0].dtype),
        cost_estimate=cost(0.1),
        name="pick_half",
    )(at.reshape(1), *rows_h, *earlier)


def token_places(seq_lengths, permutation):
    seq_ends = jnp.cumsum(seq_lengths)
    seq_starts = seq_ends - seq_lengths
    seq_id = jnp.sum((permutation[:, None] >= seq_ends[None, :]).astype(jnp.int32), axis=1)
    member = seq_id[:, None] == jnp.arange(seq_lengths.shape[0], dtype=jnp.int32)[None, :]
    return jnp.sum(jnp.where(member, seq_starts[None, :], 0), axis=1)


def near_first(a, axis, y_pos, c_pos):
    a = jnp.where(y_pos == 0, a, jnp.flip(a, axis))
    return jnp.where(c_pos == 0, a, jnp.flip(a, axis + 1))


def norm_back(grad_out, hat_rows, inv_rows, gain_row):
    grad_hat = grad_out * gain_row
    return inv_rows * (grad_hat - hat_rows * jnp.mean(grad_hat * hat_rows, axis=-1, keepdims=True))


def gather_halves(rows, beside=(), earlier=()):
    far = lax.ppermute(rows, "y", SWAP)
    core = lax.ppermute(rows, "c", SWAP)
    if beside:
        far = pass_rows(far, beside)
    far_core = lax.ppermute(far, "c", SWAP)
    return [jnp.concatenate([rows, core]), join_rows(far, far_core, earlier)]


def scatter_halves(near, far):
    sent = far[0].astype(f32) + lax.ppermute(far[1], "c", SWAP).astype(f32)
    sent = sent.astype(bf16)
    far_got = lax.ppermute(sent, "y", SWAP)
    near_got = lax.ppermute(near[1], "c", SWAP)
    return (near[0], near_got, far_got), sent


def sum_near(a):
    a = a + jnp.flip(lax.ppermute(a, "c", SWAP), -2)
    return a + jnp.flip(lax.ppermute(a, "y", SWAP), -3)


def sum_line(a, z_count):
    step = 1
    while step < z_count:
        a = a + lax.ppermute(a, "z", [(i, i ^ step) for i in range(z_count)])
        step *= 2
    return a


def local(
    z_count,
    x_count,
    block_in,
    target,
    seq_lengths,
    permutation,
    routes,
    attn_qkv,
    attn_out,
    norm_gains,
    router,
    gate_up,
    down,
):
    z_pos = lax.axis_index("z")
    x_pos = lax.axis_index("x")
    y_pos = lax.axis_index("y")
    c_pos = lax.axis_index("c")
    pair = x_count == 2
    local_rows, model_width = block_in.shape
    tok_rows = 4 * local_rows
    line_rows = z_count * tok_rows
    head_cols = attn_qkv.shape[2]
    hidden_cols = gate_up.shape[3]
    experts = gate_up.shape[1]
    wide_block = model_width // z_count
    out_block = wide_block // x_count
    wt_pos = y_pos * 2 + c_pos

    qkv_b = attn_qkv.astype(bf16)
    router_b = router.astype(bf16)

    def scatter_x(a):
        if pair:
            mine = lax.dynamic_index_in_dim(a, x_pos, 0, False)
            other = lax.dynamic_index_in_dim(a, 1 - x_pos, 0, False)
            return mine.astype(f32) + lax.ppermute(other.astype(bf16), "x", SWAP).astype(f32)
        return lax.psum_scatter(a.astype(bf16), "x", scatter_dimension=0).astype(f32)

    def of_parity(rows_h, at):
        return jnp.concatenate(
            [
                jnp.concatenate(
                    [
                        lax.dynamic_slice_in_dim(
                            r, z * wide_block + at * out_block, out_block, 1
                        )
                        for z in range(z_count)
                    ],
                    axis=1,
                )
                for r in rows_h
            ]
        )

    def far_wide(rows_h):
        return lax.ppermute(of_parity(rows_h, 1 - x_pos), "x", SWAP)

    def swap_x(parts):
        return [lax.ppermute(p, "x", SWAP) for p in parts]

    resid_in = block_in.astype(f32)
    inv_first = lax.rsqrt(jnp.mean(resid_in * resid_in, axis=-1, keepdims=True) + norm_eps)
    hat_first = resid_in * inv_first
    normed = (hat_first * norm_gains[0]).astype(bf16)
    normed_h = gather_halves(normed)

    start_all = token_places(seq_lengths, permutation)
    shape = (z_count, x_count, 2, 2, local_rows)
    tok_all = near_first(permutation.reshape(shape), 2, y_pos, c_pos)
    start_all = near_first(start_all.reshape(shape), 2, y_pos, c_pos)

    def of_x(a, at):
        return lax.dynamic_index_in_dim(a, at, 1, False).reshape(line_rows)

    tok_own = of_x(tok_all, x_pos)
    start_own = of_x(start_all, x_pos)
    tok_q = tok_own.reshape(1, line_rows)
    start_q = start_own.reshape(1, line_rows)
    half_dim = HEAD_DIM // 2
    frequency = jnp.exp(
        jnp.arange(half_dim, dtype=f32) * (-2.0 * math.log(10000.0) / HEAD_DIM)
    )
    angles = (tok_own - start_own).astype(f32)[:, None] * frequency[None, :]
    cosine, sine = jnp.cos(angles), jnp.sin(angles)
    cos_tab = jnp.concatenate([cosine, cosine], axis=1)
    sin_tab = jnp.concatenate([-sine, sine], axis=1)

    raw0, square0, v0 = project(normed_h[0], qkv_b)
    raw1, square1, v1 = project(normed_h[1], qkv_b, (v0,))
    squares = jnp.concatenate([square0[:, 0], square1[:, 0]], axis=1)
    squares = sum_near(squares.reshape(2, 2, 2, local_rows)).reshape(2, tok_rows)
    inv_qk = lax.rsqrt(squares / model_width + norm_eps)
    inv_slots = jnp.where(
        (jnp.arange(z_count, dtype=jnp.int32) == z_pos)[:, None, None], inv_qk[None], 0.0
    )
    inv_line = sum_line(inv_slots, z_count)
    gain_qk = lax.dynamic_slice_in_dim(norm_gains[2:], wt_pos * head_cols, head_cols, 1)

    def to_heads_apart(parts, earlier=()):
        near = [lax.dynamic_index_in_dim(parts, z_pos, 0, False)]
        for d in range(1, z_count):
            there = lax.dynamic_index_in_dim(parts, (z_pos + d) % z_count, 0, False)
            near.append(
                lax.ppermute(there, "z", [(i, (i + d) % z_count) for i in range(z_count)])
            )
        return arrange(near, z_pos, earlier)

    def to_heads(parts):
        return lax.all_to_all(parts, "z", 0, 0, tiled=True).reshape(line_rows, HEAD_DIM)

    def from_x(a):
        if pair:
            return lax.ppermute(a, "x", SWAP)
        return lax.all_gather(a, "x", axis=0)

    v_heads = jnp.concatenate([v0, v1], axis=1)
    values = to_heads(v_heads)
    values_far = from_x(values)
    q_heads, k_heads = pack_heads(
        raw0,
        raw1,
        inv_qk.T,
        lax.dynamic_slice_in_dim(cos_tab, z_pos * tok_rows, tok_rows),
        lax.dynamic_slice_in_dim(sin_tab, z_pos * tok_rows, tok_rows),
        gain_qk,
    )
    keys = to_heads_apart(k_heads, (values_far,))
    out_b = attn_out.astype(bf16)
    keys_far = from_x(keys)
    queries = to_heads_apart(q_heads)
    tok_col = tok_own.reshape(line_rows, 1)
    if pair:
        tok_far = of_x(tok_all, 1 - x_pos).reshape(line_rows, 1)
        groups = [(keys_far, values_far, tok_far), (keys, values, tok_col)]
        key_groups = groups[::-1]
    else:
        tok_x = jnp.moveaxis(tok_all, 1, 0).reshape(x_count, line_rows, 1)
        groups = [(keys_far[i], values_far[i], tok_x[i]) for i in range(x_count)]
        key_groups = [
            (
                keys_far.reshape(-1, HEAD_DIM),
                values_far.reshape(-1, HEAD_DIM),
                tok_x.reshape(-1, 1),
            )
        ]
    attn_f, row_lse = attend(
        queries, tok_q, start_q, key_groups
    )

    def to_tokens(rows, cols):
        parts = lax.all_to_all(
            rows.reshape(z_count, tok_rows, cols), "z", 0, 0, tiled=True
        )
        return parts

    attn_parts = to_tokens(attn_f.astype(bf16), HEAD_DIM)
    attn_far = attn_out_half(attn_parts, 1, out_b)
    attn_near = attn_out_half(attn_parts, 0, out_b)
    attn_y, attn_sent = scatter_halves(attn_near, attn_far)
    normed_pick = pick_half(normed_h, c_pos, (attn_sent,))
    normed_line = lax.all_gather(normed_pick, "z", axis=0, tiled=True)
    attn_there = lax.ppermute(attn_parts, "x", SWAP) if pair else attn_sent
    gu_b = round_weights(gate_up, (attn_sent,))
    residual, mixed_rows = row_call(
        mix_kernel,
        attn_y,
        (block_in,),
        norm_gains[1],
        (f32, bf16),
        (gu_b, normed_pick, attn_there),
    )
    down_b = round_weights(down, (mixed_rows,))
    mixed_h = gather_halves(mixed_rows, (down_b,))
    mixed_far = [far_wide([m]) for m in mixed_h] if pair else [mixed_rows, mixed_rows]

    def halves(a):
        return a[: a.shape[0] // 2], a[a.shape[0] // 2 :]

    route_rows = near_first(routes.reshape(2, 2, local_rows, -1), 0, y_pos, c_pos)
    route_rows = route_rows.reshape(tok_rows, -1)
    if pair:
        routes_far = lax.ppermute(route_rows.T.astype(f32), "x", SWAP).T.astype(jnp.int32)
    choose = jnp.sum(
        (route_rows[:, :, None] == jnp.arange(experts, dtype=jnp.int32)[None, None, :]).astype(f32),
        axis=1,
    )
    choose_h = halves(choose)
    prob_h = [
        jax.nn.softmax(jnp.dot(m, router_b, preferred_element_type=f32), axis=-1)
        for m in mixed_h
    ]
    gate_w_h = [p * ch for p, ch in zip(prob_h, choose_h)]
    pre_h = [
        jnp.einsum("td,kedf->ketf", m, gu_b, preferred_element_type=f32) for m in mixed_h
    ]
    hidden_h = []
    for pre, gate_w in zip(pre_h, gate_w_h):
        gate_act = pre[0] * jax.nn.sigmoid(pre[0])
        hidden_h.append((gate_w.T[:, :, None] * gate_act * pre[1]).astype(bf16))
    expert_y, _ = scatter_halves(
        *[
            halves(
                jnp.einsum("etf,edf->td", h, down_b, preferred_element_type=f32).astype(bf16)
            )
            for h in hidden_h
        ]
    )
    block_out, cot_local, cot_b = row_call(
        gap_kernel, expert_y, (residual, target), None, (bf16, f32, bf16),
        (mixed_far[0],),
    )
    cot_h = gather_halves(cot_b, earlier=(mixed_far[1], normed_line))

    d_pre_h = []
    d_mixed_parts = []
    router_parts = []
    for cot, pre, gate_w, prob, ch, mixed in zip(
        cot_h, pre_h, gate_w_h, prob_h, choose_h, mixed_h
    ):
        d_hid = (
            jnp.einsum("td,edf->etf", cot, down_b, preferred_element_type=f32)
            .astype(bf16)
            .astype(f32)
        )
        gate_in, up_in = pre[0], pre[1]
        gate_sig = jax.nn.sigmoid(gate_in)
        gate_act = gate_in * gate_sig
        d_gate_w = jnp.sum(d_hid * gate_act * up_in, axis=-1).T
        scaled = d_hid * gate_w.T[:, :, None]
        d_gate_in = scaled * up_in * gate_sig * (1.0 + gate_in * (1.0 - gate_sig))
        d_up_in = scaled * gate_act
        d_pre = jnp.stack([d_gate_in, d_up_in]).astype(bf16)
        d_pre_h.append(d_pre)
        d_prob = d_gate_w * ch
        d_logit = (prob * (d_prob - jnp.sum(prob * d_prob, axis=-1, keepdims=True))).astype(bf16)
        d_mixed_parts.append(
            (
                jnp.einsum("ketf,kedf->td", d_pre, gu_b, preferred_element_type=f32)
                + lax.dot_general(d_logit, router_b, DOT_NT, preferred_element_type=f32)
            ).astype(bf16)
        )
        router_parts.append(
            lax.dot_general(d_logit, mixed, (((0,), (0,)), ((), ())), preferred_element_type=f32)
        )
    router_rows = router_parts[0] + router_parts[1]
    d_mixed, d_mixed_sent = scatter_halves(*[halves(d) for d in d_mixed_parts])
    down_part = own_grad(cot_h, hidden_h, (d_mixed_sent,))

    def compact(a, taken):
        a = a.reshape(-1, experts, *a.shape[1:])
        taken = taken.T[:, None, :, None]
        parts = []
        for slot in range(taken.shape[0]):
            part = a[:, 0]
            for e in range(1, experts):
                part = jnp.where(taken[slot] == e, a[:, e], part)
            parts.append(part)
        return jnp.stack(parts, axis=1)

    def plain_part(wide_h, narrow, spec):
        return scatter_x(
            jnp.stack(
                [
                    jnp.einsum(spec, of_parity(wide_h, i), narrow, preferred_element_type=f32)
                    for i in range(x_count)
                ]
            )
        ).astype(bf16)

    d_resid, d_resid_b, gain_second = row_call(
        resid_grad_kernel,
        d_mixed,
        (residual, cot_local),
        norm_gains[1],
        (f32, bf16, None),
        (down_part,),
    )
    d_pre_h = [d.reshape(2 * experts, -1, hidden_cols) for d in d_pre_h]
    if pair:
        d_pre_far = [
            lax.ppermute(compact(d, r), "x", SWAP) for d, r in zip(d_pre_h, (route_rows[: tok_rows // 2], route_rows[tok_rows // 2 :]))
        ]
    d_resid_h = gather_halves(d_resid_b, earlier=(d_pre_far[0],) if pair else ())
    d_resid_far = [far_wide([d]) for d in d_resid_h] if pair else None
    d_attn = attn_out_grad_half(d_resid_h[0], 0, out_b)
    d_attn = attn_out_grad_half(d_resid_h[1], 1, out_b, d_attn)

    d_out = to_heads(d_attn)
    delta = jnp.sum(d_out.astype(f32) * attn_f, axis=-1).reshape(1, line_rows)
    d_query = jnp.zeros((line_rows, HEAD_DIM), f32)
    if pair:
        gate_up_part = weight_grad(
            mixed_h,
            mixed_far,
            [(d, 0) for d in d_pre_h],
            [(d, 0) for d in d_pre_far],
            out_block,
            x_pos,
            routes_far,
            experts,
            (d_attn,),
        )
    else:
        gate_up_part = plain_part(mixed_h, jnp.concatenate(d_pre_h, axis=1), "td,ntf->ndf")
    down_part = lax.psum_scatter(down_part, ("z", "x"), scatter_dimension=1, tiled=True)
    gate_up_sum = lax.psum_scatter(gate_up_part, "z", scatter_dimension=1, tiled=True)
    d_kv = []
    inner_k = []
    earlier = (gate_up_part, d_resid_far[0]) if pair else (gate_up_part,)
    for i, group in enumerate(groups):
        last = i == len(groups) - 1
        d_query, *d_group = attend_grad(
            queries,
            d_out,
            row_lse,
            delta,
            tok_q,
            start_q,
            d_query,
            group,
            f32 if pair and last else bf16,
            earlier,
        )
        d_kv.append(d_group)
        if pair and not last:
            out_part = weight_grad(
                d_resid_h,
                d_resid_far,
                [(attn_parts, 0), (attn_parts, 1)],
                [(attn_there, 0), (attn_there, 1)],
                out_block,
                x_pos,
                earlier=(d_group[0],),
            )
            earlier = (down_part, out_part)
        inner_k.append(jnp.sum(d_group[0].astype(f32) * group[0].astype(f32), axis=-1))
    if pair:
        d_key, d_value = [
            own + lax.ppermute(far, "x", SWAP).astype(f32) for far, own in zip(*d_kv)
        ]
        inner_k = inner_k[1] + lax.ppermute(inner_k[0], "x", SWAP)
    else:
        d_key, d_value = [
            lax.psum_scatter(jnp.stack(parts), "x", scatter_dimension=0).astype(f32)
            for parts in zip(*d_kv)
        ]
        inner_k = lax.psum_scatter(jnp.stack(inner_k), "x", scatter_dimension=0)
    inner = jnp.stack([jnp.sum(d_query * queries.astype(f32), axis=-1), inner_k])
    inner = sum_line(sum_near(inner.reshape(2, z_count, 2, 2, local_rows)), z_count)
    inner = inner.reshape(2, line_rows) / model_width
    inv_line = jnp.moveaxis(inv_line, 0, 1).reshape(2, line_rows)
    coef = jnp.stack([inv_line[0], inner[0], inv_line[1], inner[1]], axis=1)
    head_gain = lax.dynamic_slice_in_dim(gain_qk, z_pos * HEAD_DIM, HEAD_DIM, 1)
    d_raw, gain_sums = raw_grad(
        d_query, d_key, d_value, queries, keys, coef, cos_tab, sin_tab, head_gain, out_part if pair else d_query
    )
    gain_full = lax.dynamic_update_slice_in_dim(
        jnp.zeros((2, model_width), f32), gain_sums, (wt_pos * z_count + z_pos) * HEAD_DIM, 1
    )

    def sum_all(a):
        a = a + lax.ppermute(a, "c", SWAP)
        a = a + lax.ppermute(a, "y", SWAP)
        a = pass_rows(a, (input_grad,))
        a = a + lax.ppermute(a, "x", SWAP) if pair else lax.psum(a, "x")
        return sum_line(a, z_count)

    if pair:
        out_sum = lax.psum_scatter(out_part, "z", scatter_dimension=1, tiled=True)
    else:
        out_part = own_grad(d_resid_h, (attn_parts, attn_parts), (d_raw,))
        out_sum = lax.psum_scatter(out_part, ("z", "x"), scatter_dimension=1, tiled=True)
    out_sum = jnp.moveaxis(out_sum, 0, 1).reshape(out_block, head_cols).astype(f32)
    grad_mine, grad_other = qkv_grad(
        normed_line, d_raw, lax.ppermute(d_raw, "c", SWAP), z_count
    )
    grad_other = lax.ppermute(grad_other, "c", SWAP)
    qkv_full = jnp.where(
        c_pos == 0,
        jnp.stack([grad_mine, grad_other]),
        jnp.stack([grad_other, grad_mine]),
    ).reshape(z_count, x_count, out_block, 3 * HEAD_DIM)
    qkv_line = jnp.moveaxis(qkv_full, 1, 0)
    if pair:
        qkv_line = (
            lax.dynamic_index_in_dim(qkv_line, x_pos, 0, False),
            lax.ppermute(lax.dynamic_index_in_dim(qkv_line, 1 - x_pos, 0, False), "x", SWAP),
        )
    else:
        qkv_line = scatter_x(qkv_line).astype(bf16)
        qkv_line = (qkv_line, jnp.zeros_like(qkv_line))
    d_proj = to_tokens(d_raw, 3 * HEAD_DIM)
    *far_n, gain_first1 = project_grad_half(
        d_proj, 1, qkv_b, normed_h[1], (qkv_line[1], gate_up_sum)
    )
    *near_n, gain_first0 = project_grad_half(d_proj, 0, qkv_b, normed_h[0], (far_n[0],))
    d_normed, _ = scatter_halves(near_n, far_n)
    (input_grad,) = row_call(
        input_grad_kernel,
        d_normed,
        (block_in, d_resid),
        norm_gains[0],
        (bf16,),
    )

    small = sum_all(stack_rows(gain_first0, gain_first1, norm_gains, gain_second, gain_full, router_rows))
    gains_grad = small[:4]
    router_grad = small[4:].T

    qkv_heads = lax.all_to_all(
        add_rows(*qkv_line, (near_n[0],)), "z", 0, 0, tiled=True
    )
    qkv_part = (
        qkv_heads.reshape(z_count, out_block, 3, HEAD_DIM)
        .transpose(2, 1, 0, 3)
        .reshape(3, out_block, head_cols)
        .astype(f32)
    )
    return (
        block_out,
        input_grad,
        qkv_part,
        out_sum,
        gains_grad,
        router_grad,
        gate_up_sum.astype(f32).reshape(2, experts, out_block, hidden_cols),
        down_part.astype(f32),
    )


def solution(mesh):
    ctx_count = mesh.shape["ctx"]

    def run(*args):
        heads = args[5].shape[2] // HEAD_DIM
        z_count = heads // mesh.shape["wt"]
        x_count = ctx_count // z_count
        grid = Mesh(mesh.devices.reshape(z_count, x_count, 2, 2), ("z", "x", "y", "c"))
        ctx, wt = ("z", "x"), ("y", "c")
        return jax.shard_map(
            functools.partial(local, z_count, x_count),
            mesh=grid,
            in_specs=(
                P(ctx + wt, None),
                P(ctx + wt, None),
                P(),
                P(),
                P(ctx, None),
                P(None, None, wt),
                P(None, wt),
                P(),
                P(),
                P(None, None, None, wt),
                P(None, None, wt),
            ),
            out_specs=(
                P(ctx + wt, None),
                P(ctx + wt, None),
                P(None, ctx, wt),
                P(ctx, wt),
                P(),
                P(),
                P(None, None, ctx, wt),
                P(None, ctx, wt),
            ),
            check_vma=False,
        )(*args)

    return run
```

```python
import functools
import math

import jax
import jax.numpy as jnp
from jax import lax
from jax.experimental import pallas as pl
from jax.experimental.pallas import tpu as pltpu
from jax.sharding import Mesh
from jax.sharding import PartitionSpec as P

HEAD_DIM = 128
LOG2E = math.log2(math.e)

norm_eps = 1e-05
f32 = jnp.float32
bf16 = jnp.bfloat16

SWAP = [(0, 1), (1, 0)]


def cost(us):
    return pl.CostEstimate(flops=int(us * 1e9), bytes_accessed=1 << 20, transcendentals=0)
DOT_NT = (((1,), (1,)), ((), ()))
DOT_NN = (((1,), (0,)), ((), ()))


def attend_kernel(groups, chunk, score_scale, q_ref, tok_q_ref, start_q_ref, *refs):
    key_refs = refs[: 3 * groups]
    o_ref, lse_ref = refs[-groups - 2 : -groups]
    vt_refs = refs[-groups:]
    rows = q_ref.shape[0]

    @pl.when(pl.program_id(0) == 0)
    def _():
        for g in range(groups):
            v_ref, vt_ref = key_refs[3 * g + 1], vt_refs[g]

            def turn(j, carry):
                r = pl.ds(pl.multiple_of(j * chunk, chunk), chunk)
                vt_ref[:, r] = v_ref[r, :].T
                return carry

            lax.fori_loop(0, v_ref.shape[0] // chunk, turn, 0)

    queries = q_ref[...]
    tok_q = tok_q_ref[...]
    start_q = start_q_ref[...]
    state = (
        jnp.full((1, rows), -1e30, f32),
        jnp.zeros((1, rows), f32),
        jnp.zeros((queries.shape[1], rows), f32),
    )
    for g in range(groups):
        k_ref, _, tok_k_ref = key_refs[3 * g : 3 * g + 3]
        vt_ref = vt_refs[g]

        def step(j, carry):
            run_max, run_sum, acc = carry
            r = pl.ds(pl.multiple_of(j * chunk, chunk), chunk)
            s = lax.dot_general(k_ref[r, :], queries, DOT_NT, preferred_element_type=f32)
            tok_k = tok_k_ref[r, :]
            s = jnp.where((tok_k <= tok_q) & (tok_k >= start_q), s * score_scale, -1e30)
            new_max = jnp.maximum(run_max, jnp.max(s, axis=0, keepdims=True))
            p = jnp.exp2(s - new_max)
            shrink = jnp.exp2(run_max - new_max)
            run_sum = run_sum * shrink + jnp.sum(p, axis=0, keepdims=True)
            acc = acc * shrink + lax.dot_general(
                vt_ref[:, r], p.astype(bf16), DOT_NN, preferred_element_type=f32
            )
            return new_max, run_sum, acc

        steps = k_ref.shape[0] // chunk
        state = lax.fori_loop(0, steps, step, state, unroll=steps <= 4)
    run_max, run_sum, acc = state
    o_ref[...] = (acc / run_sum).T
    lse_ref[...] = run_max + jnp.log2(run_sum)


def attend(queries, tok_q, start_q, key_groups, earlier=()):
    rows = queries.shape[0]
    block = min(1024, rows)
    chunk = 1024
    row = pl.BlockSpec((1, block), lambda i: (0, i))
    in_specs = [pl.BlockSpec((block, HEAD_DIM), lambda i: (i, 0)), row, row]
    operands = [queries, tok_q, start_q]
    scratch = []
    keys = 0
    for group in key_groups:
        count = group[0].shape[0]
        keys += count
        in_specs += [pl.BlockSpec(a.shape, lambda i: (0, 0)) for a in group]
        operands += group
        scratch.append(pltpu.VMEM((HEAD_DIM, count), bf16))
    in_specs += [pl.BlockSpec(memory_space=pl.ANY)] * len(earlier)
    operands += earlier
    return pl.pallas_call(
        functools.partial(
            attend_kernel, len(key_groups), chunk, LOG2E / math.sqrt(HEAD_DIM)
        ),
        grid=(rows // block,),
        in_specs=in_specs,
        out_specs=[pl.BlockSpec((block, HEAD_DIM), lambda i: (i, 0)), row],
        out_shape=[
            jax.ShapeDtypeStruct((rows, HEAD_DIM), f32),
            jax.ShapeDtypeStruct((1, rows), f32),
        ],
        scratch_shapes=scratch,
        compiler_params=params(48),
        cost_estimate=cost(19),
        name="attend",
    )(*operands)


def attend_grad_kernel(
    chunk,
    score_scale,
    grad_scale,
    q_ref,
    do_ref,
    lse_ref,
    delta_ref,
    tok_q_ref,
    start_q_ref,
    dq_in_ref,
    k_ref,
    v_ref,
    tok_k_ref,
    *refs,
):
    dq_ref, dk_ref, dv_ref, inner_q_ref, inner_k_ref, kt_ref, dk_acc, dv_acc = refs[-8:]

    def row_sums(a):
        ones = jnp.ones((8, a.shape[1]), f32)
        return lax.dot_general(
            ones, a, DOT_NT, precision=lax.Precision.HIGHEST, preferred_element_type=f32
        )[:1]

    steps = k_ref.shape[0] // chunk

    @pl.when(pl.program_id(0) == 0)
    def _():
        dk_acc[...] = jnp.zeros_like(dk_acc)
        dv_acc[...] = jnp.zeros_like(dv_acc)

        def turn(j, carry):
            r = pl.ds(pl.multiple_of(j * chunk, chunk), chunk)
            kt_ref[:, r] = k_ref[r, :].T
            return carry

        lax.fori_loop(0, steps, turn, 0)

    queries = q_ref[...]
    d_out = do_ref[...]
    tok_q = tok_q_ref[...]
    start_q = start_q_ref[...]
    lse = lse_ref[...]
    delta = delta_ref[...]

    def step(j, dq_t):
        r = pl.ds(pl.multiple_of(j * chunk, chunk), chunk)
        s = lax.dot_general(k_ref[r, :], queries, DOT_NT, preferred_element_type=f32)
        tok_k = tok_k_ref[r, :]
        allowed = (tok_k <= tok_q) & (tok_k >= start_q)
        p = jnp.exp2(jnp.where(allowed, s * score_scale - lse, -1e30))
        dp = lax.dot_general(v_ref[r, :], d_out, DOT_NT, preferred_element_type=f32)
        ds = (p * (dp - delta)).astype(bf16)
        dv_acc[r, :] += lax.dot_general(
            p.astype(bf16), d_out, DOT_NN, preferred_element_type=f32
        )
        dk_acc[r, :] += lax.dot_general(ds, queries, DOT_NN, preferred_element_type=f32)
        return dq_t + lax.dot_general(kt_ref[:, r], ds, DOT_NN, preferred_element_type=f32)

    dq_t = lax.fori_loop(
        0,
        steps,
        step,
        jnp.zeros((queries.shape[1], queries.shape[0]), f32),
        unroll=steps <= 4,
    )
    d_query = dq_in_ref[...] + (dq_t * grad_scale).T
    dq_ref[...] = d_query
    inner_q_ref[...] = row_sums(d_query * queries.astype(f32))

    @pl.when(pl.program_id(0) == pl.num_programs(0) - 1)
    def _():
        d_key = dk_acc[...] * grad_scale
        dk_ref[...] = d_key.astype(dk_ref.dtype)
        inner_k_ref[...] = row_sums(d_key * k_ref[...].astype(f32))
        dv_ref[...] = dv_acc[...].astype(dv_ref.dtype)


def attend_grad(
    queries, d_out, lse, delta, tok_q, start_q, dq_in, key_group, out_type, earlier=()
):
    rows = queries.shape[0]
    keys = key_group[0].shape[0]
    block = min(1024, rows)
    chunk = 1024
    row = pl.BlockSpec((1, block), lambda i: (0, i))
    head = pl.BlockSpec((block, HEAD_DIM), lambda i: (i, 0))
    whole = pl.BlockSpec((keys, HEAD_DIM), lambda i: (0, 0))
    return pl.pallas_call(
        functools.partial(
            attend_grad_kernel,
            chunk,
            LOG2E / math.sqrt(HEAD_DIM),
            1.0 / math.sqrt(HEAD_DIM),
        ),
        grid=(rows // block,),
        in_specs=[
            head,
            head,
            row,
            row,
            row,
            row,
            head,
            whole,
            whole,
            pl.BlockSpec((keys, 1), lambda i: (0, 0)),
        ]
        + [pl.BlockSpec(memory_space=pl.ANY)] * len(earlier),
        out_specs=[head, whole, whole, row, pl.BlockSpec((1, keys), lambda i: (0, 0))],
        out_shape=[
            jax.ShapeDtypeStruct((rows, HEAD_DIM), f32),
            jax.ShapeDtypeStruct((keys, HEAD_DIM), out_type),
            jax.ShapeDtypeStruct((keys, HEAD_DIM), out_type),
            jax.ShapeDtypeStruct((1, rows), f32),
            jax.ShapeDtypeStruct((1, keys), f32),
        ],
        scratch_shapes=[
            pltpu.VMEM((HEAD_DIM, keys), bf16),
            pltpu.VMEM((keys, HEAD_DIM), f32),
            pltpu.VMEM((keys, HEAD_DIM), f32),
        ],
        compiler_params=params(48),
        cost_estimate=cost(0.5),
        name="attend_grad",
    )(queries, d_out, lse, delta, tok_q, start_q, dq_in, *key_group, *earlier)


def pack_kernel(raw0_ref, raw1_ref, inv_ref, cos_ref, sin_ref, gain_ref, q_ref, k_ref):
    half = raw0_ref.shape[1]
    cos_tab = jnp.concatenate([cos_ref[...]] * 2, axis=1)
    sin_tab = jnp.concatenate([-sin_ref[...], sin_ref[...]], axis=1)
    for i, raw_ref in enumerate((raw0_ref, raw1_ref)):
        r = slice(i * half, (i + 1) * half)
        for j in range(2):
            u = raw_ref[j] * inv_ref[r, j : j + 1] * gain_ref[j : j + 1, :]
            turned = u * cos_tab[r, :] + pltpu.roll(u, HEAD_DIM // 2, 1) * sin_tab[r, :]
            (q_ref, k_ref)[j][0, r, :] = turned.astype(bf16)


def pack_heads(raw0, raw1, inv, cos_tab, sin_tab, gains):
    half = raw0.shape[1]
    rows = 2 * half
    heads = raw0.shape[2] // HEAD_DIM
    raw = pl.BlockSpec((2, half, HEAD_DIM), lambda h: (0, 0, h))
    head = pl.BlockSpec((1, rows, HEAD_DIM), lambda h: (h, 0, 0))
    table = pl.BlockSpec((rows, HEAD_DIM // 2), lambda h: (0, 0))
    return pl.pallas_call(
        pack_kernel,
        grid=(heads,),
        in_specs=[
            raw,
            raw,
            pl.BlockSpec((rows, 2), lambda h: (0, 0)),
            table,
            table,
            pl.BlockSpec((2, HEAD_DIM), lambda h: (0, h)),
        ],
        out_specs=[head, head],
        out_shape=[jax.ShapeDtypeStruct((heads, rows, HEAD_DIM), bf16)] * 2,
        cost_estimate=cost(4.7),
        name="pack_heads",
    )(raw0, raw1, inv, cos_tab, sin_tab, gains)


def raw_grad_kernel(
    dq_ref,
    dk_ref,
    dk_far_ref,
    dv_ref,
    dv_far_ref,
    q_ref,
    k_ref,
    inv_ref,
    inner_ref,
    cos_ref,
    sin_ref,
    gain_ref,
    *refs,
):
    out_ref, sum_ref = refs[-2:]

    @pl.when(pl.program_id(0) == 0)
    def _():
        sum_ref[...] = jnp.zeros_like(sum_ref)

    cos_tab = jnp.concatenate([cos_ref[...]] * 2, axis=1)
    sin_tab = jnp.concatenate([-sin_ref[...], sin_ref[...]], axis=1)
    block = inv_ref.shape[1]
    coef = jnp.concatenate([inv_ref[...], inner_ref[...], jnp.zeros((4, block), f32)]).T

    def turn_back(u):
        return u * cos_tab - pltpu.roll(u, HEAD_DIM // 2, 1) * sin_tab

    d_key = dk_ref[...] + dk_far_ref[...].astype(f32)
    for j, (grad, rows_ref) in enumerate(((dq_ref[...], q_ref), (d_key, k_ref))):
        gain = gain_ref[j : j + 1, :]
        cols = slice(j * HEAD_DIM, (j + 1) * HEAD_DIM)
        d_norm = turn_back(grad)
        hat = turn_back(rows_ref[...].astype(f32)) / gain
        sum_ref[j : j + 1, :] += jnp.sum(d_norm * hat, axis=0, keepdims=True)
        inv = coef[:, j : j + 1]
        inner = coef[:, 2 + j : 3 + j]
        out_ref[:, cols] = (inv * (d_norm * gain - hat * inner)).astype(bf16)
    out_ref[:, 2 * HEAD_DIM :] = (dv_ref[...] + dv_far_ref[...].astype(f32)).astype(bf16)


def raw_grad(d_query, d_key, d_value, queries, keys, inv, inner, cosine, sine, gains, earlier):
    rows = queries.shape[0]
    block = min(512, rows)

    def wide(cols):
        return pl.BlockSpec((block, cols), lambda i: (i, 0))

    whole = pl.BlockSpec((2, HEAD_DIM), lambda i: (0, 0))
    return pl.pallas_call(
        raw_grad_kernel,
        grid=(rows // block,),
        in_specs=[
            *[wide(HEAD_DIM)] * 7,
            pl.BlockSpec((2, block), lambda i: (0, i)),
            pl.BlockSpec((2, block), lambda i: (0, i)),
            wide(HEAD_DIM // 2),
            wide(HEAD_DIM // 2),
            whole,
            pl.BlockSpec(memory_space=pl.ANY),
        ],
        out_specs=[wide(3 * HEAD_DIM), whole],
        out_shape=[
            jax.ShapeDtypeStruct((rows, 3 * HEAD_DIM), bf16),
            jax.ShapeDtypeStruct((2, HEAD_DIM), f32),
        ],
        cost_estimate=cost(6),
        name="raw_grad",
    )(d_query, *d_key, *d_value, queries, keys, inv, inner, cosine, sine, gains, earlier)


def weight_grad_kernel(experts, out_block, at_ref, *refs):
    wide, far, narrow, compact = refs[:2], refs[2:4], refs[4:6], refs[6:8]
    out_ref, wide_t, tall = refs[-3:]
    half = wide[0].shape[0]
    blocks = far[0].shape[1] // out_block

    @pl.when(pl.program_id(0) == 0)
    def _():
        for z in range(blocks):
            rows = slice(z * out_block, (z + 1) * out_block)
            cols = (2 * z + at_ref[0]) * out_block
            cols = pl.ds(pl.multiple_of(cols, out_block), out_block)
            for i in range(2):
                wide_t[rows, i * half : (i + 1) * half] = wide[i][:, cols].T
                wide_t[rows, (2 + i) * half : (3 + i) * half] = far[i][:, rows].T

    e = lax.rem(pl.program_id(0), experts) if experts else None
    for i in range(2):
        tall[i * half : (i + 1) * half, :] = narrow[i][0]
        there = slice((2 + i) * half, (3 + i) * half)
        if not experts:
            tall[there, :] = compact[i][0]
            continue
        routes = refs[8][i * half : (i + 1) * half, :]
        block = jnp.zeros((half, tall.shape[1]), f32)
        for slot in range(routes.shape[1]):
            block = jnp.where(
                routes[:, slot : slot + 1] == e, compact[i][0, slot].astype(f32), block
            )
        tall[there, :] = block.astype(bf16)
    out_ref[0] = jnp.dot(wide_t[...], tall[...], preferred_element_type=f32).astype(bf16)


def weight_grad(wide_h, far_h, narrow, far_narrow, out_block, at, routes=None, experts=0, earlier=()):
    half, width = wide_h[0].shape
    out_width = far_h[0].shape[1]
    count, _, cols = narrow[0][0].shape

    def part(at):
        return pl.BlockSpec((1, half, cols), lambda j, x: (j, at, 0))

    specs = [part(at) for _, at in narrow]
    if experts:
        slots = routes.shape[1]
        specs += [pl.BlockSpec((1, slots, half, cols), lambda j, x: (j // experts, 0, 0, 0))] * 2
        specs.append(pl.BlockSpec(routes.shape, lambda j, x: (0, 0)))
        earlier = (routes, *earlier)
    else:
        specs += [part(at) for _, at in far_narrow]
    return pl.pallas_call(
        functools.partial(weight_grad_kernel, experts, out_block),
        grid_spec=pltpu.PrefetchScalarGridSpec(
            num_scalar_prefetch=1,
            grid=(count,),
            in_specs=[pl.BlockSpec(w.shape, lambda j, x: (0, 0)) for w in (*wide_h, *far_h)]
            + specs
            + waits(earlier[1:] if experts else earlier),
            out_specs=pl.BlockSpec((1, out_width, cols), lambda j, x: (j, 0, 0)),
            scratch_shapes=[
                pltpu.VMEM((out_width, 4 * half), bf16),
                pltpu.VMEM((4 * half, cols), bf16),
            ],
        ),
        out_shape=jax.ShapeDtypeStruct((count, out_width, cols), bf16),
        compiler_params=params(32),
        cost_estimate=cost(0.1),
        name="weight_grad",
    )(
        at.reshape(1),
        *wide_h,
        *far_h,
        *[a for a, _ in narrow],
        *[a for a, _ in far_narrow],
        *earlier,
    )


def waits(earlier):
    return [pl.BlockSpec(memory_space=pl.ANY)] * len(earlier)


def params(mib=16):
    return pltpu.CompilerParams(vmem_limit_bytes=mib * 1024 * 1024)


def project_kernel(x_ref, w_ref, *refs):
    raw_ref, sq_ref, v_ref = refs[-3:]
    kind, j = pl.program_id(0), pl.program_id(1)
    raw = jnp.dot(x_ref[...], w_ref[0], preferred_element_type=f32)

    @pl.when(kind < 2)
    def _():
        raw_ref[0] = raw
        ones = jnp.ones((8, raw.shape[1]), f32)
        square = lax.dot_general(
            ones, raw * raw, DOT_NT, precision=lax.Precision.HIGHEST, preferred_element_type=f32
        )
        sq_ref[0] = jnp.where(j == 0, square, sq_ref[0] + square)

    @pl.when(kind == 2)
    def _():
        for h in range(v_ref.shape[0]):
            v_ref[h] = raw[:, h * HEAD_DIM : (h + 1) * HEAD_DIM].astype(bf16)


def project(x, weights, earlier=()):
    count, width = x.shape
    cols = weights.shape[2]
    block = cols // 2
    heads = block // HEAD_DIM
    row = pl.BlockSpec((count, width), lambda k, j: (0, 0))

    def held(k, j):
        return jnp.minimum(k, 1), jnp.where(k == 2, 1, j)

    return pl.pallas_call(
        project_kernel,
        grid=(3, 2),
        in_specs=[row, pl.BlockSpec((1, width, block), lambda k, j: (k, 0, j))]
        + waits(earlier),
        out_specs=[
            pl.BlockSpec((1, count, block), lambda k, j: (held(k, j)[0], 0, held(k, j)[1])),
            pl.BlockSpec((1, 8, count), lambda k, j: (jnp.minimum(k, 1), 0, 0)),
            pl.BlockSpec((heads, count, HEAD_DIM), lambda k, j: (jnp.where(k == 2, j, 0), 0, 0)),
        ],
        out_shape=[
            jax.ShapeDtypeStruct((2, count, cols), f32),
            jax.ShapeDtypeStruct((2, 8, count), f32),
            jax.ShapeDtypeStruct((2 * heads, count, HEAD_DIM), bf16),
        ],
        compiler_params=params(32),
        cost_estimate=cost(0.1),
        name="project",
    )(x, weights, *earlier)


def attn_out_kernel(x_ref, w_ref, *refs):
    own_ref, other_ref, rows = refs[-3:]
    count = own_ref.shape[0]

    @pl.when(pl.program_id(0) == 0)
    def _():
        for h in range(x_ref.shape[0]):
            rows[:, h * HEAD_DIM : (h + 1) * HEAD_DIM] = x_ref[h]

    y = lax.dot_general(rows[...], w_ref[...], DOT_NT, preferred_element_type=f32).astype(bf16)
    own_ref[...] = y[:count]
    other_ref[...] = y[count:]


def attn_out_half(parts, half, weights, earlier=()):
    heads, count, _ = parts.shape
    count //= 2
    width, cols = weights.shape
    block = width // 4
    out = pl.BlockSpec((count // 2, block), lambda i: (0, i))
    return pl.pallas_call(
        attn_out_kernel,
        grid=(4,),
        in_specs=[
            pl.BlockSpec((heads, count, HEAD_DIM), lambda i: (0, half, 0)),
            pl.BlockSpec((block, cols), lambda i: (i, 0)),
        ]
        + waits(earlier),
        out_specs=[out, out],
        out_shape=[jax.ShapeDtypeStruct((count // 2, width), bf16)] * 2,
        scratch_shapes=[pltpu.VMEM((count, cols), bf16)],
        compiler_params=params(32),
        cost_estimate=cost(0.1),
        name="attn_out",
    )(parts, weights, *earlier)


def attn_out_grad_kernel(a_ref, w_ref, *refs):
    out_ref = refs[-1]
    y = jnp.dot(a_ref[...], w_ref[...], preferred_element_type=f32).astype(bf16)
    for h in range(out_ref.shape[0]):
        out_ref[h] = y[:, h * HEAD_DIM : (h + 1) * HEAD_DIM]


def attn_out_grad_half(grads, half, weights, into=None, earlier=()):
    count, width = grads.shape
    cols = weights.shape[1]
    heads = cols // HEAD_DIM
    block = cols // 2
    row = pl.BlockSpec((count, width), lambda j: (0, 0))
    into = () if into is None else (into,)
    return pl.pallas_call(
        attn_out_grad_kernel,
        grid=(2,),
        in_specs=[row, pl.BlockSpec((width, block), lambda j: (0, j))]
        + waits(into)
        + waits(earlier),
        out_specs=pl.BlockSpec((heads // 2, count, HEAD_DIM), lambda j: (j, half, 0)),
        out_shape=jax.ShapeDtypeStruct((heads, 2 * count, HEAD_DIM), bf16),
        input_output_aliases={2: 0} if into else {},
        compiler_params=params(16),
        cost_estimate=cost(0.1),
        name="attn_out_grad",
    )(grads, weights, *into, *earlier)


def project_grad_kernel(x_ref, w_ref, *refs):
    own_ref, other_ref, rows = refs[-3:]
    count = own_ref.shape[0]
    heads = x_ref.shape[0]
    cols = heads * HEAD_DIM

    @pl.when(pl.program_id(0) == 0)
    def _():
        for k in range(3):
            for h in range(heads):
                at = k * cols + h * HEAD_DIM
                rows[:, at : at + HEAD_DIM] = x_ref[h, :, k * HEAD_DIM : (k + 1) * HEAD_DIM]

    y = None
    for k in range(3):
        term = lax.dot_general(
            rows[:, k * cols : (k + 1) * cols], w_ref[k], DOT_NT, preferred_element_type=f32
        )
        y = term if y is None else y + term
    own_ref[...] = y[:count].astype(bf16)
    other_ref[...] = y[count:].astype(bf16)


def project_grad_half(parts, half, weights, earlier=()):
    heads, count, cols = parts.shape
    count //= 2
    width = weights.shape[1]
    block = width // 4
    part = pl.BlockSpec((count // 2, block), lambda i: (0, i))
    return pl.pallas_call(
        project_grad_kernel,
        grid=(4,),
        in_specs=[
            pl.BlockSpec((heads, count, cols), lambda i: (0, half, 0)),
            pl.BlockSpec((3, block, weights.shape[2]), lambda i: (0, i, 0)),
        ]
        + waits(earlier),
        out_specs=[part, part],
        out_shape=[
            jax.ShapeDtypeStruct((count // 2, width), bf16),
            jax.ShapeDtypeStruct((count // 2, width), bf16),
        ],
        scratch_shapes=[pltpu.VMEM((count, heads * cols), bf16)],
        compiler_params=params(24),
        cost_estimate=cost(6),
        name="project_grad",
    )(parts, weights, *earlier)


def qkv_grad_kernel(wide_ref, grad_ref, grad_other_ref, *refs):
    out_ref, out_other_ref, tall, wide_t = refs[-4:]
    rows, cols = grad_ref.shape

    @pl.when(pl.program_id(0) == 0)
    def _():
        tall[:, :cols] = grad_ref[...]
        block = rows // 16
        for i in range(16):
            tall[i * block : (i + 1) * block, cols:] = grad_other_ref[
                (i ^ 1) * block : ((i ^ 1) + 1) * block, :
            ]

    wide_t[...] = wide_ref[...].T
    out = jnp.dot(wide_t[...], tall[...], preferred_element_type=f32).astype(bf16)
    out_ref[...] = out[:, :cols]
    out_other_ref[...] = out[:, cols:]


def qkv_grad(wide, grad, grad_other, z_count, earlier=()):
    assert z_count == 4
    rows, width = wide.shape
    cols = grad.shape[1]
    block = min(256, width)
    whole = pl.BlockSpec(grad.shape, lambda i: (0, 0))
    out = pl.BlockSpec((block, cols), lambda i: (i, 0))
    return pl.pallas_call(
        qkv_grad_kernel,
        grid=(width // block,),
        in_specs=[pl.BlockSpec((rows, block), lambda i: (0, i)), whole, whole] + waits(earlier),
        out_specs=[out, out],
        scratch_shapes=[pltpu.VMEM((rows, 2 * cols), bf16), pltpu.VMEM((block, rows), bf16)],
        out_shape=[jax.ShapeDtypeStruct((width, cols), bf16)] * 2,
        compiler_params=params(40),
        cost_estimate=cost(10),
        name="qkv_grad",
    )(wide, grad, grad_other, *earlier)


def arrange(near, z_pos, earlier=()):
    rows, cols = near[0].shape
    z_count = len(near)

    def kernel(z_ref, *refs):
        for i in range(z_count):

            @pl.when(pl.program_id(0) == i)
            def _():
                refs[-1][...] = refs[i][...]

    return pl.pallas_call(
        kernel,
        grid_spec=pltpu.PrefetchScalarGridSpec(
            num_scalar_prefetch=1,
            grid=(z_count,),
            in_specs=[pl.BlockSpec((rows, cols), lambda i, z: (0, 0))] * z_count + waits(earlier),
            out_specs=pl.BlockSpec(
                (rows, cols), lambda i, z: (lax.rem(z[0] - i + z_count, z_count), 0)
            ),
        ),
        out_shape=jax.ShapeDtypeStruct((z_count * rows, cols), near[0].dtype),
        compiler_params=params(),
        cost_estimate=cost(0.1),
        name="arrange",
    )(z_pos.reshape(1), *near, *earlier)


def own_grad_kernel(w0_ref, w1_ref, n0_ref, n1_ref, *refs):
    out_ref, wide_t = refs[-2:]
    half = w0_ref.shape[0]

    @pl.when(pl.program_id(0) == 0)
    def _():
        wide_t[:, :half] = w0_ref[...].T
        wide_t[:, half:] = w1_ref[...].T

    tall = jnp.concatenate(
        [n0_ref[...].reshape(n0_ref.shape[-2:]), n1_ref[...].reshape(n1_ref.shape[-2:])]
    )
    out_ref[0] = jnp.dot(wide_t[...], tall, preferred_element_type=f32).astype(bf16)


def own_grad(wide_h, narrow_h, earlier=()):
    half, width = wide_h[0].shape
    count, rows, cols = narrow_h[0].shape
    narrow = [
        pl.BlockSpec((1, half, cols), lambda j, at=i * (rows // half - 1): (j, at, 0))
        for i in range(2)
    ]
    return pl.pallas_call(
        own_grad_kernel,
        grid=(count,),
        in_specs=[pl.BlockSpec((half, width), lambda j: (0, 0))] * 2 + narrow + waits(earlier),
        out_specs=pl.BlockSpec((1, width, cols), lambda j: (j, 0, 0)),
        out_shape=jax.ShapeDtypeStruct((count, width, cols), bf16),
        scratch_shapes=[pltpu.VMEM((width, 2 * half), bf16)],
        compiler_params=params(24),
        cost_estimate=cost(3.5),
        name="own_grad",
    )(*wide_h, *narrow_h, *earlier)


def join_kernel(a_ref, b_ref, *refs):
    n = a_ref.shape[0]
    refs[-1][:n] = a_ref[...]
    refs[-1][n:] = b_ref[...]


def join_rows(a, b, earlier=()):
    rows, width = a.shape
    block = width // 2
    part = pl.BlockSpec((rows, block), lambda j: (0, j))
    return pl.pallas_call(
        join_kernel,
        grid=(2,),
        in_specs=[part, part] + waits(earlier),
        out_specs=pl.BlockSpec((2 * rows, block), lambda j: (0, j)),
        out_shape=jax.ShapeDtypeStruct((2 * rows, width), a.dtype),
        compiler_params=params(),
        cost_estimate=cost(0.1),
        name="join_rows",
    )(a, b, *earlier)


def pass_kernel(in_ref, *refs):
    refs[-1][...] = in_ref[...]


def pass_rows(a, earlier):
    rows, width = a.shape
    spec = pl.BlockSpec((rows // 2, width), lambda j: (j, 0))
    if rows < 32:
        spec = pl.BlockSpec((rows, width // 2), lambda j: (0, j))
    return pl.pallas_call(
        pass_kernel,
        grid=(2,),
        in_specs=[spec] + waits(earlier),
        out_specs=spec,
        out_shape=jax.ShapeDtypeStruct(a.shape, a.dtype),
        compiler_params=params(),
        cost_estimate=cost(0.1),
        name="pass_rows",
    )(a, *earlier)


def round_kernel(in_ref, *refs):
    refs[-1][...] = in_ref[...].astype(bf16)


def round_weights(a, earlier=()):
    flat = a.reshape(-1, a.shape[-1])
    rows, cols = flat.shape
    block = min(rows, 1 << 20 >> (cols.bit_length() - 1))
    spec = pl.BlockSpec((block, cols), lambda i: (i, 0))
    out = pl.pallas_call(
        round_kernel,
        grid=(rows // block,),
        in_specs=[spec] + waits(earlier),
        out_specs=spec,
        out_shape=jax.ShapeDtypeStruct(flat.shape, bf16),
        compiler_params=params(),
        cost_estimate=cost(9),
        name="round_weights",
    )(flat, *earlier)
    return out.reshape(a.shape)


def add_kernel(a_ref, b_ref, *refs):
    refs[-1][...] = (a_ref[...].astype(f32) + b_ref[...].astype(f32)).astype(bf16)


def add_rows(a, b, earlier=()):
    spec = pl.BlockSpec((a.shape[0] // 2, *a.shape[1:]), lambda i: (i, 0, 0))
    return pl.pallas_call(
        add_kernel,
        grid=(2,),
        in_specs=[spec, spec] + waits(earlier),
        out_specs=spec,
        out_shape=jax.ShapeDtypeStruct(a.shape, bf16),
        compiler_params=params(),
        cost_estimate=cost(1),
        name="add_rows",
    )(a, b, *earlier)


def first_gain_kernel(z_ref, w_ref, grad_ref, gain_ref, out_ref):
    total = None
    for k in range(3):
        cols = slice(k * HEAD_DIM, (k + 1) * HEAD_DIM)
        term = w_ref[k].astype(f32) * grad_ref[:, cols].astype(f32)
        total = term if total is None else total + term
    ones = jnp.ones((8, HEAD_DIM), f32)
    total = lax.dot_general(
        ones, total, DOT_NT, precision=lax.Precision.HIGHEST, preferred_element_type=f32
    )
    out_ref[...] = total[:1] / gain_ref[...]


def first_gain(weights, grad, gain, z_pos):
    width = grad.shape[0]
    block = width // 4
    line = pl.BlockSpec((1, block), lambda i, z: (0, i))
    return pl.pallas_call(
        first_gain_kernel,
        grid_spec=pltpu.PrefetchScalarGridSpec(
            num_scalar_prefetch=1,
            grid=(4,),
            in_specs=[
                pl.BlockSpec((3, block, HEAD_DIM), lambda i, z: (0, i, z[0])),
                pl.BlockSpec((block, grad.shape[1]), lambda i, z: (i, 0)),
                line,
            ],
            out_specs=line,
        ),
        out_shape=jax.ShapeDtypeStruct((1, width), f32),
        compiler_params=params(),
        cost_estimate=cost(2),
        name="first_gain",
    )(z_pos.reshape(1), weights, grad, gain.reshape(1, width))


def stack_kernel(first_ref, second_ref, qk_ref, router_ref, out_ref):
    out_ref[0:1, :] = first_ref[...]
    out_ref[1:2, :] = second_ref[...]
    out_ref[2:4, :] = qk_ref[...]
    out_ref[4:8, :] = router_ref[...]


def stack_rows(*rows):
    return pl.pallas_call(
        stack_kernel,
        out_shape=jax.ShapeDtypeStruct((8, rows[0].shape[1]), f32),
        compiler_params=params(),
        cost_estimate=cost(0.1),
        name="stack_rows",
    )(*rows)


def stack_inner_kernel(q_ref, k_ref, k_far_ref, *refs):
    refs[-1][0:1, :] = q_ref[...]
    refs[-1][1:2, :] = k_ref[...] + k_far_ref[...]


def stack_inner(inner_q, inner_k, inner_k_far, earlier):
    return pl.pallas_call(
        stack_inner_kernel,
        in_specs=[pl.BlockSpec(memory_space=pltpu.VMEM)] * 3 + waits(earlier),
        out_shape=jax.ShapeDtypeStruct((2, inner_q.shape[1]), f32),
        compiler_params=params(),
        cost_estimate=cost(0.1),
        name="stack_inner",
    )(inner_q, inner_k, inner_k_far, *earlier)


def row_sum(refs):
    return refs[0][...].astype(f32) + refs[1][...].astype(f32) + refs[2][...].astype(f32)


def inv_rms(rows):
    return lax.rsqrt(jnp.mean(rows * rows, axis=-1, keepdims=True) + norm_eps)


def mix_kernel(near, near_got, far_got, in_ref, gain_ref, *refs):
    residual_ref, mixed_ref = refs[-2:]
    residual = in_ref[...].astype(f32) + row_sum((near, near_got, far_got))
    residual_ref[...] = residual
    mixed_ref[...] = (residual * inv_rms(residual) * gain_ref[...]).astype(bf16)


def gap_kernel(near, near_got, far_got, residual_ref, target_ref, *refs):
    out_ref, gap_ref, gap_b_ref = refs[-3:]
    out = residual_ref[...] + row_sum((near, near_got, far_got))
    out_ref[...] = out.astype(bf16)
    gap = out - target_ref[...].astype(f32)
    gap_ref[...] = gap
    gap_b_ref[...] = gap.astype(bf16)


def resid_grad_kernel(near, near_got, far_got, residual_ref, gap_ref, gain_ref, *refs):
    grad_ref, grad_b_ref, sum_ref = refs[-3:]
    d_mixed = row_sum((near, near_got, far_got))
    residual = residual_ref[...]
    inv = inv_rms(residual)
    hat = residual * inv
    grad = gap_ref[...] + norm_back(d_mixed, hat, inv, gain_ref[...])
    grad_ref[...] = grad
    grad_b_ref[...] = grad.astype(bf16)

    @pl.when(pl.program_id(0) == 0)
    def _():
        sum_ref[...] = jnp.zeros_like(sum_ref)

    sum_ref[...] += jnp.sum(d_mixed * hat, axis=0, keepdims=True)


def input_grad_kernel(near, near_got, far_got, in_ref, grad_ref, gain_ref, *refs):
    rows = in_ref[...].astype(f32)
    inv = inv_rms(rows)
    d_normed = row_sum((near, near_got, far_got))
    grad = grad_ref[...] + norm_back(d_normed, rows * inv, inv, gain_ref[...])
    refs[-1][...] = grad.astype(bf16)


def row_call(kernel, terms, rows, gain, outs, earlier=()):
    count, width = rows[0].shape
    block = min(32, count)
    spec = pl.BlockSpec((block, width), lambda i: (i, 0))
    line = pl.BlockSpec((1, width), lambda i: (0, 0))
    gains = [] if gain is None else [gain.reshape(1, width)]
    return pl.pallas_call(
        kernel,
        grid=(count // block,),
        in_specs=[spec] * (len(terms) + len(rows))
        + [line] * len(gains)
        + [pl.BlockSpec(memory_space=pl.ANY)] * len(earlier),
        out_specs=[line if o is None else spec for o in outs],
        out_shape=[
            jax.ShapeDtypeStruct((1, width) if o is None else (count, width), f32 if o is None else o)
            for o in outs
        ],
        compiler_params=params(16),
        cost_estimate=cost(0.1),
        name=kernel.__name__,
    )(*terms, *rows, *gains, *earlier)


def pick_kernel(cols, z_count, c_ref, r0_ref, r1_ref, *refs):
    out_ref = refs[-1]
    half = r0_ref.shape[0]
    out_ref[:half] = r0_ref[...]
    out_ref[half:] = r1_ref[...]


def pick_half(rows_h, at, earlier=()):
    half, width = rows_h[0].shape
    cols = width // 2
    block = cols // 2
    return pl.pallas_call(
        functools.partial(pick_kernel, cols, 2),
        grid_spec=pltpu.PrefetchScalarGridSpec(
            num_scalar_prefetch=1,
            grid=(2,),
            in_specs=[pl.BlockSpec((half, block), lambda j, c: (0, 2 * c[0] + j))] * 2
            + [pl.BlockSpec(memory_space=pl.ANY)] * len(earlier),
            out_specs=pl.BlockSpec((2 * half, block), lambda j, c: (0, j)),
        ),
        out_shape=jax.ShapeDtypeStruct((2 * half, cols), rows_h[0].dtype),
        cost_estimate=cost(0.1),
        name="pick_half",
    )(at.reshape(1), *rows_h, *earlier)


def token_places(seq_lengths, permutation):
    seq_ends = jnp.cumsum(seq_lengths)
    seq_starts = seq_ends - seq_lengths
    seq_id = jnp.sum((permutation[:, None] >= seq_ends[None, :]).astype(jnp.int32), axis=1)
    member = seq_id[:, None] == jnp.arange(seq_lengths.shape[0], dtype=jnp.int32)[None, :]
    return jnp.sum(jnp.where(member, seq_starts[None, :], 0), axis=1)


def near_first(a, axis, y_pos, c_pos):
    a = jnp.where(y_pos == 0, a, jnp.flip(a, axis))
    return jnp.where(c_pos == 0, a, jnp.flip(a, axis + 1))


def norm_back(grad_out, hat_rows, inv_rows, gain_row):
    grad_hat = grad_out * gain_row
    return inv_rows * (grad_hat - hat_rows * jnp.mean(grad_hat * hat_rows, axis=-1, keepdims=True))


def gather_near(rows):
    far = lax.ppermute(rows, "y", SWAP)
    return join_rows(rows, lax.ppermute(rows, "c", SWAP)), far


def gather_far(far, beside=(), earlier=()):
    if beside:
        far = pass_rows(far, beside)
    return join_rows(far, lax.ppermute(far, "c", SWAP), earlier)


def scatter_halves(near, far):
    sent = far[0].astype(f32) + lax.ppermute(far[1], "c", SWAP).astype(f32)
    sent = sent.astype(bf16)
    far_got = lax.ppermute(sent, "y", SWAP)
    near_got = lax.ppermute(near[1], "c", SWAP)
    return (near[0], near_got, far_got), sent


def sum_near(a):
    a = a + jnp.flip(lax.ppermute(a, "c", SWAP), -2)
    return a + jnp.flip(lax.ppermute(a, "y", SWAP), -3)


def sum_line(a, z_count):
    step = 1
    while step < z_count:
        a = a + lax.ppermute(a, "z", [(i, i ^ step) for i in range(z_count)])
        step *= 2
    return a


def local(
    z_count,
    x_count,
    block_in,
    target,
    seq_lengths,
    permutation,
    routes,
    attn_qkv,
    attn_out,
    norm_gains,
    router,
    gate_up,
    down,
):
    z_pos = lax.axis_index("z")
    x_pos = lax.axis_index("x")
    y_pos = lax.axis_index("y")
    c_pos = lax.axis_index("c")
    pair = x_count == 2
    local_rows, model_width = block_in.shape
    tok_rows = 4 * local_rows
    line_rows = z_count * tok_rows
    head_cols = attn_qkv.shape[2]
    hidden_cols = gate_up.shape[3]
    experts = gate_up.shape[1]
    wide_block = model_width // z_count
    out_block = wide_block // x_count
    wt_pos = y_pos * 2 + c_pos

    qkv_b = attn_qkv.astype(bf16)
    router_b = router.astype(bf16)

    def scatter_x(a):
        if pair:
            mine = lax.dynamic_index_in_dim(a, x_pos, 0, False)
            other = lax.dynamic_index_in_dim(a, 1 - x_pos, 0, False)
            return mine.astype(f32) + lax.ppermute(other.astype(bf16), "x", SWAP).astype(f32)
        return lax.psum_scatter(a.astype(bf16), "x", scatter_dimension=0).astype(f32)

    def of_parity(rows_h, at):
        return jnp.concatenate(
            [
                jnp.concatenate(
                    [
                        lax.dynamic_slice_in_dim(
                            r, z * wide_block + at * out_block, out_block, 1
                        )
                        for z in range(z_count)
                    ],
                    axis=1,
                )
                for r in rows_h
            ]
        )

    def far_wide(rows_h):
        return lax.ppermute(of_parity(rows_h, 1 - x_pos), "x", SWAP)

    def swap_x(parts):
        return [lax.ppermute(p, "x", SWAP) for p in parts]

    resid_in = block_in.astype(f32)
    inv_first = lax.rsqrt(jnp.mean(resid_in * resid_in, axis=-1, keepdims=True) + norm_eps)
    hat_first = resid_in * inv_first
    normed = (hat_first * norm_gains[0]).astype(bf16)
    normed_near, normed_far = gather_near(normed)
    normed_h = [normed_near, gather_far(normed_far)]

    start_all = token_places(seq_lengths, permutation)
    shape = (z_count, x_count, 2, 2, local_rows)
    tok_all = near_first(permutation.reshape(shape), 2, y_pos, c_pos)
    start_all = near_first(start_all.reshape(shape), 2, y_pos, c_pos)

    def of_x(a, at):
        return lax.dynamic_index_in_dim(a, at, 1, False).reshape(line_rows)

    tok_own = of_x(tok_all, x_pos)
    start_own = of_x(start_all, x_pos)
    tok_q = tok_own.reshape(1, line_rows)
    start_q = start_own.reshape(1, line_rows)
    half_dim = HEAD_DIM // 2
    frequency = jnp.exp(
        jnp.arange(half_dim, dtype=f32) * (-2.0 * math.log(10000.0) / HEAD_DIM)
    )
    angles = (tok_own - start_own).astype(f32)[:, None] * frequency[None, :]
    cosine, sine = jnp.cos(angles), jnp.sin(angles)

    raw0, square0, v0 = project(normed_h[0], qkv_b)
    raw1, square1, v1 = project(normed_h[1], qkv_b, (v0,))
    squares = jnp.concatenate([square0[:, 0], square1[:, 0]], axis=1)
    squares = sum_near(squares.reshape(2, 2, 2, local_rows)).reshape(2, tok_rows)
    inv_qk = lax.rsqrt(squares / model_width + norm_eps)
    inv_slots = jnp.where(
        (jnp.arange(z_count, dtype=jnp.int32) == z_pos)[:, None, None], inv_qk[None], 0.0
    )
    inv_line = sum_line(inv_slots, z_count)
    gain_qk = lax.dynamic_slice_in_dim(norm_gains[2:], wt_pos * head_cols, head_cols, 1)

    def to_heads_apart(parts, earlier=()):
        near = [lax.dynamic_index_in_dim(parts, z_pos, 0, False)]
        for d in range(1, z_count):
            there = lax.dynamic_index_in_dim(parts, (z_pos + d) % z_count, 0, False)
            near.append(
                lax.ppermute(there, "z", [(i, (i + d) % z_count) for i in range(z_count)])
            )
        return arrange(near, z_pos, earlier)

    def to_heads(parts):
        return lax.all_to_all(parts, "z", 0, 0, tiled=True).reshape(line_rows, HEAD_DIM)

    def from_x(a):
        if pair:
            return lax.ppermute(a, "x", SWAP)
        return lax.all_gather(a, "x", axis=0)

    v_heads = jnp.concatenate([v0, v1], axis=1)
    q_heads, k_heads = pack_heads(
        raw0,
        raw1,
        inv_qk.T,
        lax.dynamic_slice_in_dim(cosine, z_pos * tok_rows, tok_rows),
        lax.dynamic_slice_in_dim(sine, z_pos * tok_rows, tok_rows),
        gain_qk,
    )
    values = pass_rows(to_heads(v_heads), (k_heads,))
    values_far = from_x(values)
    keys = to_heads_apart(k_heads, (values_far,))
    out_b = attn_out.astype(bf16)
    keys_far = from_x(keys)
    queries = to_heads_apart(q_heads)
    tok_col = tok_own.reshape(line_rows, 1)
    if pair:
        tok_far = of_x(tok_all, 1 - x_pos).reshape(line_rows, 1)
        groups = [(keys_far, values_far, tok_far), (keys, values, tok_col)]
        key_groups = groups[::-1]
    else:
        tok_x = jnp.moveaxis(tok_all, 1, 0).reshape(x_count, line_rows, 1)
        groups = [(keys_far[i], values_far[i], tok_x[i]) for i in range(x_count)]
        key_groups = [
            (
                keys_far.reshape(-1, HEAD_DIM),
                values_far.reshape(-1, HEAD_DIM),
                tok_x.reshape(-1, 1),
            )
        ]
    attn_f, row_lse = attend(
        queries, tok_q, start_q, key_groups
    )

    def to_tokens(rows, cols):
        parts = lax.all_to_all(
            rows.reshape(z_count, tok_rows, cols), "z", 0, 0, tiled=True
        )
        return parts

    attn_parts = to_tokens(attn_f.astype(bf16), HEAD_DIM)
    normed_pick = pick_half(normed_h, c_pos, (attn_parts,))
    attn_far = attn_out_half(attn_parts, 1, out_b)
    attn_near = attn_out_half(attn_parts, 0, out_b)
    attn_y, attn_sent = scatter_halves(attn_near, attn_far)
    normed_line = lax.all_gather(normed_pick, "z", axis=0, tiled=True)
    gu_b = round_weights(gate_up, (attn_sent,))
    residual, mixed_rows = row_call(
        mix_kernel,
        attn_y,
        (block_in,),
        norm_gains[1],
        (f32, bf16),
        (gu_b, normed_pick),
    )
    down_b = round_weights(down, (mixed_rows,))
    mixed_near, mixed_far = gather_near(mixed_rows)

    def halves(a):
        return a[: a.shape[0] // 2], a[a.shape[0] // 2 :]

    route_rows = near_first(routes.reshape(2, 2, local_rows, -1), 0, y_pos, c_pos)
    route_rows = route_rows.reshape(tok_rows, -1)
    if pair:
        routes_far = lax.ppermute(route_rows.T.astype(f32), "x", SWAP).T.astype(jnp.int32)
    choose = jnp.sum(
        (route_rows[:, :, None] == jnp.arange(experts, dtype=jnp.int32)[None, None, :]).astype(f32),
        axis=1,
    )

    def expert_rows(mixed, choose):
        prob = jax.nn.softmax(jnp.dot(mixed, router_b, preferred_element_type=f32), axis=-1)
        gate_w = prob * choose
        gate_in, up_in = jnp.einsum("td,kedf->ketf", mixed, gu_b, preferred_element_type=f32)
        gate_sig = jax.nn.sigmoid(gate_in)
        hidden = (gate_w.T[:, :, None] * (gate_in * gate_sig) * up_in).astype(bf16)
        y = jnp.einsum("etf,edf->td", hidden, down_b, preferred_element_type=f32)
        return y.astype(bf16), hidden, (mixed, choose, prob, gate_w, gate_in, up_in)

    choose_h = halves(choose)
    near_y, hidden0, kept0 = expert_rows(mixed_near, choose_h[0])
    mixed_h = [mixed_near, gather_far(mixed_far, (down_b,), (near_y,))]
    mixed_far = [far_wide([m]) for m in mixed_h] if pair else [mixed_rows, mixed_rows]
    far_y, hidden1, kept1 = expert_rows(mixed_h[1], choose_h[1])
    hidden_h = [hidden0, hidden1]
    expert_y, _ = scatter_halves(halves(near_y), halves(far_y))
    block_out, cot_local, cot_b = row_call(
        gap_kernel, expert_y, (residual, target), None, (bf16, f32, bf16),
        (mixed_far[0],),
    )
    def expert_rows_back(cot, kept):
        mixed, choose, prob, gate_w, gate_in, up_in = kept
        d_hid = (
            jnp.einsum("td,edf->etf", cot, down_b, preferred_element_type=f32)
            .astype(bf16)
            .astype(f32)
        )
        gate_sig = jax.nn.sigmoid(gate_in)
        gate_act = gate_in * gate_sig
        d_gate_w = jnp.sum(d_hid * gate_act * up_in, axis=-1).T
        scaled = d_hid * gate_w.T[:, :, None]
        d_gate_in = scaled * up_in * gate_sig * (1.0 + gate_in * (1.0 - gate_sig))
        d_pre = jnp.stack([d_gate_in, scaled * gate_act]).astype(bf16)
        d_prob = d_gate_w * choose
        d_logit = (prob * (d_prob - jnp.sum(prob * d_prob, axis=-1, keepdims=True))).astype(bf16)
        d_mixed = (
            jnp.einsum("ketf,kedf->td", d_pre, gu_b, preferred_element_type=f32)
            + lax.dot_general(d_logit, router_b, DOT_NT, preferred_element_type=f32)
        ).astype(bf16)
        router_part = lax.dot_general(
            d_logit, mixed, (((0,), (0,)), ((), ())), preferred_element_type=f32
        )
        return d_mixed, d_pre, router_part

    cot_near, cot_far = gather_near(cot_b)
    near_d, d_pre0, router0 = expert_rows_back(cot_near, kept0)
    cot_h = [cot_near, gather_far(cot_far, (), (mixed_far[1], normed_line, near_d))]
    far_d, d_pre1, router1 = expert_rows_back(cot_h[1], kept1)
    router_rows = router0 + router1
    d_pre_h = [d_pre0, d_pre1]
    d_mixed, d_mixed_sent = scatter_halves(halves(near_d), halves(far_d))
    down_part = own_grad(cot_h, hidden_h, (d_mixed_sent,))

    def compact(a, taken):
        a = a.reshape(-1, experts, *a.shape[1:])
        taken = taken.T[:, None, :, None]
        parts = []
        for slot in range(taken.shape[0]):
            part = a[:, 0]
            for e in range(1, experts):
                part = jnp.where(taken[slot] == e, a[:, e], part)
            parts.append(part)
        return jnp.stack(parts, axis=1)

    def plain_part(wide_h, narrow, spec):
        return scatter_x(
            jnp.stack(
                [
                    jnp.einsum(spec, of_parity(wide_h, i), narrow, preferred_element_type=f32)
                    for i in range(x_count)
                ]
            )
        ).astype(bf16)

    d_pre_h = [d.reshape(2 * experts, -1, hidden_cols) for d in d_pre_h]
    if pair:
        d_pre_far = [
            lax.ppermute(compact(d, r), "x", SWAP) for d, r in zip(d_pre_h, (route_rows[: tok_rows // 2], route_rows[tok_rows // 2 :]))
        ]
    d_resid, d_resid_b, gain_second = row_call(
        resid_grad_kernel,
        d_mixed,
        (residual, cot_local),
        norm_gains[1],
        (f32, bf16, None),
        (down_part, d_pre_far[0]) if pair else (down_part,),
    )
    resid_near, resid_far = gather_near(d_resid_b)
    d_resid_h = [resid_near, gather_far(resid_far, (), (d_pre_far[1],) if pair else ())]
    d_attn = attn_out_grad_half(d_resid_h[0], 0, out_b)
    d_attn = attn_out_grad_half(d_resid_h[1], 1, out_b, d_attn)

    d_out = to_heads(d_attn)
    delta = jnp.sum(d_out.astype(f32) * attn_f, axis=-1).reshape(1, line_rows)
    d_query = jnp.zeros((line_rows, HEAD_DIM), f32)
    if pair:
        gate_up_part = weight_grad(
            mixed_h,
            mixed_far,
            [(d, 0) for d in d_pre_h],
            [(d, 0) for d in d_pre_far],
            out_block,
            x_pos,
            routes_far,
            experts,
            (d_attn,),
        )
    else:
        gate_up_part = plain_part(mixed_h, jnp.concatenate(d_pre_h, axis=1), "td,ntf->ndf")
    down_part = lax.psum_scatter(down_part, "z", scatter_dimension=1, tiled=True)
    gate_up_sum = lax.psum_scatter(gate_up_part, "z", scatter_dimension=1, tiled=True)
    d_kv = []
    inner_k = []
    earlier = (gate_up_part,)
    for i, group in enumerate(groups):
        last = i == len(groups) - 1
        d_query, *d_group, inner_q, inner_k_part = attend_grad(
            queries,
            d_out,
            row_lse,
            delta,
            tok_q,
            start_q,
            d_query,
            group,
            f32 if pair and last else bf16,
            earlier,
        )
        d_kv.append(d_group)
        inner_k.append(inner_k_part)
        if i == 0:
            earlier = (down_part,)
    if pair:
        d_key, d_value = [
            (own, lax.ppermute(far, "x", SWAP)) for far, own in zip(*d_kv)
        ]
        inner = stack_inner(
            inner_q, inner_k[1], lax.ppermute(inner_k[0], "x", SWAP), (d_key[1], d_value[1])
        )
    else:
        d_key, d_value = [
            (
                lax.psum_scatter(jnp.stack(parts), "x", scatter_dimension=0).astype(f32),
                jnp.zeros((line_rows, HEAD_DIM), bf16),
            )
            for parts in zip(*d_kv)
        ]
        inner_k = lax.psum_scatter(jnp.stack(inner_k), "x", scatter_dimension=0)
        inner = jnp.concatenate([inner_q, inner_k])
    inner = sum_line(sum_near(inner.reshape(2, z_count, 2, 2, local_rows)), z_count)
    inner = inner.reshape(2, line_rows) / model_width
    inv_line = jnp.moveaxis(inv_line, 0, 1).reshape(2, line_rows)
    head_gain = lax.dynamic_slice_in_dim(gain_qk, z_pos * HEAD_DIM, HEAD_DIM, 1)
    d_raw, gain_sums = raw_grad(
        d_query,
        d_key,
        d_value,
        queries,
        keys,
        inv_line,
        inner,
        cosine,
        sine,
        head_gain,
        gate_up_sum,
    )
    gain_full = lax.dynamic_update_slice_in_dim(
        jnp.zeros((2, model_width), f32), gain_sums, (wt_pos * z_count + z_pos) * HEAD_DIM, 1
    )

    def sum_all(a):
        a = a + lax.ppermute(a, "c", SWAP)
        a = a + lax.ppermute(a, "y", SWAP)
        a = a + lax.ppermute(a, "x", SWAP) if pair else lax.psum(a, "x")
        a = pass_rows(a, (input_grad,))
        return sum_line(a, z_count)

    grad_mine, grad_other = qkv_grad(
        normed_line, d_raw, lax.ppermute(d_raw, "c", SWAP), z_count
    )
    grad_other = lax.ppermute(grad_other, "c", SWAP)
    qkv_full = jnp.where(
        c_pos == 0,
        jnp.stack([grad_mine, grad_other]),
        jnp.stack([grad_other, grad_mine]),
    ).reshape(z_count, x_count, out_block, 3 * HEAD_DIM)
    gain_first = first_gain(
        qkv_b, qkv_full.reshape(model_width, 3 * HEAD_DIM), norm_gains[0], z_pos
    )
    qkv_line = jnp.moveaxis(qkv_full, 1, 0)
    if pair:
        qkv_line = (
            lax.dynamic_index_in_dim(qkv_line, x_pos, 0, False),
            lax.ppermute(lax.dynamic_index_in_dim(qkv_line, 1 - x_pos, 0, False), "x", SWAP),
        )
    else:
        qkv_line = scatter_x(qkv_line).astype(bf16)
        qkv_line = (qkv_line, jnp.zeros_like(qkv_line))
    d_proj = to_tokens(d_raw, 3 * HEAD_DIM)
    out_part = own_grad(
        d_resid_h, (attn_parts, attn_parts), (d_proj, qkv_line[1])
    )
    far_n = project_grad_half(
        d_proj, 1, qkv_b, (out_part,)
    )
    out_part = lax.psum_scatter(out_part, "z", scatter_dimension=1, tiled=True)
    near_n = project_grad_half(d_proj, 0, qkv_b, (far_n[0],))
    d_normed, _ = scatter_halves(near_n, far_n)
    (input_grad,) = row_call(
        input_grad_kernel,
        d_normed,
        (block_in, d_resid),
        norm_gains[0],
        (bf16,),
    )
    small = sum_all(stack_rows(gain_first, gain_second, gain_full, router_rows))

    gains_grad = small[:4]
    router_grad = small[4:].T

    qkv_heads = lax.all_to_all(
        add_rows(*qkv_line, (near_n[0],)), "z", 0, 0, tiled=True
    )
    qkv_part = (
        qkv_heads.reshape(z_count, out_block, 3, HEAD_DIM)
        .transpose(2, 1, 0, 3)
        .reshape(3, out_block, head_cols)
        .astype(f32)
    )
    def own_block(a):
        return scatter_x(jnp.moveaxis(a.reshape(a.shape[0], x_count, out_block, -1), 1, 0))

    return (
        block_out,
        input_grad,
        qkv_part,
        jnp.moveaxis(own_block(out_part), 0, 1).reshape(out_block, head_cols),
        gains_grad,
        router_grad,
        gate_up_sum.astype(f32).reshape(2, experts, out_block, hidden_cols),
        own_block(down_part),
    )


def solution(mesh):
    ctx_count = mesh.shape["ctx"]

    def run(*args):
        heads = args[5].shape[2] // HEAD_DIM
        z_count = heads // mesh.shape["wt"]
        x_count = ctx_count // z_count
        grid = Mesh(mesh.devices.reshape(z_count, x_count, 2, 2), ("z", "x", "y", "c"))
        ctx, wt = ("z", "x"), ("y", "c")
        return jax.shard_map(
            functools.partial(local, z_count, x_count),
            mesh=grid,
            in_specs=(
                P(ctx + wt, None),
                P(ctx + wt, None),
                P(),
                P(),
                P(ctx, None),
                P(None, None, wt),
                P(None, wt),
                P(),
                P(),
                P(None, None, None, wt),
                P(None, None, wt),
            ),
            out_specs=(
                P(ctx + wt, None),
                P(ctx + wt, None),
                P(None, ctx, wt),
                P(ctx, wt),
                P(),
                P(),
                P(None, None, ctx, wt),
                P(None, ctx, wt),
            ),
            check_vma=False,
        )(*args)

    return run
```

```python
import functools
import math

import jax
import jax.numpy as jnp
from jax import lax
from jax.experimental import pallas as pl
from jax.experimental.pallas import tpu as pltpu
from jax.sharding import Mesh
from jax.sharding import PartitionSpec as P

HEAD_DIM = 128
LOG2E = math.log2(math.e)

norm_eps = 1e-05
f32 = jnp.float32
bf16 = jnp.bfloat16

SWAP = [(0, 1), (1, 0)]


def cost(us):
    return pl.CostEstimate(flops=int(us * 1e9), bytes_accessed=1 << 20, transcendentals=0)
DOT_NT = (((1,), (1,)), ((), ()))
DOT_NN = (((1,), (0,)), ((), ()))


def attend_kernel(groups, chunk, score_scale, q_ref, tok_q_ref, start_q_ref, *refs):
    key_refs = refs[: 3 * groups]
    o_ref, lse_ref = refs[-groups - 2 : -groups]
    vt_refs = refs[-groups:]
    rows = q_ref.shape[0]

    @pl.when(pl.program_id(0) == 0)
    def _():
        for g in range(groups):
            v_ref, vt_ref = key_refs[3 * g + 1], vt_refs[g]

            def turn(j, carry):
                r = pl.ds(pl.multiple_of(j * chunk, chunk), chunk)
                vt_ref[:, r] = v_ref[r, :].T
                return carry

            lax.fori_loop(0, v_ref.shape[0] // chunk, turn, 0)

    queries = q_ref[...]
    tok_q = tok_q_ref[...]
    start_q = start_q_ref[...]
    state = (
        jnp.full((1, rows), -1e30, f32),
        jnp.zeros((1, rows), f32),
        jnp.zeros((queries.shape[1], rows), f32),
    )
    for g in range(groups):
        k_ref, _, tok_k_ref = key_refs[3 * g : 3 * g + 3]
        vt_ref = vt_refs[g]

        def step(j, carry):
            run_max, run_sum, acc = carry
            r = pl.ds(pl.multiple_of(j * chunk, chunk), chunk)
            s = lax.dot_general(k_ref[r, :], queries, DOT_NT, preferred_element_type=f32)
            tok_k = tok_k_ref[r, :]
            s = jnp.where((tok_k <= tok_q) & (tok_k >= start_q), s * score_scale, -1e30)
            new_max = jnp.maximum(run_max, jnp.max(s, axis=0, keepdims=True))
            p = jnp.exp2(s - new_max)
            shrink = jnp.exp2(run_max - new_max)
            run_sum = run_sum * shrink + jnp.sum(p, axis=0, keepdims=True)
            acc = acc * shrink + lax.dot_general(
                vt_ref[:, r], p.astype(bf16), DOT_NN, preferred_element_type=f32
            )
            return new_max, run_sum, acc

        steps = k_ref.shape[0] // chunk
        state = lax.fori_loop(0, steps, step, state, unroll=steps <= 4)
    run_max, run_sum, acc = state
    o_ref[...] = (acc / run_sum).T
    lse_ref[...] = run_max + jnp.log2(run_sum)


def attend(queries, tok_q, start_q, key_groups, earlier=()):
    rows = queries.shape[0]
    block = min(1024, rows)
    chunk = 1024
    row = pl.BlockSpec((1, block), lambda i: (0, i))
    in_specs = [pl.BlockSpec((block, HEAD_DIM), lambda i: (i, 0)), row, row]
    operands = [queries, tok_q, start_q]
    scratch = []
    keys = 0
    for group in key_groups:
        count = group[0].shape[0]
        keys += count
        in_specs += [pl.BlockSpec(a.shape, lambda i: (0, 0)) for a in group]
        operands += group
        scratch.append(pltpu.VMEM((HEAD_DIM, count), bf16))
    in_specs += [pl.BlockSpec(memory_space=pl.ANY)] * len(earlier)
    operands += earlier
    return pl.pallas_call(
        functools.partial(
            attend_kernel, len(key_groups), chunk, LOG2E / math.sqrt(HEAD_DIM)
        ),
        grid=(rows // block,),
        in_specs=in_specs,
        out_specs=[pl.BlockSpec((block, HEAD_DIM), lambda i: (i, 0)), row],
        out_shape=[
            jax.ShapeDtypeStruct((rows, HEAD_DIM), f32),
            jax.ShapeDtypeStruct((1, rows), f32),
        ],
        scratch_shapes=scratch,
        compiler_params=params(48),
        cost_estimate=cost(19),
        name="attend",
    )(*operands)


def attend_grad_kernel(
    chunk,
    score_scale,
    grad_scale,
    q_ref,
    do_ref,
    lse_ref,
    delta_ref,
    tok_q_ref,
    start_q_ref,
    dq_in_ref,
    k_ref,
    v_ref,
    tok_k_ref,
    *refs,
):
    dq_ref, dk_ref, dv_ref, inner_q_ref, inner_k_ref, kt_ref, dk_acc, dv_acc = refs[-8:]

    def row_sums(a):
        ones = jnp.ones((8, a.shape[1]), f32)
        return lax.dot_general(
            ones, a, DOT_NT, precision=lax.Precision.HIGHEST, preferred_element_type=f32
        )[:1]

    steps = k_ref.shape[0] // chunk

    @pl.when(pl.program_id(0) == 0)
    def _():
        dk_acc[...] = jnp.zeros_like(dk_acc)
        dv_acc[...] = jnp.zeros_like(dv_acc)

        def turn(j, carry):
            r = pl.ds(pl.multiple_of(j * chunk, chunk), chunk)
            kt_ref[:, r] = k_ref[r, :].T
            return carry

        lax.fori_loop(0, steps, turn, 0)

    queries = q_ref[...]
    d_out = do_ref[...]
    tok_q = tok_q_ref[...]
    start_q = start_q_ref[...]
    lse = lse_ref[...]
    delta = delta_ref[...]

    def step(j, dq_t):
        r = pl.ds(pl.multiple_of(j * chunk, chunk), chunk)
        s = lax.dot_general(k_ref[r, :], queries, DOT_NT, preferred_element_type=f32)
        tok_k = tok_k_ref[r, :]
        allowed = (tok_k <= tok_q) & (tok_k >= start_q)
        p = jnp.exp2(jnp.where(allowed, s * score_scale - lse, -1e30))
        dp = lax.dot_general(v_ref[r, :], d_out, DOT_NT, preferred_element_type=f32)
        ds = (p * (dp - delta)).astype(bf16)
        dv_acc[r, :] += lax.dot_general(
            p.astype(bf16), d_out, DOT_NN, preferred_element_type=f32
        )
        dk_acc[r, :] += lax.dot_general(ds, queries, DOT_NN, preferred_element_type=f32)
        return dq_t + lax.dot_general(kt_ref[:, r], ds, DOT_NN, preferred_element_type=f32)

    dq_t = lax.fori_loop(
        0,
        steps,
        step,
        jnp.zeros((queries.shape[1], queries.shape[0]), f32),
        unroll=steps <= 4,
    )
    d_query = dq_in_ref[...] + (dq_t * grad_scale).T
    dq_ref[...] = d_query
    inner_q_ref[...] = row_sums(d_query * queries.astype(f32))

    @pl.when(pl.program_id(0) == pl.num_programs(0) - 1)
    def _():
        d_key = dk_acc[...] * grad_scale
        dk_ref[...] = d_key.astype(dk_ref.dtype)
        inner_k_ref[...] = row_sums(d_key * k_ref[...].astype(f32))
        dv_ref[...] = dv_acc[...].astype(dv_ref.dtype)


def attend_grad(
    queries, d_out, lse, delta, tok_q, start_q, dq_in, key_group, out_type, earlier=()
):
    rows = queries.shape[0]
    keys = key_group[0].shape[0]
    block = min(1024, rows)
    chunk = 1024
    row = pl.BlockSpec((1, block), lambda i: (0, i))
    head = pl.BlockSpec((block, HEAD_DIM), lambda i: (i, 0))
    whole = pl.BlockSpec((keys, HEAD_DIM), lambda i: (0, 0))
    return pl.pallas_call(
        functools.partial(
            attend_grad_kernel,
            chunk,
            LOG2E / math.sqrt(HEAD_DIM),
            1.0 / math.sqrt(HEAD_DIM),
        ),
        grid=(rows // block,),
        in_specs=[
            head,
            head,
            row,
            row,
            row,
            row,
            head,
            whole,
            whole,
            pl.BlockSpec((keys, 1), lambda i: (0, 0)),
        ]
        + [pl.BlockSpec(memory_space=pl.ANY)] * len(earlier),
        out_specs=[head, whole, whole, row, pl.BlockSpec((1, keys), lambda i: (0, 0))],
        out_shape=[
            jax.ShapeDtypeStruct((rows, HEAD_DIM), f32),
            jax.ShapeDtypeStruct((keys, HEAD_DIM), out_type),
            jax.ShapeDtypeStruct((keys, HEAD_DIM), out_type),
            jax.ShapeDtypeStruct((1, rows), f32),
            jax.ShapeDtypeStruct((1, keys), f32),
        ],
        scratch_shapes=[
            pltpu.VMEM((HEAD_DIM, keys), bf16),
            pltpu.VMEM((keys, HEAD_DIM), f32),
            pltpu.VMEM((keys, HEAD_DIM), f32),
        ],
        compiler_params=params(48),
        cost_estimate=cost(0.5),
        name="attend_grad",
    )(queries, d_out, lse, delta, tok_q, start_q, dq_in, *key_group, *earlier)


def pack_kernel(raw0_ref, raw1_ref, inv_ref, cos_ref, sin_ref, gain_ref, q_ref, k_ref):
    half = raw0_ref.shape[1]
    cos_tab = jnp.concatenate([cos_ref[...]] * 2, axis=1)
    sin_tab = jnp.concatenate([-sin_ref[...], sin_ref[...]], axis=1)
    for i, raw_ref in enumerate((raw0_ref, raw1_ref)):
        r = slice(i * half, (i + 1) * half)
        for j in range(2):
            u = raw_ref[j] * inv_ref[r, j : j + 1] * gain_ref[j : j + 1, :]
            turned = u * cos_tab[r, :] + pltpu.roll(u, HEAD_DIM // 2, 1) * sin_tab[r, :]
            (q_ref, k_ref)[j][0, r, :] = turned.astype(bf16)


def pack_heads(raw0, raw1, inv, cos_tab, sin_tab, gains):
    half = raw0.shape[1]
    rows = 2 * half
    heads = raw0.shape[2] // HEAD_DIM
    raw = pl.BlockSpec((2, half, HEAD_DIM), lambda h: (0, 0, h))
    head = pl.BlockSpec((1, rows, HEAD_DIM), lambda h: (h, 0, 0))
    table = pl.BlockSpec((rows, HEAD_DIM // 2), lambda h: (0, 0))
    return pl.pallas_call(
        pack_kernel,
        grid=(heads,),
        in_specs=[
            raw,
            raw,
            pl.BlockSpec((rows, 2), lambda h: (0, 0)),
            table,
            table,
            pl.BlockSpec((2, HEAD_DIM), lambda h: (0, h)),
        ],
        out_specs=[head, head],
        out_shape=[jax.ShapeDtypeStruct((heads, rows, HEAD_DIM), bf16)] * 2,
        cost_estimate=cost(4.7),
        name="pack_heads",
    )(raw0, raw1, inv, cos_tab, sin_tab, gains)


def raw_grad_kernel(
    dq_ref,
    dk_ref,
    dk_far_ref,
    dv_ref,
    dv_far_ref,
    q_ref,
    k_ref,
    inv_ref,
    inner_ref,
    cos_ref,
    sin_ref,
    gain_ref,
    *refs,
):
    out_ref, sum_ref = refs[-2:]

    @pl.when(pl.program_id(0) == 0)
    def _():
        sum_ref[...] = jnp.zeros_like(sum_ref)

    cos_tab = jnp.concatenate([cos_ref[...]] * 2, axis=1)
    sin_tab = jnp.concatenate([-sin_ref[...], sin_ref[...]], axis=1)
    block = inv_ref.shape[1]
    coef = jnp.concatenate([inv_ref[...], inner_ref[...], jnp.zeros((4, block), f32)]).T

    def turn_back(u):
        return u * cos_tab - pltpu.roll(u, HEAD_DIM // 2, 1) * sin_tab

    d_key = dk_ref[...] + dk_far_ref[...].astype(f32)
    for j, (grad, rows_ref) in enumerate(((dq_ref[...], q_ref), (d_key, k_ref))):
        gain = gain_ref[j : j + 1, :]
        cols = slice(j * HEAD_DIM, (j + 1) * HEAD_DIM)
        d_norm = turn_back(grad)
        hat = turn_back(rows_ref[...].astype(f32)) / gain
        sum_ref[j : j + 1, :] += jnp.sum(d_norm * hat, axis=0, keepdims=True)
        inv = coef[:, j : j + 1]
        inner = coef[:, 2 + j : 3 + j]
        out_ref[:, cols] = (inv * (d_norm * gain - hat * inner)).astype(bf16)
    out_ref[:, 2 * HEAD_DIM :] = (dv_ref[...] + dv_far_ref[...].astype(f32)).astype(bf16)


def raw_grad(d_query, d_key, d_value, queries, keys, inv, inner, cosine, sine, gains, earlier):
    rows = queries.shape[0]
    block = min(512, rows)

    def wide(cols):
        return pl.BlockSpec((block, cols), lambda i: (i, 0))

    whole = pl.BlockSpec((2, HEAD_DIM), lambda i: (0, 0))
    return pl.pallas_call(
        raw_grad_kernel,
        grid=(rows // block,),
        in_specs=[
            *[wide(HEAD_DIM)] * 7,
            pl.BlockSpec((2, block), lambda i: (0, i)),
            pl.BlockSpec((2, block), lambda i: (0, i)),
            wide(HEAD_DIM // 2),
            wide(HEAD_DIM // 2),
            whole,
            pl.BlockSpec(memory_space=pl.ANY),
        ],
        out_specs=[wide(3 * HEAD_DIM), whole],
        out_shape=[
            jax.ShapeDtypeStruct((rows, 3 * HEAD_DIM), bf16),
            jax.ShapeDtypeStruct((2, HEAD_DIM), f32),
        ],
        cost_estimate=cost(6),
        name="raw_grad",
    )(d_query, *d_key, *d_value, queries, keys, inv, inner, cosine, sine, gains, earlier)


def weight_grad_kernel(experts, out_block, at_ref, *refs):
    wide, far, narrow, compact = refs[:2], refs[2:4], refs[4:6], refs[6:8]
    out_ref, wide_t, tall = refs[-3:]
    half = wide[0].shape[0]
    blocks = far[0].shape[1] // out_block

    @pl.when(pl.program_id(0) == 0)
    def _():
        for z in range(blocks):
            rows = slice(z * out_block, (z + 1) * out_block)
            cols = (2 * z + at_ref[0]) * out_block
            cols = pl.ds(pl.multiple_of(cols, out_block), out_block)
            for i in range(2):
                wide_t[rows, i * half : (i + 1) * half] = wide[i][:, cols].T
                wide_t[rows, (2 + i) * half : (3 + i) * half] = far[i][:, rows].T

    e = lax.rem(pl.program_id(0), experts) if experts else None
    for i in range(2):
        tall[i * half : (i + 1) * half, :] = narrow[i][0]
        there = slice((2 + i) * half, (3 + i) * half)
        if not experts:
            tall[there, :] = compact[i][0]
            continue
        routes = refs[8][i * half : (i + 1) * half, :]
        block = jnp.zeros((half, tall.shape[1]), f32)
        for slot in range(routes.shape[1]):
            block = jnp.where(
                routes[:, slot : slot + 1] == e, compact[i][0, slot].astype(f32), block
            )
        tall[there, :] = block.astype(bf16)
    out_ref[0] = jnp.dot(wide_t[...], tall[...], preferred_element_type=f32).astype(bf16)


def weight_grad(wide_h, far_h, narrow, far_narrow, out_block, at, routes=None, experts=0, earlier=()):
    half, width = wide_h[0].shape
    out_width = far_h[0].shape[1]
    count, _, cols = narrow[0][0].shape

    def part(at):
        return pl.BlockSpec((1, half, cols), lambda j, x: (j, at, 0))

    specs = [part(at) for _, at in narrow]
    if experts:
        slots = routes.shape[1]
        specs += [pl.BlockSpec((1, slots, half, cols), lambda j, x: (j // experts, 0, 0, 0))] * 2
        specs.append(pl.BlockSpec(routes.shape, lambda j, x: (0, 0)))
        earlier = (routes, *earlier)
    else:
        specs += [part(at) for _, at in far_narrow]
    return pl.pallas_call(
        functools.partial(weight_grad_kernel, experts, out_block),
        grid_spec=pltpu.PrefetchScalarGridSpec(
            num_scalar_prefetch=1,
            grid=(count,),
            in_specs=[pl.BlockSpec(w.shape, lambda j, x: (0, 0)) for w in (*wide_h, *far_h)]
            + specs
            + waits(earlier[1:] if experts else earlier),
            out_specs=pl.BlockSpec((1, out_width, cols), lambda j, x: (j, 0, 0)),
            scratch_shapes=[
                pltpu.VMEM((out_width, 4 * half), bf16),
                pltpu.VMEM((4 * half, cols), bf16),
            ],
        ),
        out_shape=jax.ShapeDtypeStruct((count, out_width, cols), bf16),
        compiler_params=params(32),
        cost_estimate=cost(0.1),
        name="weight_grad",
    )(
        at.reshape(1),
        *wide_h,
        *far_h,
        *[a for a, _ in narrow],
        *[a for a, _ in far_narrow],
        *earlier,
    )


def waits(earlier):
    return [pl.BlockSpec(memory_space=pl.ANY)] * len(earlier)


def params(mib=16):
    return pltpu.CompilerParams(vmem_limit_bytes=mib * 1024 * 1024)


def project_kernel(x_ref, w_ref, *refs):
    raw_ref, sq_ref, v_ref = refs[-3:]
    kind, j = pl.program_id(0), pl.program_id(1)
    raw = jnp.dot(x_ref[...], w_ref[0], preferred_element_type=f32)

    @pl.when(kind < 2)
    def _():
        raw_ref[0] = raw
        ones = jnp.ones((8, raw.shape[1]), f32)
        square = lax.dot_general(
            ones, raw * raw, DOT_NT, precision=lax.Precision.HIGHEST, preferred_element_type=f32
        )
        sq_ref[0] = jnp.where(j == 0, square, sq_ref[0] + square)

    @pl.when(kind == 2)
    def _():
        for h in range(v_ref.shape[0]):
            v_ref[h] = raw[:, h * HEAD_DIM : (h + 1) * HEAD_DIM].astype(bf16)


def project(x, weights, earlier=()):
    count, width = x.shape
    cols = weights.shape[2]
    block = cols // 2
    heads = block // HEAD_DIM
    row = pl.BlockSpec((count, width), lambda k, j: (0, 0))

    def held(k, j):
        return jnp.minimum(k, 1), jnp.where(k == 2, 1, j)

    return pl.pallas_call(
        project_kernel,
        grid=(3, 2),
        in_specs=[row, pl.BlockSpec((1, width, block), lambda k, j: (k, 0, j))]
        + waits(earlier),
        out_specs=[
            pl.BlockSpec((1, count, block), lambda k, j: (held(k, j)[0], 0, held(k, j)[1])),
            pl.BlockSpec((1, 8, count), lambda k, j: (jnp.minimum(k, 1), 0, 0)),
            pl.BlockSpec((heads, count, HEAD_DIM), lambda k, j: (jnp.where(k == 2, j, 0), 0, 0)),
        ],
        out_shape=[
            jax.ShapeDtypeStruct((2, count, cols), f32),
            jax.ShapeDtypeStruct((2, 8, count), f32),
            jax.ShapeDtypeStruct((2 * heads, count, HEAD_DIM), bf16),
        ],
        compiler_params=params(32),
        cost_estimate=cost(0.1),
        name="project",
    )(x, weights, *earlier)


def attn_out_kernel(x_ref, w_ref, *refs):
    own_ref, other_ref, rows = refs[-3:]
    count = own_ref.shape[0]

    @pl.when(pl.program_id(0) == 0)
    def _():
        for h in range(x_ref.shape[0]):
            rows[:, h * HEAD_DIM : (h + 1) * HEAD_DIM] = x_ref[h]

    y = lax.dot_general(rows[...], w_ref[...], DOT_NT, preferred_element_type=f32).astype(bf16)
    own_ref[...] = y[:count]
    other_ref[...] = y[count:]


def attn_out_half(parts, half, weights, earlier=()):
    heads, count, _ = parts.shape
    count //= 2
    width, cols = weights.shape
    block = width // 4
    out = pl.BlockSpec((count // 2, block), lambda i: (0, i))
    return pl.pallas_call(
        attn_out_kernel,
        grid=(4,),
        in_specs=[
            pl.BlockSpec((heads, count, HEAD_DIM), lambda i: (0, half, 0)),
            pl.BlockSpec((block, cols), lambda i: (i, 0)),
        ]
        + waits(earlier),
        out_specs=[out, out],
        out_shape=[jax.ShapeDtypeStruct((count // 2, width), bf16)] * 2,
        scratch_shapes=[pltpu.VMEM((count, cols), bf16)],
        compiler_params=params(32),
        cost_estimate=cost(0.1),
        name="attn_out",
    )(parts, weights, *earlier)


def attn_out_grad_kernel(a_ref, w_ref, *refs):
    out_ref = refs[-1]
    y = jnp.dot(a_ref[...], w_ref[...], preferred_element_type=f32).astype(bf16)
    for h in range(out_ref.shape[0]):
        out_ref[h] = y[:, h * HEAD_DIM : (h + 1) * HEAD_DIM]


def attn_out_grad_half(grads, half, weights, into=None, earlier=()):
    count, width = grads.shape
    cols = weights.shape[1]
    heads = cols // HEAD_DIM
    block = cols // 2
    row = pl.BlockSpec((count, width), lambda j: (0, 0))
    into = () if into is None else (into,)
    return pl.pallas_call(
        attn_out_grad_kernel,
        grid=(2,),
        in_specs=[row, pl.BlockSpec((width, block), lambda j: (0, j))]
        + waits(into)
        + waits(earlier),
        out_specs=pl.BlockSpec((heads // 2, count, HEAD_DIM), lambda j: (j, half, 0)),
        out_shape=jax.ShapeDtypeStruct((heads, 2 * count, HEAD_DIM), bf16),
        input_output_aliases={2: 0} if into else {},
        compiler_params=params(16),
        cost_estimate=cost(0.1),
        name="attn_out_grad",
    )(grads, weights, *into, *earlier)


def project_grad_kernel(x_ref, w_ref, *refs):
    own_ref, other_ref, rows = refs[-3:]
    count = own_ref.shape[0]
    heads = x_ref.shape[0]
    cols = heads * HEAD_DIM

    @pl.when(pl.program_id(0) == 0)
    def _():
        for k in range(3):
            for h in range(heads):
                at = k * cols + h * HEAD_DIM
                rows[:, at : at + HEAD_DIM] = x_ref[h, :, k * HEAD_DIM : (k + 1) * HEAD_DIM]

    y = None
    for k in range(3):
        term = lax.dot_general(
            rows[:, k * cols : (k + 1) * cols], w_ref[k], DOT_NT, preferred_element_type=f32
        )
        y = term if y is None else y + term
    own_ref[...] = y[:count].astype(bf16)
    other_ref[...] = y[count:].astype(bf16)


def project_grad_half(parts, half, weights, earlier=()):
    heads, count, cols = parts.shape
    count //= 2
    width = weights.shape[1]
    block = width // 4
    part = pl.BlockSpec((count // 2, block), lambda i: (0, i))
    return pl.pallas_call(
        project_grad_kernel,
        grid=(4,),
        in_specs=[
            pl.BlockSpec((heads, count, cols), lambda i: (0, half, 0)),
            pl.BlockSpec((3, block, weights.shape[2]), lambda i: (0, i, 0)),
        ]
        + waits(earlier),
        out_specs=[part, part],
        out_shape=[
            jax.ShapeDtypeStruct((count // 2, width), bf16),
            jax.ShapeDtypeStruct((count // 2, width), bf16),
        ],
        scratch_shapes=[pltpu.VMEM((count, heads * cols), bf16)],
        compiler_params=params(24),
        cost_estimate=cost(6),
        name="project_grad",
    )(parts, weights, *earlier)


def qkv_grad_kernel(wide_ref, grad_ref, grad_other_ref, *refs):
    out_ref, out_other_ref, tall, wide_t = refs[-4:]
    rows, cols = grad_ref.shape

    @pl.when(pl.program_id(0) == 0)
    def _():
        tall[:, :cols] = grad_ref[...]
        block = rows // 16
        for i in range(16):
            tall[i * block : (i + 1) * block, cols:] = grad_other_ref[
                (i ^ 1) * block : ((i ^ 1) + 1) * block, :
            ]

    wide_t[...] = wide_ref[...].T
    out = jnp.dot(wide_t[...], tall[...], preferred_element_type=f32).astype(bf16)
    out_ref[...] = out[:, :cols]
    out_other_ref[...] = out[:, cols:]


def qkv_grad(wide, grad, grad_other, z_count, earlier=()):
    assert z_count == 4
    rows, width = wide.shape
    cols = grad.shape[1]
    block = min(256, width)
    whole = pl.BlockSpec(grad.shape, lambda i: (0, 0))
    out = pl.BlockSpec((block, cols), lambda i: (i, 0))
    return pl.pallas_call(
        qkv_grad_kernel,
        grid=(width // block,),
        in_specs=[pl.BlockSpec((rows, block), lambda i: (0, i)), whole, whole] + waits(earlier),
        out_specs=[out, out],
        scratch_shapes=[pltpu.VMEM((rows, 2 * cols), bf16), pltpu.VMEM((block, rows), bf16)],
        out_shape=[jax.ShapeDtypeStruct((width, cols), bf16)] * 2,
        compiler_params=params(40),
        cost_estimate=cost(10),
        name="qkv_grad",
    )(wide, grad, grad_other, *earlier)


def arrange(near, z_pos, earlier=()):
    rows, cols = near[0].shape
    z_count = len(near)

    def kernel(z_ref, *refs):
        for i in range(z_count):

            @pl.when(pl.program_id(0) == i)
            def _():
                refs[-1][...] = refs[i][...]

    return pl.pallas_call(
        kernel,
        grid_spec=pltpu.PrefetchScalarGridSpec(
            num_scalar_prefetch=1,
            grid=(z_count,),
            in_specs=[pl.BlockSpec((rows, cols), lambda i, z: (0, 0))] * z_count + waits(earlier),
            out_specs=pl.BlockSpec(
                (rows, cols), lambda i, z: (lax.rem(z[0] - i + z_count, z_count), 0)
            ),
        ),
        out_shape=jax.ShapeDtypeStruct((z_count * rows, cols), near[0].dtype),
        compiler_params=params(),
        cost_estimate=cost(0.1),
        name="arrange",
    )(z_pos.reshape(1), *near, *earlier)


def own_grad_kernel(w0_ref, w1_ref, n0_ref, n1_ref, *refs):
    out_ref, wide_t = refs[-2:]
    half = w0_ref.shape[0]

    @pl.when(pl.program_id(0) == 0)
    def _():
        wide_t[:, :half] = w0_ref[...].T
        wide_t[:, half:] = w1_ref[...].T

    tall = jnp.concatenate(
        [n0_ref[...].reshape(n0_ref.shape[-2:]), n1_ref[...].reshape(n1_ref.shape[-2:])]
    )
    out_ref[0] = jnp.dot(wide_t[...], tall, preferred_element_type=f32).astype(bf16)


def own_grad(wide_h, narrow_h, earlier=()):
    half, width = wide_h[0].shape
    count, rows, cols = narrow_h[0].shape
    narrow = [
        pl.BlockSpec((1, half, cols), lambda j, at=i * (rows // half - 1): (j, at, 0))
        for i in range(2)
    ]
    return pl.pallas_call(
        own_grad_kernel,
        grid=(count,),
        in_specs=[pl.BlockSpec((half, width), lambda j: (0, 0))] * 2 + narrow + waits(earlier),
        out_specs=pl.BlockSpec((1, width, cols), lambda j: (j, 0, 0)),
        out_shape=jax.ShapeDtypeStruct((count, width, cols), bf16),
        scratch_shapes=[pltpu.VMEM((width, 2 * half), bf16)],
        compiler_params=params(24),
        cost_estimate=cost(3.5),
        name="own_grad",
    )(*wide_h, *narrow_h, *earlier)


def join_kernel(a_ref, b_ref, *refs):
    n = a_ref.shape[0]
    refs[-1][:n] = a_ref[...]
    refs[-1][n:] = b_ref[...]


def join_rows(a, b, earlier=()):
    rows, width = a.shape
    block = width // 2
    part = pl.BlockSpec((rows, block), lambda j: (0, j))
    return pl.pallas_call(
        join_kernel,
        grid=(2,),
        in_specs=[part, part] + waits(earlier),
        out_specs=pl.BlockSpec((2 * rows, block), lambda j: (0, j)),
        out_shape=jax.ShapeDtypeStruct((2 * rows, width), a.dtype),
        compiler_params=params(),
        cost_estimate=cost(0.1),
        name="join_rows",
    )(a, b, *earlier)


def pass_kernel(in_ref, *refs):
    refs[-1][...] = in_ref[...]


def pass_rows(a, earlier):
    rows, width = a.shape
    spec = pl.BlockSpec((rows // 2, width), lambda j: (j, 0))
    if rows < 32:
        spec = pl.BlockSpec((rows, width // 2), lambda j: (0, j))
    return pl.pallas_call(
        pass_kernel,
        grid=(2,),
        in_specs=[spec] + waits(earlier),
        out_specs=spec,
        out_shape=jax.ShapeDtypeStruct(a.shape, a.dtype),
        compiler_params=params(),
        cost_estimate=cost(0.1),
        name="pass_rows",
    )(a, *earlier)


def round_kernel(in_ref, *refs):
    refs[-1][...] = in_ref[...].astype(bf16)


def round_weights(a, earlier=()):
    flat = a.reshape(-1, a.shape[-1])
    rows, cols = flat.shape
    block = min(rows, 1 << 20 >> (cols.bit_length() - 1))
    spec = pl.BlockSpec((block, cols), lambda i: (i, 0))
    out = pl.pallas_call(
        round_kernel,
        grid=(rows // block,),
        in_specs=[spec] + waits(earlier),
        out_specs=spec,
        out_shape=jax.ShapeDtypeStruct(flat.shape, bf16),
        compiler_params=params(),
        cost_estimate=cost(9),
        name="round_weights",
    )(flat, *earlier)
    return out.reshape(a.shape)


def add_kernel(a_ref, b_ref, *refs):
    refs[-1][...] = (a_ref[...].astype(f32) + b_ref[...].astype(f32)).astype(bf16)


def add_rows(a, b, earlier=()):
    spec = pl.BlockSpec((a.shape[0] // 2, *a.shape[1:]), lambda i: (i, 0, 0))
    return pl.pallas_call(
        add_kernel,
        grid=(2,),
        in_specs=[spec, spec] + waits(earlier),
        out_specs=spec,
        out_shape=jax.ShapeDtypeStruct(a.shape, bf16),
        compiler_params=params(),
        cost_estimate=cost(1),
        name="add_rows",
    )(a, b, *earlier)


def first_gain_kernel(z_ref, w_ref, grad_ref, gain_ref, out_ref):
    total = None
    for k in range(3):
        cols = slice(k * HEAD_DIM, (k + 1) * HEAD_DIM)
        term = w_ref[k].astype(f32) * grad_ref[:, cols].astype(f32)
        total = term if total is None else total + term
    ones = jnp.ones((8, HEAD_DIM), f32)
    total = lax.dot_general(
        ones, total, DOT_NT, precision=lax.Precision.HIGHEST, preferred_element_type=f32
    )
    out_ref[...] = total[:1] / gain_ref[...]


def first_gain(weights, grad, gain, z_pos):
    width = grad.shape[0]
    block = width // 4
    line = pl.BlockSpec((1, block), lambda i, z: (0, i))
    return pl.pallas_call(
        first_gain_kernel,
        grid_spec=pltpu.PrefetchScalarGridSpec(
            num_scalar_prefetch=1,
            grid=(4,),
            in_specs=[
                pl.BlockSpec((3, block, HEAD_DIM), lambda i, z: (0, i, z[0])),
                pl.BlockSpec((block, grad.shape[1]), lambda i, z: (i, 0)),
                line,
            ],
            out_specs=line,
        ),
        out_shape=jax.ShapeDtypeStruct((1, width), f32),
        compiler_params=params(),
        cost_estimate=cost(2),
        name="first_gain",
    )(z_pos.reshape(1), weights, grad, gain.reshape(1, width))


def stack_kernel(first_ref, second_ref, qk_ref, router_ref, out_ref):
    out_ref[0:1, :] = first_ref[...]
    out_ref[1:2, :] = second_ref[...]
    out_ref[2:4, :] = qk_ref[...]
    out_ref[4:8, :] = router_ref[...]


def stack_rows(*rows):
    return pl.pallas_call(
        stack_kernel,
        out_shape=jax.ShapeDtypeStruct((8, rows[0].shape[1]), f32),
        compiler_params=params(),
        cost_estimate=cost(0.1),
        name="stack_rows",
    )(*rows)


def stack_inner_kernel(q_ref, k_ref, k_far_ref, *refs):
    refs[-1][0:1, :] = q_ref[...]
    refs[-1][1:2, :] = k_ref[...] + k_far_ref[...]


def stack_inner(inner_q, inner_k, inner_k_far, earlier):
    return pl.pallas_call(
        stack_inner_kernel,
        in_specs=[pl.BlockSpec(memory_space=pltpu.VMEM)] * 3 + waits(earlier),
        out_shape=jax.ShapeDtypeStruct((2, inner_q.shape[1]), f32),
        compiler_params=params(),
        cost_estimate=cost(0.1),
        name="stack_inner",
    )(inner_q, inner_k, inner_k_far, *earlier)


def row_sum(refs):
    return refs[0][...].astype(f32) + refs[1][...].astype(f32) + refs[2][...].astype(f32)


def inv_rms(rows):
    return lax.rsqrt(jnp.mean(rows * rows, axis=-1, keepdims=True) + norm_eps)


def mix_kernel(near, near_got, far_got, in_ref, gain_ref, *refs):
    residual_ref, mixed_ref = refs[-2:]
    residual = in_ref[...].astype(f32) + row_sum((near, near_got, far_got))
    residual_ref[...] = residual
    mixed_ref[...] = (residual * inv_rms(residual) * gain_ref[...]).astype(bf16)


def gap_kernel(near, near_got, far_got, residual_ref, target_ref, *refs):
    out_ref, gap_ref, gap_b_ref = refs[-3:]
    out = residual_ref[...] + row_sum((near, near_got, far_got))
    out_ref[...] = out.astype(bf16)
    gap = out - target_ref[...].astype(f32)
    gap_ref[...] = gap
    gap_b_ref[...] = gap.astype(bf16)


def resid_grad_kernel(near, near_got, far_got, residual_ref, gap_ref, gain_ref, *refs):
    grad_ref, grad_b_ref, sum_ref = refs[-3:]
    d_mixed = row_sum((near, near_got, far_got))
    residual = residual_ref[...]
    inv = inv_rms(residual)
    hat = residual * inv
    grad = gap_ref[...] + norm_back(d_mixed, hat, inv, gain_ref[...])
    grad_ref[...] = grad
    grad_b_ref[...] = grad.astype(bf16)

    @pl.when(pl.program_id(0) == 0)
    def _():
        sum_ref[...] = jnp.zeros_like(sum_ref)

    sum_ref[...] += jnp.sum(d_mixed * hat, axis=0, keepdims=True)


def input_grad_kernel(near, near_got, far_got, in_ref, grad_ref, gain_ref, *refs):
    rows = in_ref[...].astype(f32)
    inv = inv_rms(rows)
    d_normed = row_sum((near, near_got, far_got))
    grad = grad_ref[...] + norm_back(d_normed, rows * inv, inv, gain_ref[...])
    refs[-1][...] = grad.astype(bf16)


def row_call(kernel, terms, rows, gain, outs, earlier=()):
    count, width = rows[0].shape
    block = min(32, count)
    spec = pl.BlockSpec((block, width), lambda i: (i, 0))
    line = pl.BlockSpec((1, width), lambda i: (0, 0))
    gains = [] if gain is None else [gain.reshape(1, width)]
    return pl.pallas_call(
        kernel,
        grid=(count // block,),
        in_specs=[spec] * (len(terms) + len(rows))
        + [line] * len(gains)
        + [pl.BlockSpec(memory_space=pl.ANY)] * len(earlier),
        out_specs=[line if o is None else spec for o in outs],
        out_shape=[
            jax.ShapeDtypeStruct((1, width) if o is None else (count, width), f32 if o is None else o)
            for o in outs
        ],
        compiler_params=params(16),
        cost_estimate=cost(0.1),
        name=kernel.__name__,
    )(*terms, *rows, *gains, *earlier)


def pick_kernel(cols, z_count, c_ref, r0_ref, r1_ref, *refs):
    out_ref = refs[-1]
    half = r0_ref.shape[0]
    out_ref[:half] = r0_ref[...]
    out_ref[half:] = r1_ref[...]


def pick_half(rows_h, at, earlier=()):
    half, width = rows_h[0].shape
    cols = width // 2
    block = cols // 2
    return pl.pallas_call(
        functools.partial(pick_kernel, cols, 2),
        grid_spec=pltpu.PrefetchScalarGridSpec(
            num_scalar_prefetch=1,
            grid=(2,),
            in_specs=[pl.BlockSpec((half, block), lambda j, c: (0, 2 * c[0] + j))] * 2
            + [pl.BlockSpec(memory_space=pl.ANY)] * len(earlier),
            out_specs=pl.BlockSpec((2 * half, block), lambda j, c: (0, j)),
        ),
        out_shape=jax.ShapeDtypeStruct((2 * half, cols), rows_h[0].dtype),
        cost_estimate=cost(0.1),
        name="pick_half",
    )(at.reshape(1), *rows_h, *earlier)


def token_places(seq_lengths, permutation):
    seq_ends = jnp.cumsum(seq_lengths)
    seq_starts = seq_ends - seq_lengths
    seq_id = jnp.sum((permutation[:, None] >= seq_ends[None, :]).astype(jnp.int32), axis=1)
    member = seq_id[:, None] == jnp.arange(seq_lengths.shape[0], dtype=jnp.int32)[None, :]
    return jnp.sum(jnp.where(member, seq_starts[None, :], 0), axis=1)


def near_first(a, axis, y_pos, c_pos):
    a = jnp.where(y_pos == 0, a, jnp.flip(a, axis))
    return jnp.where(c_pos == 0, a, jnp.flip(a, axis + 1))


def norm_back(grad_out, hat_rows, inv_rows, gain_row):
    grad_hat = grad_out * gain_row
    return inv_rows * (grad_hat - hat_rows * jnp.mean(grad_hat * hat_rows, axis=-1, keepdims=True))


def gather_near(rows):
    far = lax.ppermute(rows, "y", SWAP)
    return join_rows(rows, lax.ppermute(rows, "c", SWAP)), far


def gather_far(far, beside=(), earlier=()):
    if beside:
        far = pass_rows(far, beside)
    return join_rows(far, lax.ppermute(far, "c", SWAP), earlier)


def scatter_halves(near, far):
    sent = far[0].astype(f32) + lax.ppermute(far[1], "c", SWAP).astype(f32)
    sent = sent.astype(bf16)
    far_got = lax.ppermute(sent, "y", SWAP)
    near_got = lax.ppermute(near[1], "c", SWAP)
    return (near[0], near_got, far_got), sent


def sum_near(a):
    a = a + jnp.flip(lax.ppermute(a, "c", SWAP), -2)
    return a + jnp.flip(lax.ppermute(a, "y", SWAP), -3)


def sum_line(a, z_count):
    step = 1
    while step < z_count:
        a = a + lax.ppermute(a, "z", [(i, i ^ step) for i in range(z_count)])
        step *= 2
    return a


def local(
    z_count,
    x_count,
    block_in,
    target,
    seq_lengths,
    permutation,
    routes,
    attn_qkv,
    attn_out,
    norm_gains,
    router,
    gate_up,
    down,
):
    z_pos = lax.axis_index("z")
    x_pos = lax.axis_index("x")
    y_pos = lax.axis_index("y")
    c_pos = lax.axis_index("c")
    pair = x_count == 2
    local_rows, model_width = block_in.shape
    tok_rows = 4 * local_rows
    line_rows = z_count * tok_rows
    head_cols = attn_qkv.shape[2]
    hidden_cols = gate_up.shape[3]
    experts = gate_up.shape[1]
    wide_block = model_width // z_count
    out_block = wide_block // x_count
    wt_pos = y_pos * 2 + c_pos

    qkv_b = attn_qkv.astype(bf16)
    router_b = router.astype(bf16)

    def scatter_x(a):
        if pair:
            mine = lax.dynamic_index_in_dim(a, x_pos, 0, False)
            other = lax.dynamic_index_in_dim(a, 1 - x_pos, 0, False)
            return mine.astype(f32) + lax.ppermute(other.astype(bf16), "x", SWAP).astype(f32)
        return lax.psum_scatter(a.astype(bf16), "x", scatter_dimension=0).astype(f32)

    def of_parity(rows_h, at):
        return jnp.concatenate(
            [
                jnp.concatenate(
                    [
                        lax.dynamic_slice_in_dim(
                            r, z * wide_block + at * out_block, out_block, 1
                        )
                        for z in range(z_count)
                    ],
                    axis=1,
                )
                for r in rows_h
            ]
        )

    def far_wide(rows_h):
        return lax.ppermute(of_parity(rows_h, 1 - x_pos), "x", SWAP)

    def swap_x(parts):
        return [lax.ppermute(p, "x", SWAP) for p in parts]

    resid_in = block_in.astype(f32)
    inv_first = lax.rsqrt(jnp.mean(resid_in * resid_in, axis=-1, keepdims=True) + norm_eps)
    hat_first = resid_in * inv_first
    normed = (hat_first * norm_gains[0]).astype(bf16)
    normed_near, normed_far = gather_near(normed)
    normed_h = [normed_near, gather_far(normed_far)]

    start_all = token_places(seq_lengths, permutation)
    shape = (z_count, x_count, 2, 2, local_rows)
    tok_all = near_first(permutation.reshape(shape), 2, y_pos, c_pos)
    start_all = near_first(start_all.reshape(shape), 2, y_pos, c_pos)

    def of_x(a, at):
        return lax.dynamic_index_in_dim(a, at, 1, False).reshape(line_rows)

    tok_own = of_x(tok_all, x_pos)
    start_own = of_x(start_all, x_pos)
    tok_q = tok_own.reshape(1, line_rows)
    start_q = start_own.reshape(1, line_rows)
    half_dim = HEAD_DIM // 2
    frequency = jnp.exp(
        jnp.arange(half_dim, dtype=f32) * (-2.0 * math.log(10000.0) / HEAD_DIM)
    )
    angles = (tok_own - start_own).astype(f32)[:, None] * frequency[None, :]
    cosine, sine = jnp.cos(angles), jnp.sin(angles)

    raw0, square0, v0 = project(normed_h[0], qkv_b)
    raw1, square1, v1 = project(normed_h[1], qkv_b, (v0,))
    squares = jnp.concatenate([square0[:, 0], square1[:, 0]], axis=1)
    squares = sum_near(squares.reshape(2, 2, 2, local_rows)).reshape(2, tok_rows)
    inv_qk = lax.rsqrt(squares / model_width + norm_eps)
    inv_slots = jnp.where(
        (jnp.arange(z_count, dtype=jnp.int32) == z_pos)[:, None, None], inv_qk[None], 0.0
    )
    inv_line = sum_line(inv_slots, z_count)
    gain_qk = lax.dynamic_slice_in_dim(norm_gains[2:], wt_pos * head_cols, head_cols, 1)

    def to_heads_apart(parts, earlier=(), beside=None):
        near = [lax.dynamic_index_in_dim(parts, z_pos, 0, False)]
        for d in range(1, z_count):
            there = lax.dynamic_index_in_dim(parts, (z_pos + d) % z_count, 0, False)
            near.append(
                lax.ppermute(there, "z", [(i, (i + d) % z_count) for i in range(z_count)])
            )
        if beside is None:
            return arrange(near, z_pos, earlier)
        beside = beside(near[1])
        return arrange(near, z_pos, (*earlier, beside)), beside

    def to_heads(parts):
        return lax.all_to_all(parts, "z", 0, 0, tiled=True).reshape(line_rows, HEAD_DIM)

    def from_x(a):
        if pair:
            return lax.ppermute(a, "x", SWAP)
        return lax.all_gather(a, "x", axis=0)

    v_heads = jnp.concatenate([v0, v1], axis=1)
    q_heads, k_heads = pack_heads(
        raw0,
        raw1,
        inv_qk.T,
        lax.dynamic_slice_in_dim(cosine, z_pos * tok_rows, tok_rows),
        lax.dynamic_slice_in_dim(sine, z_pos * tok_rows, tok_rows),
        gain_qk,
    )
    values = pass_rows(to_heads(v_heads), (k_heads,))
    values_far = from_x(values)
    keys = to_heads_apart(k_heads, (values_far,))
    out_b = attn_out.astype(bf16)
    keys_far = from_x(keys)
    queries = to_heads_apart(q_heads)
    tok_col = tok_own.reshape(line_rows, 1)
    if pair:
        tok_far = of_x(tok_all, 1 - x_pos).reshape(line_rows, 1)
        groups = [(keys_far, values_far, tok_far), (keys, values, tok_col)]
        key_groups = groups[::-1]
    else:
        tok_x = jnp.moveaxis(tok_all, 1, 0).reshape(x_count, line_rows, 1)
        groups = [(keys_far[i], values_far[i], tok_x[i]) for i in range(x_count)]
        key_groups = [
            (
                keys_far.reshape(-1, HEAD_DIM),
                values_far.reshape(-1, HEAD_DIM),
                tok_x.reshape(-1, 1),
            )
        ]
    attn_f, row_lse = attend(
        queries, tok_q, start_q, key_groups
    )

    def to_tokens(rows, cols):
        parts = lax.all_to_all(
            rows.reshape(z_count, tok_rows, cols), "z", 0, 0, tiled=True
        )
        return parts

    attn_parts = to_tokens(attn_f.astype(bf16), HEAD_DIM)
    normed_pick = pick_half(normed_h, c_pos, (attn_parts,))
    attn_far = attn_out_half(attn_parts, 1, out_b)
    attn_near = attn_out_half(attn_parts, 0, out_b)
    attn_y, attn_sent = scatter_halves(attn_near, attn_far)
    normed_line = lax.all_gather(normed_pick, "z", axis=0, tiled=True)
    gu_b = round_weights(gate_up, (attn_sent,))
    residual, mixed_rows = row_call(
        mix_kernel,
        attn_y,
        (block_in,),
        norm_gains[1],
        (f32, bf16),
        (gu_b, normed_pick),
    )
    down_b = round_weights(down, (mixed_rows,))
    mixed_near, mixed_far = gather_near(mixed_rows)

    def halves(a):
        return a[: a.shape[0] // 2], a[a.shape[0] // 2 :]

    route_rows = near_first(routes.reshape(2, 2, local_rows, -1), 0, y_pos, c_pos)
    route_rows = route_rows.reshape(tok_rows, -1)
    if pair:
        routes_far = lax.ppermute(route_rows.T.astype(f32), "x", SWAP).T.astype(jnp.int32)
    choose = jnp.sum(
        (route_rows[:, :, None] == jnp.arange(experts, dtype=jnp.int32)[None, None, :]).astype(f32),
        axis=1,
    )

    def expert_rows(mixed, choose):
        prob = jax.nn.softmax(jnp.dot(mixed, router_b, preferred_element_type=f32), axis=-1)
        gate_w = prob * choose
        gate_in, up_in = jnp.einsum("td,kedf->ketf", mixed, gu_b, preferred_element_type=f32)
        gate_sig = jax.nn.sigmoid(gate_in)
        hidden = (gate_w.T[:, :, None] * (gate_in * gate_sig) * up_in).astype(bf16)
        y = jnp.einsum("etf,edf->td", hidden, down_b, preferred_element_type=f32)
        return y.astype(bf16), hidden, (mixed, choose, prob, gate_w, gate_in, up_in)

    choose_h = halves(choose)
    near_y, hidden0, kept0 = expert_rows(mixed_near, choose_h[0])
    mixed_h = [mixed_near, gather_far(mixed_far, (down_b,), (near_y,))]
    mixed_far = [far_wide([m]) for m in mixed_h] if pair else [mixed_rows, mixed_rows]
    far_y, hidden1, kept1 = expert_rows(mixed_h[1], choose_h[1])
    hidden_h = [hidden0, hidden1]
    expert_y, _ = scatter_halves(halves(near_y), halves(far_y))
    block_out, cot_local, cot_b = row_call(
        gap_kernel, expert_y, (residual, target), None, (bf16, f32, bf16),
        (mixed_far[0],),
    )
    def expert_rows_back(cot, kept):
        mixed, choose, prob, gate_w, gate_in, up_in = kept
        d_hid = (
            jnp.einsum("td,edf->etf", cot, down_b, preferred_element_type=f32)
            .astype(bf16)
            .astype(f32)
        )
        gate_sig = jax.nn.sigmoid(gate_in)
        gate_act = gate_in * gate_sig
        d_gate_w = jnp.sum(d_hid * gate_act * up_in, axis=-1).T
        scaled = d_hid * gate_w.T[:, :, None]
        d_gate_in = scaled * up_in * gate_sig * (1.0 + gate_in * (1.0 - gate_sig))
        d_pre = jnp.stack([d_gate_in, scaled * gate_act]).astype(bf16)
        d_prob = d_gate_w * choose
        d_logit = (prob * (d_prob - jnp.sum(prob * d_prob, axis=-1, keepdims=True))).astype(bf16)
        d_mixed = (
            jnp.einsum("ketf,kedf->td", d_pre, gu_b, preferred_element_type=f32)
            + lax.dot_general(d_logit, router_b, DOT_NT, preferred_element_type=f32)
        ).astype(bf16)
        router_part = lax.dot_general(
            d_logit, mixed, (((0,), (0,)), ((), ())), preferred_element_type=f32
        )
        return d_mixed, d_pre, router_part

    cot_near, cot_far = gather_near(cot_b)
    near_d, d_pre0, router0 = expert_rows_back(cot_near, kept0)
    cot_h = [cot_near, gather_far(cot_far, (), (mixed_far[1], normed_line, near_d))]
    far_d, d_pre1, router1 = expert_rows_back(cot_h[1], kept1)
    router_rows = router0 + router1
    d_pre_h = [d_pre0, d_pre1]
    d_mixed, d_mixed_sent = scatter_halves(halves(near_d), halves(far_d))
    down_part = own_grad(cot_h, hidden_h, (d_mixed_sent,))

    def compact(a, taken):
        a = a.reshape(-1, experts, *a.shape[1:])
        taken = taken.T[:, None, :, None]
        parts = []
        for slot in range(taken.shape[0]):
            part = a[:, 0]
            for e in range(1, experts):
                part = jnp.where(taken[slot] == e, a[:, e], part)
            parts.append(part)
        return jnp.stack(parts, axis=1)

    def plain_part(wide_h, narrow, spec):
        return scatter_x(
            jnp.stack(
                [
                    jnp.einsum(spec, of_parity(wide_h, i), narrow, preferred_element_type=f32)
                    for i in range(x_count)
                ]
            )
        ).astype(bf16)

    d_pre_h = [d.reshape(2 * experts, -1, hidden_cols) for d in d_pre_h]
    if pair:
        d_pre_far = [
            lax.ppermute(compact(d, r), "x", SWAP) for d, r in zip(d_pre_h, (route_rows[: tok_rows // 2], route_rows[tok_rows // 2 :]))
        ]
    d_resid, d_resid_b, gain_second = row_call(
        resid_grad_kernel,
        d_mixed,
        (residual, cot_local),
        norm_gains[1],
        (f32, bf16, None),
        (down_part, d_pre_far[0]) if pair else (down_part,),
    )
    resid_near, resid_far = gather_near(d_resid_b)
    d_resid_h = [resid_near, gather_far(resid_far, (), (d_pre_far[1],) if pair else ())]
    d_attn = attn_out_grad_half(d_resid_h[0], 0, out_b)
    d_attn = attn_out_grad_half(d_resid_h[1], 1, out_b, d_attn)

    if pair:

        def gate_up_beside(piece):
            return weight_grad(
                mixed_h,
                mixed_far,
                [(d, 0) for d in d_pre_h],
                [(d, 0) for d in d_pre_far],
                out_block,
                x_pos,
                routes_far,
                experts,
                (piece,),
            )

        d_out, gate_up_part = to_heads_apart(d_attn, beside=gate_up_beside)
    else:
        d_out = to_heads(d_attn)
        gate_up_part = plain_part(mixed_h, jnp.concatenate(d_pre_h, axis=1), "td,ntf->ndf")
    delta = jnp.sum(d_out.astype(f32) * attn_f, axis=-1).reshape(1, line_rows)
    d_query = jnp.zeros((line_rows, HEAD_DIM), f32)
    down_part = lax.psum_scatter(down_part, "z", scatter_dimension=1, tiled=True)
    gate_up_sum = lax.psum_scatter(gate_up_part, "z", scatter_dimension=1, tiled=True)
    d_kv = []
    inner_k = []
    earlier = (gate_up_part,)
    for i, group in enumerate(groups):
        last = i == len(groups) - 1
        d_query, *d_group, inner_q, inner_k_part = attend_grad(
            queries,
            d_out,
            row_lse,
            delta,
            tok_q,
            start_q,
            d_query,
            group,
            f32 if pair and last else bf16,
            earlier,
        )
        d_kv.append(d_group)
        inner_k.append(inner_k_part)
        if i == 0:
            earlier = (down_part,)
    if pair:
        d_key, d_value = [
            (own, lax.ppermute(far, "x", SWAP)) for far, own in zip(*d_kv)
        ]
        inner = stack_inner(
            inner_q, inner_k[1], lax.ppermute(inner_k[0], "x", SWAP), (d_key[1], d_value[1])
        )
    else:
        d_key, d_value = [
            (
                lax.psum_scatter(jnp.stack(parts), "x", scatter_dimension=0).astype(f32),
                jnp.zeros((line_rows, HEAD_DIM), bf16),
            )
            for parts in zip(*d_kv)
        ]
        inner_k = lax.psum_scatter(jnp.stack(inner_k), "x", scatter_dimension=0)
        inner = jnp.concatenate([inner_q, inner_k])
    inner = sum_line(sum_near(inner.reshape(2, z_count, 2, 2, local_rows)), z_count)
    inner = inner.reshape(2, line_rows) / model_width
    inv_line = jnp.moveaxis(inv_line, 0, 1).reshape(2, line_rows)
    head_gain = lax.dynamic_slice_in_dim(gain_qk, z_pos * HEAD_DIM, HEAD_DIM, 1)
    d_raw, gain_sums = raw_grad(
        d_query,
        d_key,
        d_value,
        queries,
        keys,
        inv_line,
        inner,
        cosine,
        sine,
        head_gain,
        d_kv[-1][0],
    )
    gain_full = lax.dynamic_update_slice_in_dim(
        jnp.zeros((2, model_width), f32), gain_sums, (wt_pos * z_count + z_pos) * HEAD_DIM, 1
    )

    def sum_all(a):
        a = a + lax.ppermute(a, "c", SWAP)
        a = a + lax.ppermute(a, "y", SWAP)
        a = a + lax.ppermute(a, "x", SWAP) if pair else lax.psum(a, "x")
        a = pass_rows(a, (input_grad,))
        return sum_line(a, z_count)

    grad_mine, grad_other = qkv_grad(
        normed_line, d_raw, lax.ppermute(d_raw, "c", SWAP), z_count
    )
    grad_other = lax.ppermute(grad_other, "c", SWAP)
    qkv_full = jnp.where(
        c_pos == 0,
        jnp.stack([grad_mine, grad_other]),
        jnp.stack([grad_other, grad_mine]),
    ).reshape(z_count, x_count, out_block, 3 * HEAD_DIM)
    gain_first = first_gain(
        qkv_b, qkv_full.reshape(model_width, 3 * HEAD_DIM), norm_gains[0], z_pos
    )
    qkv_line = jnp.moveaxis(qkv_full, 1, 0)
    if pair:
        qkv_line = (
            lax.dynamic_index_in_dim(qkv_line, x_pos, 0, False),
            lax.ppermute(lax.dynamic_index_in_dim(qkv_line, 1 - x_pos, 0, False), "x", SWAP),
        )
    else:
        qkv_line = scatter_x(qkv_line).astype(bf16)
        qkv_line = (qkv_line, jnp.zeros_like(qkv_line))
    d_proj = to_tokens(d_raw, 3 * HEAD_DIM)
    out_part = own_grad(
        d_resid_h, (attn_parts, attn_parts), (d_proj, qkv_line[1])
    )
    far_n = project_grad_half(d_proj, 1, qkv_b, (out_part, gate_up_sum))
    out_part = lax.psum_scatter(out_part, "z", scatter_dimension=1, tiled=True)
    near_n = project_grad_half(d_proj, 0, qkv_b, (far_n[0],))
    d_normed, _ = scatter_halves(near_n, far_n)
    (input_grad,) = row_call(
        input_grad_kernel,
        d_normed,
        (block_in, d_resid),
        norm_gains[0],
        (bf16,),
    )
    small = sum_all(stack_rows(gain_first, gain_second, gain_full, router_rows))

    gains_grad = small[:4]
    router_grad = small[4:].T

    qkv_heads = lax.all_to_all(
        add_rows(*qkv_line, (near_n[0],)), "z", 0, 0, tiled=True
    )
    qkv_part = (
        qkv_heads.reshape(z_count, out_block, 3, HEAD_DIM)
        .transpose(2, 1, 0, 3)
        .reshape(3, out_block, head_cols)
        .astype(f32)
    )
    def own_block(a):
        return scatter_x(jnp.moveaxis(a.reshape(a.shape[0], x_count, out_block, -1), 1, 0))

    return (
        block_out,
        input_grad,
        qkv_part,
        jnp.moveaxis(own_block(out_part), 0, 1).reshape(out_block, head_cols),
        gains_grad,
        router_grad,
        gate_up_sum.astype(f32).reshape(2, experts, out_block, hidden_cols),
        own_block(down_part),
    )


def solution(mesh):
    ctx_count = mesh.shape["ctx"]

    def run(*args):
        heads = args[5].shape[2] // HEAD_DIM
        z_count = heads // mesh.shape["wt"]
        x_count = ctx_count // z_count
        grid = Mesh(mesh.devices.reshape(z_count, x_count, 2, 2), ("z", "x", "y", "c"))
        ctx, wt = ("z", "x"), ("y", "c")
        return jax.shard_map(
            functools.partial(local, z_count, x_count),
            mesh=grid,
            in_specs=(
                P(ctx + wt, None),
                P(ctx + wt, None),
                P(),
                P(),
                P(ctx, None),
                P(None, None, wt),
                P(None, wt),
                P(),
                P(),
                P(None, None, None, wt),
                P(None, None, wt),
            ),
            out_specs=(
                P(ctx + wt, None),
                P(ctx + wt, None),
                P(None, ctx, wt),
                P(ctx, wt),
                P(),
                P(),
                P(None, None, ctx, wt),
                P(None, ctx, wt),
            ),
            check_vma=False,
        )(*args)

    return run
```

```python
import functools
import math

import jax
import jax.numpy as jnp
from jax import lax
from jax.experimental import pallas as pl
from jax.experimental.pallas import tpu as pltpu
from jax.sharding import Mesh
from jax.sharding import PartitionSpec as P

HEAD_DIM = 128
LOG2E = math.log2(math.e)

norm_eps = 1e-05
f32 = jnp.float32
bf16 = jnp.bfloat16

SWAP = [(0, 1), (1, 0)]


def cost(us):
    return pl.CostEstimate(flops=int(us * 1e9), bytes_accessed=1 << 20, transcendentals=0)
DOT_NT = (((1,), (1,)), ((), ()))
DOT_NN = (((1,), (0,)), ((), ()))


def attend_kernel(groups, chunk, score_scale, q_ref, tok_q_ref, start_q_ref, *refs):
    key_refs = refs[: 3 * groups]
    o_ref, lse_ref = refs[-groups - 2 : -groups]
    vt_refs = refs[-groups:]
    rows = q_ref.shape[0]

    @pl.when(pl.program_id(0) == 0)
    def _():
        for g in range(groups):
            v_ref, vt_ref = key_refs[3 * g + 1], vt_refs[g]

            def turn(j, carry):
                r = pl.ds(pl.multiple_of(j * chunk, chunk), chunk)
                vt_ref[:, r] = v_ref[r, :].T
                return carry

            lax.fori_loop(0, v_ref.shape[0] // chunk, turn, 0)

    queries = q_ref[...]
    tok_q = tok_q_ref[...]
    start_q = start_q_ref[...]
    state = (
        jnp.full((1, rows), -1e30, f32),
        jnp.zeros((1, rows), f32),
        jnp.zeros((queries.shape[1], rows), f32),
    )
    for g in range(groups):
        k_ref, _, tok_k_ref = key_refs[3 * g : 3 * g + 3]
        vt_ref = vt_refs[g]

        def step(j, carry):
            run_max, run_sum, acc = carry
            r = pl.ds(pl.multiple_of(j * chunk, chunk), chunk)
            s = lax.dot_general(k_ref[r, :], queries, DOT_NT, preferred_element_type=f32)
            tok_k = tok_k_ref[r, :]
            s = jnp.where((tok_k <= tok_q) & (tok_k >= start_q), s * score_scale, -1e30)
            new_max = jnp.maximum(run_max, jnp.max(s, axis=0, keepdims=True))
            p = jnp.exp2(s - new_max)
            shrink = jnp.exp2(run_max - new_max)
            run_sum = run_sum * shrink + jnp.sum(p, axis=0, keepdims=True)
            acc = acc * shrink + lax.dot_general(
                vt_ref[:, r], p.astype(bf16), DOT_NN, preferred_element_type=f32
            )
            return new_max, run_sum, acc

        steps = k_ref.shape[0] // chunk
        state = lax.fori_loop(0, steps, step, state, unroll=steps <= 4)
    run_max, run_sum, acc = state
    o_ref[...] = (acc / run_sum).T
    lse_ref[...] = run_max + jnp.log2(run_sum)


def attend(queries, tok_q, start_q, key_groups, earlier=()):
    rows = queries.shape[0]
    block = min(1024, rows)
    chunk = 1024
    row = pl.BlockSpec((1, block), lambda i: (0, i))
    in_specs = [pl.BlockSpec((block, HEAD_DIM), lambda i: (i, 0)), row, row]
    operands = [queries, tok_q, start_q]
    scratch = []
    keys = 0
    for group in key_groups:
        count = group[0].shape[0]
        keys += count
        in_specs += [pl.BlockSpec(a.shape, lambda i: (0, 0)) for a in group]
        operands += group
        scratch.append(pltpu.VMEM((HEAD_DIM, count), bf16))
    in_specs += [pl.BlockSpec(memory_space=pl.ANY)] * len(earlier)
    operands += earlier
    return pl.pallas_call(
        functools.partial(
            attend_kernel, len(key_groups), chunk, LOG2E / math.sqrt(HEAD_DIM)
        ),
        grid=(rows // block,),
        in_specs=in_specs,
        out_specs=[pl.BlockSpec((block, HEAD_DIM), lambda i: (i, 0)), row],
        out_shape=[
            jax.ShapeDtypeStruct((rows, HEAD_DIM), f32),
            jax.ShapeDtypeStruct((1, rows), f32),
        ],
        scratch_shapes=scratch,
        compiler_params=params(48),
        cost_estimate=cost(19),
        name="attend",
    )(*operands)


def attend_grad_kernel(
    chunk,
    score_scale,
    grad_scale,
    q_ref,
    do_ref,
    lse_ref,
    delta_ref,
    tok_q_ref,
    start_q_ref,
    dq_in_ref,
    k_ref,
    v_ref,
    tok_k_ref,
    *refs,
):
    dq_ref, dk_ref, dv_ref, inner_q_ref, inner_k_ref, kt_ref, dk_acc, dv_acc = refs[-8:]

    def row_sums(a):
        ones = jnp.ones((8, a.shape[1]), f32)
        return lax.dot_general(
            ones, a, DOT_NT, precision=lax.Precision.HIGHEST, preferred_element_type=f32
        )[:1]

    steps = k_ref.shape[0] // chunk

    @pl.when(pl.program_id(0) == 0)
    def _():
        dk_acc[...] = jnp.zeros_like(dk_acc)
        dv_acc[...] = jnp.zeros_like(dv_acc)

        def turn(j, carry):
            r = pl.ds(pl.multiple_of(j * chunk, chunk), chunk)
            kt_ref[:, r] = k_ref[r, :].T
            return carry

        lax.fori_loop(0, steps, turn, 0)

    queries = q_ref[...]
    d_out = do_ref[...]
    tok_q = tok_q_ref[...]
    start_q = start_q_ref[...]
    lse = lse_ref[...]
    delta = delta_ref[...]

    def step(j, dq_t):
        r = pl.ds(pl.multiple_of(j * chunk, chunk), chunk)
        s = lax.dot_general(k_ref[r, :], queries, DOT_NT, preferred_element_type=f32)
        tok_k = tok_k_ref[r, :]
        allowed = (tok_k <= tok_q) & (tok_k >= start_q)
        p = jnp.exp2(jnp.where(allowed, s * score_scale - lse, -1e30))
        dp = lax.dot_general(v_ref[r, :], d_out, DOT_NT, preferred_element_type=f32)
        ds = (p * (dp - delta)).astype(bf16)
        dv_acc[r, :] += lax.dot_general(
            p.astype(bf16), d_out, DOT_NN, preferred_element_type=f32
        )
        dk_acc[r, :] += lax.dot_general(ds, queries, DOT_NN, preferred_element_type=f32)
        return dq_t + lax.dot_general(kt_ref[:, r], ds, DOT_NN, preferred_element_type=f32)

    dq_t = lax.fori_loop(
        0,
        steps,
        step,
        jnp.zeros((queries.shape[1], queries.shape[0]), f32),
        unroll=steps <= 4,
    )
    d_query = dq_in_ref[...] + (dq_t * grad_scale).T
    dq_ref[...] = d_query
    inner_q_ref[...] = row_sums(d_query * queries.astype(f32))

    @pl.when(pl.program_id(0) == pl.num_programs(0) - 1)
    def _():
        d_key = dk_acc[...] * grad_scale
        dk_ref[...] = d_key.astype(dk_ref.dtype)
        inner_k_ref[...] = row_sums(d_key * k_ref[...].astype(f32))
        dv_ref[...] = dv_acc[...].astype(dv_ref.dtype)


def attend_grad(
    queries, d_out, lse, delta, tok_q, start_q, dq_in, key_group, out_type, earlier=()
):
    rows = queries.shape[0]
    keys = key_group[0].shape[0]
    block = min(1024, rows)
    chunk = 1024
    row = pl.BlockSpec((1, block), lambda i: (0, i))
    head = pl.BlockSpec((block, HEAD_DIM), lambda i: (i, 0))
    whole = pl.BlockSpec((keys, HEAD_DIM), lambda i: (0, 0))
    return pl.pallas_call(
        functools.partial(
            attend_grad_kernel,
            chunk,
            LOG2E / math.sqrt(HEAD_DIM),
            1.0 / math.sqrt(HEAD_DIM),
        ),
        grid=(rows // block,),
        in_specs=[
            head,
            head,
            row,
            row,
            row,
            row,
            head,
            whole,
            whole,
            pl.BlockSpec((keys, 1), lambda i: (0, 0)),
        ]
        + [pl.BlockSpec(memory_space=pl.ANY)] * len(earlier),
        out_specs=[head, whole, whole, row, pl.BlockSpec((1, keys), lambda i: (0, 0))],
        out_shape=[
            jax.ShapeDtypeStruct((rows, HEAD_DIM), f32),
            jax.ShapeDtypeStruct((keys, HEAD_DIM), out_type),
            jax.ShapeDtypeStruct((keys, HEAD_DIM), out_type),
            jax.ShapeDtypeStruct((1, rows), f32),
            jax.ShapeDtypeStruct((1, keys), f32),
        ],
        scratch_shapes=[
            pltpu.VMEM((HEAD_DIM, keys), bf16),
            pltpu.VMEM((keys, HEAD_DIM), f32),
            pltpu.VMEM((keys, HEAD_DIM), f32),
        ],
        compiler_params=params(48),
        cost_estimate=cost(0.5),
        name="attend_grad",
    )(queries, d_out, lse, delta, tok_q, start_q, dq_in, *key_group, *earlier)


def pack_kernel(raw0_ref, raw1_ref, inv_ref, cos_ref, sin_ref, gain_ref, q_ref, k_ref):
    half = raw0_ref.shape[1]
    cos_tab = jnp.concatenate([cos_ref[...]] * 2, axis=1)
    sin_tab = jnp.concatenate([-sin_ref[...], sin_ref[...]], axis=1)
    for i, raw_ref in enumerate((raw0_ref, raw1_ref)):
        r = slice(i * half, (i + 1) * half)
        for j in range(2):
            u = raw_ref[j] * inv_ref[r, j : j + 1] * gain_ref[j : j + 1, :]
            turned = u * cos_tab[r, :] + pltpu.roll(u, HEAD_DIM // 2, 1) * sin_tab[r, :]
            (q_ref, k_ref)[j][0, r, :] = turned.astype(bf16)


def pack_heads(raw0, raw1, inv, cos_tab, sin_tab, gains):
    half = raw0.shape[1]
    rows = 2 * half
    heads = raw0.shape[2] // HEAD_DIM
    raw = pl.BlockSpec((2, half, HEAD_DIM), lambda h: (0, 0, h))
    head = pl.BlockSpec((1, rows, HEAD_DIM), lambda h: (h, 0, 0))
    table = pl.BlockSpec((rows, HEAD_DIM // 2), lambda h: (0, 0))
    return pl.pallas_call(
        pack_kernel,
        grid=(heads,),
        in_specs=[
            raw,
            raw,
            pl.BlockSpec((rows, 2), lambda h: (0, 0)),
            table,
            table,
            pl.BlockSpec((2, HEAD_DIM), lambda h: (0, h)),
        ],
        out_specs=[head, head],
        out_shape=[jax.ShapeDtypeStruct((heads, rows, HEAD_DIM), bf16)] * 2,
        cost_estimate=cost(4.7),
        name="pack_heads",
    )(raw0, raw1, inv, cos_tab, sin_tab, gains)


def raw_grad_kernel(
    dq_ref,
    dk_ref,
    dk_far_ref,
    dv_ref,
    dv_far_ref,
    q_ref,
    k_ref,
    inv_ref,
    inner_ref,
    cos_ref,
    sin_ref,
    gain_ref,
    *refs,
):
    out_ref, sum_ref = refs[-2:]

    @pl.when(pl.program_id(0) == 0)
    def _():
        sum_ref[...] = jnp.zeros_like(sum_ref)

    cos_tab = jnp.concatenate([cos_ref[...]] * 2, axis=1)
    sin_tab = jnp.concatenate([-sin_ref[...], sin_ref[...]], axis=1)
    block = inv_ref.shape[1]
    coef = jnp.concatenate([inv_ref[...], inner_ref[...], jnp.zeros((4, block), f32)]).T

    def turn_back(u):
        return u * cos_tab - pltpu.roll(u, HEAD_DIM // 2, 1) * sin_tab

    d_key = dk_ref[...] + dk_far_ref[...].astype(f32)
    for j, (grad, rows_ref) in enumerate(((dq_ref[...], q_ref), (d_key, k_ref))):
        gain = gain_ref[j : j + 1, :]
        cols = slice(j * HEAD_DIM, (j + 1) * HEAD_DIM)
        d_norm = turn_back(grad)
        hat = turn_back(rows_ref[...].astype(f32)) / gain
        sum_ref[j : j + 1, :] += jnp.sum(d_norm * hat, axis=0, keepdims=True)
        inv = coef[:, j : j + 1]
        inner = coef[:, 2 + j : 3 + j]
        out_ref[:, cols] = (inv * (d_norm * gain - hat * inner)).astype(bf16)
    out_ref[:, 2 * HEAD_DIM :] = (dv_ref[...] + dv_far_ref[...].astype(f32)).astype(bf16)


def raw_grad(d_query, d_key, d_value, queries, keys, inv, inner, cosine, sine, gains, earlier):
    rows = queries.shape[0]
    block = min(512, rows)

    def wide(cols):
        return pl.BlockSpec((block, cols), lambda i: (i, 0))

    whole = pl.BlockSpec((2, HEAD_DIM), lambda i: (0, 0))
    return pl.pallas_call(
        raw_grad_kernel,
        grid=(rows // block,),
        in_specs=[
            *[wide(HEAD_DIM)] * 7,
            pl.BlockSpec((2, block), lambda i: (0, i)),
            pl.BlockSpec((2, block), lambda i: (0, i)),
            wide(HEAD_DIM // 2),
            wide(HEAD_DIM // 2),
            whole,
            pl.BlockSpec(memory_space=pl.ANY),
        ],
        out_specs=[wide(3 * HEAD_DIM), whole],
        out_shape=[
            jax.ShapeDtypeStruct((rows, 3 * HEAD_DIM), bf16),
            jax.ShapeDtypeStruct((2, HEAD_DIM), f32),
        ],
        cost_estimate=cost(6),
        name="raw_grad",
    )(d_query, *d_key, *d_value, queries, keys, inv, inner, cosine, sine, gains, earlier)


def weight_grad_kernel(experts, out_block, at_ref, *refs):
    wide, far, narrow, compact = refs[:2], refs[2:4], refs[4:6], refs[6:8]
    out_ref, wide_t, tall = refs[-3:]
    half = wide[0].shape[0]
    blocks = far[0].shape[1] // out_block

    @pl.when(pl.program_id(0) == 0)
    def _():
        for z in range(blocks):
            rows = slice(z * out_block, (z + 1) * out_block)
            cols = (2 * z + at_ref[0]) * out_block
            cols = pl.ds(pl.multiple_of(cols, out_block), out_block)
            for i in range(2):
                wide_t[rows, i * half : (i + 1) * half] = wide[i][:, cols].T
                wide_t[rows, (2 + i) * half : (3 + i) * half] = far[i][:, rows].T

    e = lax.rem(pl.program_id(0), experts) if experts else None
    for i in range(2):
        tall[i * half : (i + 1) * half, :] = narrow[i][0]
        there = slice((2 + i) * half, (3 + i) * half)
        if not experts:
            tall[there, :] = compact[i][0]
            continue
        routes = refs[8][i * half : (i + 1) * half, :]
        block = jnp.zeros((half, tall.shape[1]), f32)
        for slot in range(routes.shape[1]):
            block = jnp.where(
                routes[:, slot : slot + 1] == e, compact[i][0, slot].astype(f32), block
            )
        tall[there, :] = block.astype(bf16)
    out_ref[0] = jnp.dot(wide_t[...], tall[...], preferred_element_type=f32).astype(bf16)


def weight_grad(wide_h, far_h, narrow, far_narrow, out_block, at, routes=None, experts=0, earlier=()):
    half, width = wide_h[0].shape
    out_width = far_h[0].shape[1]
    count, _, cols = narrow[0][0].shape

    def part(at):
        return pl.BlockSpec((1, half, cols), lambda j, x: (j, at, 0))

    specs = [part(at) for _, at in narrow]
    if experts:
        slots = routes.shape[1]
        specs += [pl.BlockSpec((1, slots, half, cols), lambda j, x: (j // experts, 0, 0, 0))] * 2
        specs.append(pl.BlockSpec(routes.shape, lambda j, x: (0, 0)))
        earlier = (routes, *earlier)
    else:
        specs += [part(at) for _, at in far_narrow]
    return pl.pallas_call(
        functools.partial(weight_grad_kernel, experts, out_block),
        grid_spec=pltpu.PrefetchScalarGridSpec(
            num_scalar_prefetch=1,
            grid=(count,),
            in_specs=[pl.BlockSpec(w.shape, lambda j, x: (0, 0)) for w in (*wide_h, *far_h)]
            + specs
            + waits(earlier[1:] if experts else earlier),
            out_specs=pl.BlockSpec((1, out_width, cols), lambda j, x: (j, 0, 0)),
            scratch_shapes=[
                pltpu.VMEM((out_width, 4 * half), bf16),
                pltpu.VMEM((4 * half, cols), bf16),
            ],
        ),
        out_shape=jax.ShapeDtypeStruct((count, out_width, cols), bf16),
        compiler_params=params(32),
        cost_estimate=cost(0.1),
        name="weight_grad",
    )(
        at.reshape(1),
        *wide_h,
        *far_h,
        *[a for a, _ in narrow],
        *[a for a, _ in far_narrow],
        *earlier,
    )


def waits(earlier):
    return [pl.BlockSpec(memory_space=pl.ANY)] * len(earlier)


def params(mib=16):
    return pltpu.CompilerParams(vmem_limit_bytes=mib * 1024 * 1024)


def project_kernel(x_ref, w_ref, *refs):
    raw_ref, sq_ref, v_ref = refs[-3:]
    kind, j = pl.program_id(0), pl.program_id(1)
    raw = jnp.dot(x_ref[...], w_ref[0], preferred_element_type=f32)

    @pl.when(kind < 2)
    def _():
        raw_ref[0] = raw
        ones = jnp.ones((8, raw.shape[1]), f32)
        square = lax.dot_general(
            ones, raw * raw, DOT_NT, precision=lax.Precision.HIGHEST, preferred_element_type=f32
        )
        sq_ref[0] = jnp.where(j == 0, square, sq_ref[0] + square)

    @pl.when(kind == 2)
    def _():
        for h in range(v_ref.shape[0]):
            v_ref[h] = raw[:, h * HEAD_DIM : (h + 1) * HEAD_DIM].astype(bf16)


def project(x, weights, earlier=()):
    count, width = x.shape
    cols = weights.shape[2]
    block = cols // 2
    heads = block // HEAD_DIM
    row = pl.BlockSpec((count, width), lambda k, j: (0, 0))

    def held(k, j):
        return jnp.minimum(k, 1), jnp.where(k == 2, 1, j)

    return pl.pallas_call(
        project_kernel,
        grid=(3, 2),
        in_specs=[row, pl.BlockSpec((1, width, block), lambda k, j: (k, 0, j))]
        + waits(earlier),
        out_specs=[
            pl.BlockSpec((1, count, block), lambda k, j: (held(k, j)[0], 0, held(k, j)[1])),
            pl.BlockSpec((1, 8, count), lambda k, j: (jnp.minimum(k, 1), 0, 0)),
            pl.BlockSpec((heads, count, HEAD_DIM), lambda k, j: (jnp.where(k == 2, j, 0), 0, 0)),
        ],
        out_shape=[
            jax.ShapeDtypeStruct((2, count, cols), f32),
            jax.ShapeDtypeStruct((2, 8, count), f32),
            jax.ShapeDtypeStruct((2 * heads, count, HEAD_DIM), bf16),
        ],
        compiler_params=params(32),
        cost_estimate=cost(0.1),
        name="project",
    )(x, weights, *earlier)


def attn_out_kernel(x_ref, w_ref, *refs):
    own_ref, other_ref, rows = refs[-3:]
    count = own_ref.shape[0]

    @pl.when(pl.program_id(0) == 0)
    def _():
        for h in range(x_ref.shape[0]):
            rows[:, h * HEAD_DIM : (h + 1) * HEAD_DIM] = x_ref[h]

    y = lax.dot_general(rows[...], w_ref[...], DOT_NT, preferred_element_type=f32).astype(bf16)
    own_ref[...] = y[:count]
    other_ref[...] = y[count:]


def attn_out_half(parts, half, weights, earlier=()):
    heads, count, _ = parts.shape
    count //= 2
    width, cols = weights.shape
    block = width // 4
    out = pl.BlockSpec((count // 2, block), lambda i: (0, i))
    return pl.pallas_call(
        attn_out_kernel,
        grid=(4,),
        in_specs=[
            pl.BlockSpec((heads, count, HEAD_DIM), lambda i: (0, half, 0)),
            pl.BlockSpec((block, cols), lambda i: (i, 0)),
        ]
        + waits(earlier),
        out_specs=[out, out],
        out_shape=[jax.ShapeDtypeStruct((count // 2, width), bf16)] * 2,
        scratch_shapes=[pltpu.VMEM((count, cols), bf16)],
        compiler_params=params(32),
        cost_estimate=cost(0.1),
        name="attn_out",
    )(parts, weights, *earlier)


def attn_out_grad_kernel(a_ref, w_ref, *refs):
    out_ref = refs[-1]
    y = jnp.dot(a_ref[...], w_ref[...], preferred_element_type=f32).astype(bf16)
    for h in range(out_ref.shape[0]):
        out_ref[h] = y[:, h * HEAD_DIM : (h + 1) * HEAD_DIM]


def attn_out_grad_half(grads, half, weights, into=None, earlier=()):
    count, width = grads.shape
    cols = weights.shape[1]
    heads = cols // HEAD_DIM
    block = cols // 2
    row = pl.BlockSpec((count, width), lambda j: (0, 0))
    into = () if into is None else (into,)
    return pl.pallas_call(
        attn_out_grad_kernel,
        grid=(2,),
        in_specs=[row, pl.BlockSpec((width, block), lambda j: (0, j))]
        + waits(into)
        + waits(earlier),
        out_specs=pl.BlockSpec((heads // 2, count, HEAD_DIM), lambda j: (j, half, 0)),
        out_shape=jax.ShapeDtypeStruct((heads, 2 * count, HEAD_DIM), bf16),
        input_output_aliases={2: 0} if into else {},
        compiler_params=params(16),
        cost_estimate=cost(0.1),
        name="attn_out_grad",
    )(grads, weights, *into, *earlier)


def project_grad_kernel(x_ref, w_ref, *refs):
    own_ref, other_ref, rows = refs[-3:]
    count = own_ref.shape[0]
    heads = x_ref.shape[0]
    cols = heads * HEAD_DIM

    @pl.when(pl.program_id(0) == 0)
    def _():
        for k in range(3):
            for h in range(heads):
                at = k * cols + h * HEAD_DIM
                rows[:, at : at + HEAD_DIM] = x_ref[h, :, k * HEAD_DIM : (k + 1) * HEAD_DIM]

    y = None
    for k in range(3):
        term = lax.dot_general(
            rows[:, k * cols : (k + 1) * cols], w_ref[k], DOT_NT, preferred_element_type=f32
        )
        y = term if y is None else y + term
    own_ref[...] = y[:count].astype(bf16)
    other_ref[...] = y[count:].astype(bf16)


def project_grad_half(parts, half, weights, earlier=()):
    heads, count, cols = parts.shape
    count //= 2
    width = weights.shape[1]
    block = width // 4
    part = pl.BlockSpec((count // 2, block), lambda i: (0, i))
    return pl.pallas_call(
        project_grad_kernel,
        grid=(4,),
        in_specs=[
            pl.BlockSpec((heads, count, cols), lambda i: (0, half, 0)),
            pl.BlockSpec((3, block, weights.shape[2]), lambda i: (0, i, 0)),
        ]
        + waits(earlier),
        out_specs=[part, part],
        out_shape=[
            jax.ShapeDtypeStruct((count // 2, width), bf16),
            jax.ShapeDtypeStruct((count // 2, width), bf16),
        ],
        scratch_shapes=[pltpu.VMEM((count, heads * cols), bf16)],
        compiler_params=params(24),
        cost_estimate=cost(6),
        name="project_grad",
    )(parts, weights, *earlier)


def qkv_grad_kernel(wide_ref, grad_ref, grad_other_ref, *refs):
    out_ref, out_other_ref, tall, wide_t = refs[-4:]
    rows, cols = grad_ref.shape

    @pl.when(pl.program_id(0) == 0)
    def _():
        tall[:, :cols] = grad_ref[...]
        block = rows // 16
        for i in range(16):
            tall[i * block : (i + 1) * block, cols:] = grad_other_ref[
                (i ^ 1) * block : ((i ^ 1) + 1) * block, :
            ]

    wide_t[...] = wide_ref[...].T
    out = jnp.dot(wide_t[...], tall[...], preferred_element_type=f32).astype(bf16)
    out_ref[...] = out[:, :cols]
    out_other_ref[...] = out[:, cols:]


def qkv_grad(wide, grad, grad_other, z_count, earlier=()):
    assert z_count == 4
    rows, width = wide.shape
    cols = grad.shape[1]
    block = min(256, width)
    whole = pl.BlockSpec(grad.shape, lambda i: (0, 0))
    out = pl.BlockSpec((block, cols), lambda i: (i, 0))
    return pl.pallas_call(
        qkv_grad_kernel,
        grid=(width // block,),
        in_specs=[pl.BlockSpec((rows, block), lambda i: (0, i)), whole, whole] + waits(earlier),
        out_specs=[out, out],
        scratch_shapes=[pltpu.VMEM((rows, 2 * cols), bf16), pltpu.VMEM((block, rows), bf16)],
        out_shape=[jax.ShapeDtypeStruct((width, cols), bf16)] * 2,
        compiler_params=params(40),
        cost_estimate=cost(10),
        name="qkv_grad",
    )(wide, grad, grad_other, *earlier)


def arrange(near, z_pos, earlier=()):
    rows, cols = near[0].shape
    z_count = len(near)

    def kernel(z_ref, *refs):
        for i in range(z_count):

            @pl.when(pl.program_id(0) == i)
            def _():
                refs[-1][...] = refs[i][...]

    return pl.pallas_call(
        kernel,
        grid_spec=pltpu.PrefetchScalarGridSpec(
            num_scalar_prefetch=1,
            grid=(z_count,),
            in_specs=[pl.BlockSpec((rows, cols), lambda i, z: (0, 0))] * z_count + waits(earlier),
            out_specs=pl.BlockSpec(
                (rows, cols), lambda i, z: (lax.rem(z[0] - i + z_count, z_count), 0)
            ),
        ),
        out_shape=jax.ShapeDtypeStruct((z_count * rows, cols), near[0].dtype),
        compiler_params=params(),
        cost_estimate=cost(0.1),
        name="arrange",
    )(z_pos.reshape(1), *near, *earlier)


def own_grad_kernel(w0_ref, w1_ref, n0_ref, n1_ref, *refs):
    out_ref, wide_t = refs[-2:]
    half = w0_ref.shape[0]

    @pl.when(pl.program_id(0) == 0)
    def _():
        wide_t[:, :half] = w0_ref[...].T
        wide_t[:, half:] = w1_ref[...].T

    tall = jnp.concatenate(
        [n0_ref[...].reshape(n0_ref.shape[-2:]), n1_ref[...].reshape(n1_ref.shape[-2:])]
    )
    out_ref[0] = jnp.dot(wide_t[...], tall, preferred_element_type=f32).astype(bf16)


def own_grad(wide_h, narrow_h, earlier=()):
    half, width = wide_h[0].shape
    count, rows, cols = narrow_h[0].shape
    narrow = [
        pl.BlockSpec((1, half, cols), lambda j, at=i * (rows // half - 1): (j, at, 0))
        for i in range(2)
    ]
    return pl.pallas_call(
        own_grad_kernel,
        grid=(count,),
        in_specs=[pl.BlockSpec((half, width), lambda j: (0, 0))] * 2 + narrow + waits(earlier),
        out_specs=pl.BlockSpec((1, width, cols), lambda j: (j, 0, 0)),
        out_shape=jax.ShapeDtypeStruct((count, width, cols), bf16),
        scratch_shapes=[pltpu.VMEM((width, 2 * half), bf16)],
        compiler_params=params(24),
        cost_estimate=cost(3.5),
        name="own_grad",
    )(*wide_h, *narrow_h, *earlier)


def join_kernel(a_ref, b_ref, *refs):
    n = a_ref.shape[0]
    refs[-1][:n] = a_ref[...]
    refs[-1][n:] = b_ref[...]


def join_rows(a, b, earlier=()):
    rows, width = a.shape
    block = width // 2
    part = pl.BlockSpec((rows, block), lambda j: (0, j))
    return pl.pallas_call(
        join_kernel,
        grid=(2,),
        in_specs=[part, part] + waits(earlier),
        out_specs=pl.BlockSpec((2 * rows, block), lambda j: (0, j)),
        out_shape=jax.ShapeDtypeStruct((2 * rows, width), a.dtype),
        compiler_params=params(),
        cost_estimate=cost(0.1),
        name="join_rows",
    )(a, b, *earlier)


def pass_kernel(in_ref, *refs):
    refs[-1][...] = in_ref[...]


def pass_rows(a, earlier):
    rows, width = a.shape
    spec = pl.BlockSpec((rows // 2, width), lambda j: (j, 0))
    if rows < 32:
        spec = pl.BlockSpec((rows, width // 2), lambda j: (0, j))
    return pl.pallas_call(
        pass_kernel,
        grid=(2,),
        in_specs=[spec] + waits(earlier),
        out_specs=spec,
        out_shape=jax.ShapeDtypeStruct(a.shape, a.dtype),
        compiler_params=params(),
        cost_estimate=cost(0.1),
        name="pass_rows",
    )(a, *earlier)


def round_kernel(in_ref, *refs):
    refs[-1][...] = in_ref[...].astype(bf16)


def round_weights(a, earlier=()):
    flat = a.reshape(-1, a.shape[-1])
    rows, cols = flat.shape
    block = min(rows, 1 << 20 >> (cols.bit_length() - 1))
    spec = pl.BlockSpec((block, cols), lambda i: (i, 0))
    out = pl.pallas_call(
        round_kernel,
        grid=(rows // block,),
        in_specs=[spec] + waits(earlier),
        out_specs=spec,
        out_shape=jax.ShapeDtypeStruct(flat.shape, bf16),
        compiler_params=params(),
        cost_estimate=cost(9),
        name="round_weights",
    )(flat, *earlier)
    return out.reshape(a.shape)


def add_kernel(a_ref, b_ref, *refs):
    refs[-1][...] = (a_ref[...].astype(f32) + b_ref[...].astype(f32)).astype(bf16)


def add_rows(a, b, earlier=()):
    spec = pl.BlockSpec((a.shape[0] // 2, *a.shape[1:]), lambda i: (i, 0, 0))
    return pl.pallas_call(
        add_kernel,
        grid=(2,),
        in_specs=[spec, spec] + waits(earlier),
        out_specs=spec,
        out_shape=jax.ShapeDtypeStruct(a.shape, bf16),
        compiler_params=params(),
        cost_estimate=cost(1),
        name="add_rows",
    )(a, b, *earlier)


def first_gain_kernel(z_ref, w_ref, grad_ref, gain_ref, out_ref):
    total = None
    for k in range(3):
        cols = slice(k * HEAD_DIM, (k + 1) * HEAD_DIM)
        term = w_ref[k].astype(f32) * grad_ref[:, cols].astype(f32)
        total = term if total is None else total + term
    ones = jnp.ones((8, HEAD_DIM), f32)
    total = lax.dot_general(
        ones, total, DOT_NT, precision=lax.Precision.HIGHEST, preferred_element_type=f32
    )
    out_ref[...] = total[:1] / gain_ref[...]


def first_gain(weights, grad, gain, z_pos):
    width = grad.shape[0]
    block = width // 4
    line = pl.BlockSpec((1, block), lambda i, z: (0, i))
    return pl.pallas_call(
        first_gain_kernel,
        grid_spec=pltpu.PrefetchScalarGridSpec(
            num_scalar_prefetch=1,
            grid=(4,),
            in_specs=[
                pl.BlockSpec((3, block, HEAD_DIM), lambda i, z: (0, i, z[0])),
                pl.BlockSpec((block, grad.shape[1]), lambda i, z: (i, 0)),
                line,
            ],
            out_specs=line,
        ),
        out_shape=jax.ShapeDtypeStruct((1, width), f32),
        compiler_params=params(),
        cost_estimate=cost(2),
        name="first_gain",
    )(z_pos.reshape(1), weights, grad, gain.reshape(1, width))


def stack_kernel(first_ref, second_ref, qk_ref, router_ref, out_ref):
    out_ref[0:1, :] = first_ref[...]
    out_ref[1:2, :] = second_ref[...]
    out_ref[2:4, :] = qk_ref[...]
    out_ref[4:8, :] = router_ref[...]


def stack_rows(*rows):
    return pl.pallas_call(
        stack_kernel,
        out_shape=jax.ShapeDtypeStruct((8, rows[0].shape[1]), f32),
        compiler_params=params(),
        cost_estimate=cost(0.1),
        name="stack_rows",
    )(*rows)


def stack_inner_kernel(q_ref, k_ref, k_far_ref, *refs):
    refs[-1][0:1, :] = q_ref[...]
    refs[-1][1:2, :] = k_ref[...] + k_far_ref[...]


def stack_inner(inner_q, inner_k, inner_k_far, earlier):
    return pl.pallas_call(
        stack_inner_kernel,
        in_specs=[pl.BlockSpec(memory_space=pltpu.VMEM)] * 3 + waits(earlier),
        out_shape=jax.ShapeDtypeStruct((2, inner_q.shape[1]), f32),
        compiler_params=params(),
        cost_estimate=cost(0.1),
        name="stack_inner",
    )(inner_q, inner_k, inner_k_far, *earlier)


def row_sum(refs):
    return refs[0][...].astype(f32) + refs[1][...].astype(f32) + refs[2][...].astype(f32)


def inv_rms(rows):
    return lax.rsqrt(jnp.mean(rows * rows, axis=-1, keepdims=True) + norm_eps)


def mix_kernel(near, near_got, far_got, in_ref, gain_ref, *refs):
    residual_ref, mixed_ref = refs[-2:]
    residual = in_ref[...].astype(f32) + row_sum((near, near_got, far_got))
    residual_ref[...] = residual
    mixed_ref[...] = (residual * inv_rms(residual) * gain_ref[...]).astype(bf16)


def gap_kernel(near, near_got, far_got, residual_ref, target_ref, *refs):
    out_ref, gap_ref, gap_b_ref = refs[-3:]
    out = residual_ref[...] + row_sum((near, near_got, far_got))
    out_ref[...] = out.astype(bf16)
    gap = out - target_ref[...].astype(f32)
    gap_ref[...] = gap
    gap_b_ref[...] = gap.astype(bf16)


def resid_grad_kernel(near, near_got, far_got, residual_ref, gap_ref, gain_ref, *refs):
    grad_ref, grad_b_ref, sum_ref = refs[-3:]
    d_mixed = row_sum((near, near_got, far_got))
    residual = residual_ref[...]
    inv = inv_rms(residual)
    hat = residual * inv
    grad = gap_ref[...] + norm_back(d_mixed, hat, inv, gain_ref[...])
    grad_ref[...] = grad
    grad_b_ref[...] = grad.astype(bf16)

    @pl.when(pl.program_id(0) == 0)
    def _():
        sum_ref[...] = jnp.zeros_like(sum_ref)

    sum_ref[...] += jnp.sum(d_mixed * hat, axis=0, keepdims=True)


def input_grad_kernel(near, near_got, far_got, in_ref, grad_ref, gain_ref, *refs):
    rows = in_ref[...].astype(f32)
    inv = inv_rms(rows)
    d_normed = row_sum((near, near_got, far_got))
    grad = grad_ref[...] + norm_back(d_normed, rows * inv, inv, gain_ref[...])
    refs[-1][...] = grad.astype(bf16)


def row_call(kernel, terms, rows, gain, outs, earlier=()):
    count, width = rows[0].shape
    block = min(32, count)
    spec = pl.BlockSpec((block, width), lambda i: (i, 0))
    line = pl.BlockSpec((1, width), lambda i: (0, 0))
    gains = [] if gain is None else [gain.reshape(1, width)]
    return pl.pallas_call(
        kernel,
        grid=(count // block,),
        in_specs=[spec] * (len(terms) + len(rows))
        + [line] * len(gains)
        + [pl.BlockSpec(memory_space=pl.ANY)] * len(earlier),
        out_specs=[line if o is None else spec for o in outs],
        out_shape=[
            jax.ShapeDtypeStruct((1, width) if o is None else (count, width), f32 if o is None else o)
            for o in outs
        ],
        compiler_params=params(16),
        cost_estimate=cost(0.1),
        name=kernel.__name__,
    )(*terms, *rows, *gains, *earlier)


def pick_kernel(cols, z_count, c_ref, r0_ref, r1_ref, *refs):
    out_ref = refs[-1]
    half = r0_ref.shape[0]
    out_ref[:half] = r0_ref[...]
    out_ref[half:] = r1_ref[...]


def pick_half(rows_h, at, earlier=()):
    half, width = rows_h[0].shape
    cols = width // 2
    block = cols // 2
    return pl.pallas_call(
        functools.partial(pick_kernel, cols, 2),
        grid_spec=pltpu.PrefetchScalarGridSpec(
            num_scalar_prefetch=1,
            grid=(2,),
            in_specs=[pl.BlockSpec((half, block), lambda j, c: (0, 2 * c[0] + j))] * 2
            + [pl.BlockSpec(memory_space=pl.ANY)] * len(earlier),
            out_specs=pl.BlockSpec((2 * half, block), lambda j, c: (0, j)),
        ),
        out_shape=jax.ShapeDtypeStruct((2 * half, cols), rows_h[0].dtype),
        cost_estimate=cost(0.1),
        name="pick_half",
    )(at.reshape(1), *rows_h, *earlier)


def token_places(seq_lengths, permutation):
    seq_ends = jnp.cumsum(seq_lengths)
    seq_starts = seq_ends - seq_lengths
    seq_id = jnp.sum((permutation[:, None] >= seq_ends[None, :]).astype(jnp.int32), axis=1)
    member = seq_id[:, None] == jnp.arange(seq_lengths.shape[0], dtype=jnp.int32)[None, :]
    return jnp.sum(jnp.where(member, seq_starts[None, :], 0), axis=1)


def near_first(a, axis, y_pos, c_pos):
    a = jnp.where(y_pos == 0, a, jnp.flip(a, axis))
    return jnp.where(c_pos == 0, a, jnp.flip(a, axis + 1))


def norm_back(grad_out, hat_rows, inv_rows, gain_row):
    grad_hat = grad_out * gain_row
    return inv_rows * (grad_hat - hat_rows * jnp.mean(grad_hat * hat_rows, axis=-1, keepdims=True))


def gather_near(rows):
    far = lax.ppermute(rows, "y", SWAP)
    return join_rows(rows, lax.ppermute(rows, "c", SWAP)), far


def gather_far(far, beside=(), earlier=()):
    if beside:
        far = pass_rows(far, beside)
    return join_rows(far, lax.ppermute(far, "c", SWAP), earlier)


def scatter_halves(near, far):
    sent = far[0].astype(f32) + lax.ppermute(far[1], "c", SWAP).astype(f32)
    sent = sent.astype(bf16)
    far_got = lax.ppermute(sent, "y", SWAP)
    near_got = lax.ppermute(near[1], "c", SWAP)
    return (near[0], near_got, far_got), sent


def sum_near(a):
    a = a + jnp.flip(lax.ppermute(a, "c", SWAP), -2)
    return a + jnp.flip(lax.ppermute(a, "y", SWAP), -3)


def sum_line(a, z_count):
    step = 1
    while step < z_count:
        a = a + lax.ppermute(a, "z", [(i, i ^ step) for i in range(z_count)])
        step *= 2
    return a


def local(
    z_count,
    x_count,
    block_in,
    target,
    seq_lengths,
    permutation,
    routes,
    attn_qkv,
    attn_out,
    norm_gains,
    router,
    gate_up,
    down,
):
    z_pos = lax.axis_index("z")
    x_pos = lax.axis_index("x")
    y_pos = lax.axis_index("y")
    c_pos = lax.axis_index("c")
    pair = x_count == 2
    local_rows, model_width = block_in.shape
    tok_rows = 4 * local_rows
    line_rows = z_count * tok_rows
    head_cols = attn_qkv.shape[2]
    hidden_cols = gate_up.shape[3]
    experts = gate_up.shape[1]
    wide_block = model_width // z_count
    out_block = wide_block // x_count
    wt_pos = y_pos * 2 + c_pos

    qkv_b = attn_qkv.astype(bf16)
    router_b = router.astype(bf16)

    def scatter_x(a):
        if pair:
            mine = lax.dynamic_index_in_dim(a, x_pos, 0, False)
            other = lax.dynamic_index_in_dim(a, 1 - x_pos, 0, False)
            return mine.astype(f32) + lax.ppermute(other.astype(bf16), "x", SWAP).astype(f32)
        return lax.psum_scatter(a.astype(bf16), "x", scatter_dimension=0).astype(f32)

    def of_parity(rows_h, at):
        return jnp.concatenate(
            [
                jnp.concatenate(
                    [
                        lax.dynamic_slice_in_dim(
                            r, z * wide_block + at * out_block, out_block, 1
                        )
                        for z in range(z_count)
                    ],
                    axis=1,
                )
                for r in rows_h
            ]
        )

    def far_wide(rows_h):
        return lax.ppermute(of_parity(rows_h, 1 - x_pos), "x", SWAP)

    def swap_x(parts):
        return [lax.ppermute(p, "x", SWAP) for p in parts]

    resid_in = block_in.astype(f32)
    inv_first = lax.rsqrt(jnp.mean(resid_in * resid_in, axis=-1, keepdims=True) + norm_eps)
    hat_first = resid_in * inv_first
    normed = (hat_first * norm_gains[0]).astype(bf16)
    normed_near, normed_far = gather_near(normed)
    normed_h = [normed_near, gather_far(normed_far)]

    start_all = token_places(seq_lengths, permutation)
    shape = (z_count, x_count, 2, 2, local_rows)
    tok_all = near_first(permutation.reshape(shape), 2, y_pos, c_pos)
    start_all = near_first(start_all.reshape(shape), 2, y_pos, c_pos)

    def of_x(a, at):
        return lax.dynamic_index_in_dim(a, at, 1, False).reshape(line_rows)

    tok_own = of_x(tok_all, x_pos)
    start_own = of_x(start_all, x_pos)
    tok_q = tok_own.reshape(1, line_rows)
    start_q = start_own.reshape(1, line_rows)
    half_dim = HEAD_DIM // 2
    frequency = jnp.exp(
        jnp.arange(half_dim, dtype=f32) * (-2.0 * math.log(10000.0) / HEAD_DIM)
    )
    angles = (tok_own - start_own).astype(f32)[:, None] * frequency[None, :]
    cosine, sine = jnp.cos(angles), jnp.sin(angles)

    raw0, square0, v0 = project(normed_h[0], qkv_b)
    raw1, square1, v1 = project(normed_h[1], qkv_b, (v0,))
    squares = jnp.concatenate([square0[:, 0], square1[:, 0]], axis=1)
    squares = sum_near(squares.reshape(2, 2, 2, local_rows)).reshape(2, tok_rows)
    inv_qk = lax.rsqrt(squares / model_width + norm_eps)
    inv_slots = jnp.where(
        (jnp.arange(z_count, dtype=jnp.int32) == z_pos)[:, None, None], inv_qk[None], 0.0
    )
    inv_line = sum_line(inv_slots, z_count)
    gain_qk = lax.dynamic_slice_in_dim(norm_gains[2:], wt_pos * head_cols, head_cols, 1)

    def to_heads_apart(parts, earlier=(), beside=None):
        near = [lax.dynamic_index_in_dim(parts, z_pos, 0, False)]
        for d in range(1, z_count):
            there = lax.dynamic_index_in_dim(parts, (z_pos + d) % z_count, 0, False)
            near.append(
                lax.ppermute(there, "z", [(i, (i + d) % z_count) for i in range(z_count)])
            )
        if beside is None:
            return arrange(near, z_pos, earlier)
        beside = beside(near[1])
        return arrange(near, z_pos, (*earlier, beside)), beside

    def to_heads(parts):
        return lax.all_to_all(parts, "z", 0, 0, tiled=True).reshape(line_rows, HEAD_DIM)

    def from_x(a):
        if pair:
            return lax.ppermute(a, "x", SWAP)
        return lax.all_gather(a, "x", axis=0)

    v_heads = jnp.concatenate([v0, v1], axis=1)
    q_heads, k_heads = pack_heads(
        raw0,
        raw1,
        inv_qk.T,
        lax.dynamic_slice_in_dim(cosine, z_pos * tok_rows, tok_rows),
        lax.dynamic_slice_in_dim(sine, z_pos * tok_rows, tok_rows),
        gain_qk,
    )
    values = pass_rows(to_heads(v_heads), (k_heads,))
    values_far = from_x(values)
    keys = to_heads_apart(k_heads, (values_far,))
    out_b = attn_out.astype(bf16)
    keys_far = from_x(keys)
    queries = to_heads_apart(q_heads)
    tok_col = tok_own.reshape(line_rows, 1)
    if pair:
        tok_far = of_x(tok_all, 1 - x_pos).reshape(line_rows, 1)
        groups = [(keys_far, values_far, tok_far), (keys, values, tok_col)]
        key_groups = groups[::-1]
    else:
        tok_x = jnp.moveaxis(tok_all, 1, 0).reshape(x_count, line_rows, 1)
        groups = [(keys_far[i], values_far[i], tok_x[i]) for i in range(x_count)]
        key_groups = [
            (
                keys_far.reshape(-1, HEAD_DIM),
                values_far.reshape(-1, HEAD_DIM),
                tok_x.reshape(-1, 1),
            )
        ]
    attn_f, row_lse = attend(
        queries, tok_q, start_q, key_groups
    )

    def to_tokens(rows, cols):
        parts = lax.all_to_all(
            rows.reshape(z_count, tok_rows, cols), "z", 0, 0, tiled=True
        )
        return parts

    attn_parts = to_tokens(attn_f.astype(bf16), HEAD_DIM)
    normed_pick = pick_half(normed_h, c_pos, (attn_parts,))
    attn_far = attn_out_half(attn_parts, 1, out_b)
    attn_near = attn_out_half(attn_parts, 0, out_b)
    attn_y, attn_sent = scatter_halves(attn_near, attn_far)
    normed_line = lax.all_gather(normed_pick, "z", axis=0, tiled=True)
    gu_b = round_weights(gate_up, (attn_sent,))
    residual, mixed_rows = row_call(
        mix_kernel,
        attn_y,
        (block_in,),
        norm_gains[1],
        (f32, bf16),
        (gu_b, normed_pick),
    )
    down_b = round_weights(down, (mixed_rows,))
    mixed_near, mixed_far = gather_near(mixed_rows)

    def halves(a):
        return a[: a.shape[0] // 2], a[a.shape[0] // 2 :]

    route_rows = near_first(routes.reshape(2, 2, local_rows, -1), 0, y_pos, c_pos)
    route_rows = route_rows.reshape(tok_rows, -1)
    if pair:
        routes_far = lax.ppermute(route_rows.T.astype(f32), "x", SWAP).T.astype(jnp.int32)
    choose = jnp.sum(
        (route_rows[:, :, None] == jnp.arange(experts, dtype=jnp.int32)[None, None, :]).astype(f32),
        axis=1,
    )

    def expert_rows(mixed, choose):
        prob = jax.nn.softmax(jnp.dot(mixed, router_b, preferred_element_type=f32), axis=-1)
        gate_w = prob * choose
        gate_in, up_in = jnp.einsum("td,kedf->ketf", mixed, gu_b, preferred_element_type=f32)
        gate_sig = jax.nn.sigmoid(gate_in)
        hidden = (gate_w.T[:, :, None] * (gate_in * gate_sig) * up_in).astype(bf16)
        y = jnp.einsum("etf,edf->td", hidden, down_b, preferred_element_type=f32)
        return y.astype(bf16), hidden, (mixed, choose, prob, gate_w, gate_in, up_in)

    choose_h = halves(choose)
    near_y, hidden0, kept0 = expert_rows(mixed_near, choose_h[0])
    mixed_h = [mixed_near, gather_far(mixed_far, (down_b,), (near_y,))]
    mixed_far = [far_wide([m]) for m in mixed_h] if pair else [mixed_rows, mixed_rows]
    far_y, hidden1, kept1 = expert_rows(mixed_h[1], choose_h[1])
    hidden_h = [hidden0, hidden1]
    expert_y, _ = scatter_halves(halves(near_y), halves(far_y))
    block_out, cot_local, cot_b = row_call(
        gap_kernel, expert_y, (residual, target), None, (bf16, f32, bf16),
        (mixed_far[0],),
    )
    def expert_rows_back(cot, kept):
        mixed, choose, prob, gate_w, gate_in, up_in = kept
        d_hid = (
            jnp.einsum("td,edf->etf", cot, down_b, preferred_element_type=f32)
            .astype(bf16)
            .astype(f32)
        )
        gate_sig = jax.nn.sigmoid(gate_in)
        gate_act = gate_in * gate_sig
        d_gate_w = jnp.sum(d_hid * gate_act * up_in, axis=-1).T
        scaled = d_hid * gate_w.T[:, :, None]
        d_gate_in = scaled * up_in * gate_sig * (1.0 + gate_in * (1.0 - gate_sig))
        d_pre = jnp.stack([d_gate_in, scaled * gate_act]).astype(bf16)
        d_prob = d_gate_w * choose
        d_logit = (prob * (d_prob - jnp.sum(prob * d_prob, axis=-1, keepdims=True))).astype(bf16)
        d_mixed = (
            jnp.einsum("ketf,kedf->td", d_pre, gu_b, preferred_element_type=f32)
            + lax.dot_general(d_logit, router_b, DOT_NT, preferred_element_type=f32)
        ).astype(bf16)
        router_part = lax.dot_general(
            d_logit, mixed, (((0,), (0,)), ((), ())), preferred_element_type=f32
        )
        return d_mixed, d_pre, router_part

    cot_near, cot_far = gather_near(cot_b)
    near_d, d_pre0, router0 = expert_rows_back(cot_near, kept0)
    cot_h = [cot_near, gather_far(cot_far, (), (mixed_far[1], normed_line, near_d))]
    far_d, d_pre1, router1 = expert_rows_back(cot_h[1], kept1)
    router_rows = router0 + router1
    d_pre_h = [d_pre0, d_pre1]
    d_mixed, d_mixed_sent = scatter_halves(halves(near_d), halves(far_d))
    down_part = own_grad(cot_h, hidden_h, (d_mixed_sent,))

    def compact(a, taken):
        a = a.reshape(-1, experts, *a.shape[1:])
        taken = taken.T[:, None, :, None]
        parts = []
        for slot in range(taken.shape[0]):
            part = a[:, 0]
            for e in range(1, experts):
                part = jnp.where(taken[slot] == e, a[:, e], part)
            parts.append(part)
        return jnp.stack(parts, axis=1)

    def plain_part(wide_h, narrow, spec):
        return scatter_x(
            jnp.stack(
                [
                    jnp.einsum(spec, of_parity(wide_h, i), narrow, preferred_element_type=f32)
                    for i in range(x_count)
                ]
            )
        ).astype(bf16)

    d_pre_h = [d.reshape(2 * experts, -1, hidden_cols) for d in d_pre_h]
    if pair:
        d_pre_far = [
            lax.ppermute(compact(d, r), "x", SWAP) for d, r in zip(d_pre_h, (route_rows[: tok_rows // 2], route_rows[tok_rows // 2 :]))
        ]
    d_resid, d_resid_b, gain_second = row_call(
        resid_grad_kernel,
        d_mixed,
        (residual, cot_local),
        norm_gains[1],
        (f32, bf16, None),
        (down_part, d_pre_far[0]) if pair else (down_part,),
    )
    resid_near, resid_far = gather_near(d_resid_b)
    d_resid_h = [resid_near, gather_far(resid_far, (), (d_pre_far[1],) if pair else ())]
    d_attn = attn_out_grad_half(d_resid_h[0], 0, out_b)
    d_attn = attn_out_grad_half(d_resid_h[1], 1, out_b, d_attn)

    if pair:

        def gate_up_beside(piece):
            return weight_grad(
                mixed_h,
                mixed_far,
                [(d, 0) for d in d_pre_h],
                [(d, 0) for d in d_pre_far],
                out_block,
                x_pos,
                routes_far,
                experts,
                (piece,),
            )

        d_out, gate_up_part = to_heads_apart(d_attn, beside=gate_up_beside)
    else:
        d_out = to_heads(d_attn)
        gate_up_part = plain_part(mixed_h, jnp.concatenate(d_pre_h, axis=1), "td,ntf->ndf")
    delta = jnp.sum(d_out.astype(f32) * attn_f, axis=-1).reshape(1, line_rows)
    d_query = jnp.zeros((line_rows, HEAD_DIM), f32)
    down_part = lax.psum_scatter(down_part, "z", scatter_dimension=1, tiled=True)
    gate_up_sum = lax.psum_scatter(gate_up_part, "z", scatter_dimension=1, tiled=True)
    d_kv = []
    inner_k = []
    earlier = (gate_up_part,)
    for i, group in enumerate(groups):
        last = i == len(groups) - 1
        d_query, *d_group, inner_q, inner_k_part = attend_grad(
            queries,
            d_out,
            row_lse,
            delta,
            tok_q,
            start_q,
            d_query,
            group,
            f32 if pair and last else bf16,
            earlier,
        )
        d_kv.append(d_group)
        inner_k.append(inner_k_part)
        if i == 0:
            earlier = (down_part,)
    if pair:
        d_key, d_value = [
            (own, lax.ppermute(far, "x", SWAP)) for far, own in zip(*d_kv)
        ]
        inner = stack_inner(
            inner_q, inner_k[1], lax.ppermute(inner_k[0], "x", SWAP), (d_key[1], d_value[1])
        )
    else:
        d_key, d_value = [
            (
                lax.psum_scatter(jnp.stack(parts), "x", scatter_dimension=0).astype(f32),
                jnp.zeros((line_rows, HEAD_DIM), bf16),
            )
            for parts in zip(*d_kv)
        ]
        inner_k = lax.psum_scatter(jnp.stack(inner_k), "x", scatter_dimension=0)
        inner = jnp.concatenate([inner_q, inner_k])
    inner = sum_line(sum_near(inner.reshape(2, z_count, 2, 2, local_rows)), z_count)
    inner = inner.reshape(2, line_rows) / model_width
    inv_line = jnp.moveaxis(inv_line, 0, 1).reshape(2, line_rows)
    head_gain = lax.dynamic_slice_in_dim(gain_qk, z_pos * HEAD_DIM, HEAD_DIM, 1)
    d_raw, gain_sums = raw_grad(
        d_query,
        d_key,
        d_value,
        queries,
        keys,
        inv_line,
        inner,
        cosine,
        sine,
        head_gain,
        d_kv[-1][0],
    )
    gain_full = lax.dynamic_update_slice_in_dim(
        jnp.zeros((2, model_width), f32), gain_sums, (wt_pos * z_count + z_pos) * HEAD_DIM, 1
    )

    def sum_plane(a):
        a = a + lax.ppermute(a, "c", SWAP)
        a = a + lax.ppermute(a, "y", SWAP)
        return a + lax.ppermute(a, "x", SWAP) if pair else lax.psum(a, "x")

    grad_mine, grad_other = qkv_grad(
        normed_line, d_raw, lax.ppermute(d_raw, "c", SWAP), z_count
    )
    grad_other = lax.ppermute(grad_other, "c", SWAP)
    qkv_full = jnp.where(
        c_pos == 0,
        jnp.stack([grad_mine, grad_other]),
        jnp.stack([grad_other, grad_mine]),
    ).reshape(z_count, x_count, out_block, 3 * HEAD_DIM)
    gain_first = first_gain(
        qkv_b, qkv_full.reshape(model_width, 3 * HEAD_DIM), norm_gains[0], z_pos
    )
    qkv_line = jnp.moveaxis(qkv_full, 1, 0)
    if pair:
        qkv_line = (
            lax.dynamic_index_in_dim(qkv_line, x_pos, 0, False),
            lax.ppermute(lax.dynamic_index_in_dim(qkv_line, 1 - x_pos, 0, False), "x", SWAP),
        )
    else:
        qkv_line = scatter_x(qkv_line).astype(bf16)
        qkv_line = (qkv_line, jnp.zeros_like(qkv_line))
    d_proj = to_tokens(d_raw, 3 * HEAD_DIM)
    small = sum_plane(stack_rows(gain_first, gain_second, gain_full, router_rows))
    out_part = own_grad(
        d_resid_h, (attn_parts, attn_parts), (d_proj, qkv_line[1], small)
    )
    small = sum_line(small, z_count)
    far_n = project_grad_half(d_proj, 1, qkv_b, (out_part, gate_up_sum, small))
    out_part = lax.psum_scatter(out_part, "z", scatter_dimension=1, tiled=True)
    near_n = project_grad_half(d_proj, 0, qkv_b, (far_n[0],))
    d_normed, _ = scatter_halves(near_n, far_n)
    (input_grad,) = row_call(
        input_grad_kernel,
        d_normed,
        (block_in, d_resid),
        norm_gains[0],
        (bf16,),
    )

    gains_grad = small[:4]
    router_grad = small[4:].T

    qkv_heads = lax.all_to_all(
        add_rows(*qkv_line, (near_n[0],)), "z", 0, 0, tiled=True
    )
    qkv_part = (
        qkv_heads.reshape(z_count, out_block, 3, HEAD_DIM)
        .transpose(2, 1, 0, 3)
        .reshape(3, out_block, head_cols)
        .astype(f32)
    )
    def own_block(a):
        return scatter_x(jnp.moveaxis(a.reshape(a.shape[0], x_count, out_block, -1), 1, 0))

    return (
        block_out,
        input_grad,
        qkv_part,
        jnp.moveaxis(own_block(out_part), 0, 1).reshape(out_block, head_cols),
        gains_grad,
        router_grad,
        gate_up_sum.astype(f32).reshape(2, experts, out_block, hidden_cols),
        own_block(down_part),
    )


def solution(mesh):
    ctx_count = mesh.shape["ctx"]

    def run(*args):
        heads = args[5].shape[2] // HEAD_DIM
        z_count = heads // mesh.shape["wt"]
        x_count = ctx_count // z_count
        grid = Mesh(mesh.devices.reshape(z_count, x_count, 2, 2), ("z", "x", "y", "c"))
        ctx, wt = ("z", "x"), ("y", "c")
        return jax.shard_map(
            functools.partial(local, z_count, x_count),
            mesh=grid,
            in_specs=(
                P(ctx + wt, None),
                P(ctx + wt, None),
                P(),
                P(),
                P(ctx, None),
                P(None, None, wt),
                P(None, wt),
                P(),
                P(),
                P(None, None, None, wt),
                P(None, None, wt),
            ),
            out_specs=(
                P(ctx + wt, None),
                P(ctx + wt, None),
                P(None, ctx, wt),
                P(ctx, wt),
                P(),
                P(),
                P(None, None, ctx, wt),
                P(None, ctx, wt),
            ),
            check_vma=False,
        )(*args)

    return run
```
